32 devices in a mesh: dp: 16 (over z, x, core), seq: 2 (over y).
Axes of the slice: x: 2, y: 2, z: 4, core: 2. Of those that a mesh axis runs over, the one named last changes fastest.
Arguments:
- inputs: bfloat16 [16, 1024, 1024], P('dp', 'seq'), may hold values from -6 to 6
- doc_ids: int32 [16, 1024], P('dp', 'seq'), may hold values from 0 to 7, never falling along the last dimension, each value on 1 to 256 neighbouring positions
- w_qkv: bfloat16 [1024, 3072], replicated, may hold values from -0.1875 to 0.1875
- bias_q: bfloat16 [1024], replicated, may hold values from -3 to 3
- bias_v: bfloat16 [1024], replicated, may hold values from -3 to 3
- w_out: bfloat16 [1024, 1024], replicated, may hold values from -0.375 to 0.375
- bias_out: bfloat16 [1024], replicated, may hold values from -2 to 2
- norm1_gain: bfloat16 [1024], replicated, may hold values from 0.5 to 1.5
- norm1_bias: bfloat16 [1024], replicated, may hold values from -2 to 2
- norm2_gain: bfloat16 [1024], replicated, may hold values from 0.5 to 1.5
- norm2_bias: bfloat16 [1024], replicated, may hold values from -2 to 2
- w_up: bfloat16 [1024, 4096], replicated, may hold values from -0.1875 to 0.1875
- bias_up: bfloat16 [4096], replicated, may hold values from -2 to 2
- w_down: bfloat16 [4096, 1024], replicated, may hold values from -0.125 to 0.125
- bias_down: bfloat16 [1024], replicated, may hold values from -2 to 2
- cotangent: bfloat16 [16, 1024, 1024], P('dp', 'seq'), may hold values from -6 to 6
Outputs:
- out: bfloat16 [16, 1024, 1024], P('dp', 'seq')
- grad_inputs: float32 [16, 1024, 1024], P('dp', 'seq')
- grad_w_qkv: float32 [1024, 3072], P('dp', 'seq')
- grad_bias_q: float32 [1024], replicated
- grad_bias_v: float32 [1024], replicated
- grad_w_out: float32 [1024, 1024], P('dp', 'seq')
- grad_bias_out: float32 [1024], replicated
- grad_norm1_gain: float32 [1024], replicated
- grad_norm1_bias: float32 [1024], replicated
- grad_norm2_gain: float32 [1024], replicated
- grad_norm2_bias: float32 [1024], replicated
- grad_w_up: float32 [1024, 4096], P('dp', 'seq')
- grad_bias_up: float32 [4096], replicated
- grad_w_down: float32 [4096, 1024], P('dp', 'seq')
- grad_bias_down: float32 [1024], replicated
The draws below stay inside these ranges and needn't reach their ends.
Inputs may be any that keep to these rules, and one draw needn't show every extreme that they name: `doc_ids`: non-decreasing along each row; each row holds 8 documents of 1 to 256 tokens, one of exactly 256.
All inputs are finite; a program needn't handle non-finite values.
Results may differ from the reference program's by a relative error of at most 0.017.
Values may be sent and summed in bfloat16 or wider, within the bound.
A program may use at most 192 MiB of HBM per device.

```python
import math
import jax
import jax.numpy as jnp
import numpy as np
from jax import lax

D = 1024
HEAD_DIM = 128
FF = 4096
ROWS = 16
SEQ_LEN = 1024


def levels(key, dims, split, least, largest):
    loudness = 1.0
    for dim, blocks in split:
        steps = jax.random.uniform(jax.random.fold_in(jax.random.fold_in(key, 6), dim), (blocks,), jnp.float32, least / len(split), largest / len(split))
        loudness = loudness * jnp.repeat(jnp.exp(steps), dims[dim] // blocks).reshape((-1,) + (1,) * (len(dims) - 1 - dim))
    return loudness


def length_profile(count, total, most, slope):
    portions = [(1 << 20) // math.isqrt(standing ** slope) + 1 for standing in range(2, count + 1)]
    surplus, holding = total - most - (count - 1), [1] * (count - 1)
    while surplus > 0:
        free = [i for i in range(count - 1) if holding[i] < most]
        mass, remaining = sum([portions[i] for i in free]), surplus
        for i in free:
            more = min(most - holding[i], max(1, remaining * portions[i] // mass), surplus)
            holding[i] = holding[i] + more
            surplus = surplus - more
    return np.array([most] + holding)


def uneven_parts(stream_key, number_of, total, limit, skew):
    if number_of == 2:
        one = jax.random.randint(stream_key, (), max(1, total - limit), min(limit, total - 1) + 1)
        return jnp.stack([one, total - one])
    tallies = jnp.asarray(length_profile(number_of, total, limit, skew), jnp.int32)
    pairs = (number_of - 1) // 2
    giver, sink = tallies[1:1 + 2 * pairs:2], tallies[2:2 + 2 * pairs:2]
    slack = jnp.minimum(giver - 1, limit - sink)
    passed = jax.random.randint(jax.random.fold_in(stream_key, 1), (pairs,), 0, 1 << 20) % (slack + 1)
    tallies = tallies.at[1:1 + 2 * pairs:2].set(giver - passed).at[2:2 + 2 * pairs:2].set(sink + passed)
    return tallies[jax.random.permutation(jax.random.fold_in(stream_key, 2), number_of)]


def normal_values(key, dims, spread, limit, cuts=(), held_as=jnp.bfloat16):
    drawn = spread * jax.random.normal(key, dims, jnp.float32)
    if cuts:
        drawn = drawn * levels(key, dims, cuts, -0.22, 0.18)
    return jnp.clip(drawn, -limit, limit).astype(held_as)


def setup_inputs(seed: int = 0) -> dict:
    splits = jax.random.split(jax.random.key(seed), 17)
    inputs = normal_values(splits[0], (ROWS, SEQ_LEN, D), 1.0, 6.0, ((0, 16), (1, 2)))
    doc_ids = jax.vmap(lambda own: jnp.searchsorted(jnp.cumsum(uneven_parts(own, 8, SEQ_LEN, SEQ_LEN // 4, 1)), jnp.arange(SEQ_LEN), side="right"))(jax.random.split(splits[1], ROWS)).reshape((ROWS, SEQ_LEN)).astype(jnp.int32)
    w_qkv = normal_values(splits[2], (D, 3 * D), D ** -0.5, 0.1875)
    bias_q = normal_values(splits[3], (D,), 0.5, 3.0)
    bias_v = normal_values(splits[4], (D,), 0.5, 3.0)
    w_out = normal_values(splits[5], (D, D), (D // 4) ** -0.5, 0.375)
    bias_out = normal_values(splits[6], (D,), 0.3, 2.0)
    norm1_gain = jnp.clip(1.0 + 0.1 * jax.random.normal(splits[7], (D,), jnp.float32), 0.5, 1.5).astype(jnp.bfloat16)
    norm1_bias = normal_values(splits[8], (D,), 0.3, 2.0)
    norm2_gain = jnp.clip(1.0 + 0.1 * jax.random.normal(splits[9], (D,), jnp.float32), 0.5, 1.5).astype(jnp.bfloat16)
    norm2_bias = normal_values(splits[10], (D,), 0.3, 2.0)
    w_up = normal_values(splits[11], (D, FF), D ** -0.5, 0.1875)
    bias_up = normal_values(splits[12], (FF,), 0.3, 2.0)
    w_down = normal_values(splits[13], (FF, D), (FF // 2) ** -0.5, 0.125)
    bias_down = normal_values(splits[14], (D,), 0.3, 2.0)
    cotangent = normal_values(splits[15], (ROWS, SEQ_LEN, D), 1.0, 6.0, ((0, 16), (1, 2)))
    return {"inputs": inputs, "doc_ids": doc_ids, "w_qkv": w_qkv, "bias_q": bias_q, "bias_v": bias_v, "w_out": w_out, "bias_out": bias_out, "norm1_gain": norm1_gain, "norm1_bias": norm1_bias, "norm2_gain": norm2_gain, "norm2_bias": norm2_bias, "w_up": w_up, "bias_up": bias_up, "w_down": w_down, "bias_down": bias_down, "cotangent": cotangent}


@jax.custom_vjp
def low(v):
    return lax.optimization_barrier(v.astype(jnp.bfloat16)).astype(jnp.float32)

@jax.custom_vjp
def low_back(v):
    return v

def low_keep(v):
    return (low(v), None)

def low_pass(kept, grad):
    return (grad,)

def back_keep(v):
    return (v, None)

def back_low(kept, grad):
    return (low(grad),)
low.defvjp(low_keep, low_pass)
low_back.defvjp(back_keep, back_low)
norm_eps = 1e-05
masked_score = -1e+30
highest = lax.Precision.HIGHEST

def round_both(values):
    return low_back(low(values))

def layer_norm(values, norm_gain, norm_shift):
    center = values - lax.optimization_barrier(jnp.mean(values, axis=-1, keepdims=True))
    inv_std = lax.rsqrt(lax.optimization_barrier(jnp.mean(center * center, axis=-1, keepdims=True)) + norm_eps)
    return center * inv_std * norm_gain + norm_shift

def row_forward(row_inputs, doc_row, params):
    w_qkv, bias_q, bias_v, w_out, bias_out, gain_one, shift_one, gain_two, shift_two, w_up, bias_up, w_down, bias_down = params
    model_width = w_out.shape[0]
    length = row_inputs.shape[0]
    head_count = model_width // HEAD_DIM
    act_one = low(layer_norm(row_inputs, gain_one, shift_one))
    projected = jnp.dot(act_one, w_qkv, precision=highest)
    query_rows = round_both(projected[:, :model_width] + bias_q)
    key_rows = round_both(projected[:, model_width:2 * model_width])
    value_rows = round_both(projected[:, 2 * model_width:] + bias_v)
    block_rows = min(512, length)
    slopes = jnp.exp2(-(jnp.arange(head_count, dtype=jnp.int32) + 1).astype(row_inputs.dtype))
    head_q = query_rows.reshape(length, head_count, HEAD_DIM).transpose(1, 0, 2)
    head_k = key_rows.reshape(length, head_count, HEAD_DIM).transpose(1, 0, 2)
    head_v = value_rows.reshape(length, head_count, HEAD_DIM).transpose(1, 0, 2)

    def one_head(operands):
        query_head, key_head, value_head, head_slope = operands

        def one_block(block_args):
            query_block, first_row = block_args
            raw_scores = jnp.dot(query_block, key_head.T, precision=highest)
            query_pos = first_row + jnp.arange(block_rows, dtype=jnp.int32)
            key_pos = jnp.arange(length, dtype=jnp.int32)
            offset = query_pos[:, None] - key_pos[None, :]
            query_doc = lax.dynamic_slice_in_dim(doc_row, first_row, block_rows)
            allowed = (offset >= 0) & (query_doc[:, None] == doc_row[None, :])
            scores = low_back(raw_scores * HEAD_DIM ** (-0.5) - head_slope * offset.astype(raw_scores.dtype))
            scores = jnp.where(allowed, scores, masked_score)
            row_max = lax.optimization_barrier(jnp.max(scores, axis=-1, keepdims=True))
            exponent = jnp.exp(scores - row_max)
            weights = exponent / lax.optimization_barrier(jnp.sum(exponent, axis=-1, keepdims=True))
            return jnp.dot(low(weights), value_head, precision=highest)
        starts = jnp.arange(length // block_rows, dtype=jnp.int32) * block_rows
        block_outs = lax.map(jax.checkpoint(one_block), (query_head.reshape(-1, block_rows, HEAD_DIM), starts))
        return block_outs.reshape(length, HEAD_DIM)
    head_outs = lax.map(one_head, (head_q, head_k, head_v, slopes))
    mixed_heads = round_both(head_outs.transpose(1, 0, 2).reshape(length, model_width))
    attention = low_back(jnp.dot(mixed_heads, w_out, precision=highest) + bias_out)
    second = row_inputs + attention
    act_two = low(layer_norm(second, gain_two, shift_two))
    pre_act = low_back(jnp.dot(act_two, w_up, precision=highest) + bias_up)
    hidden = low(jax.nn.gelu(pre_act, approximate=True))
    feed = low_back(jnp.dot(hidden, w_down, precision=highest) + bias_down)
    return second + feed

def reference(inputs, doc_ids, w_qkv, bias_q, bias_v, w_out, bias_out, norm1_gain, norm1_bias, norm2_gain, norm2_bias, w_up, bias_up, w_down, bias_down, cotangent):
    params = (w_qkv.astype(jnp.float32), bias_q.astype(jnp.float32), bias_v.astype(jnp.float32), w_out.astype(jnp.float32), bias_out.astype(jnp.float32), norm1_gain.astype(jnp.float32), norm1_bias.astype(jnp.float32), norm2_gain.astype(jnp.float32), norm2_bias.astype(jnp.float32), w_up.astype(jnp.float32), bias_up.astype(jnp.float32), w_down.astype(jnp.float32), bias_down.astype(jnp.float32))
    float_inputs = inputs.astype(jnp.float32)
    float_cot = cotangent.astype(jnp.float32)

    def one_row(totals, row_args):
        row_in, doc_row, row_cot = row_args

        def forward(row_values, all_params):
            return row_forward(row_values, doc_row, all_params)
        row_out, pullback = jax.vjp(forward, row_in, params)
        row_grad, param_grads = pullback(row_cot)
        totals = jax.tree.map(lambda first, second: first + second, totals, param_grads)
        return (totals, (row_out.astype(jnp.bfloat16), row_grad))
    zero_grads = jax.tree.map(jnp.zeros_like, params)
    grads, (result, grad_inputs) = lax.scan(one_row, zero_grads, (float_inputs, doc_ids, float_cot))
    return (result, grad_inputs, grads[0], grads[1], grads[2], grads[3], grads[4], grads[5], grads[6], grads[7], grads[8], grads[9], grads[10], grads[11], grads[12])
```

```python
import functools

import jax
import jax.numpy as jnp
import numpy as np
from jax import lax
from jax.experimental import pallas as pl
from jax.experimental.pallas import tpu as pltpu
from jax.sharding import PartitionSpec as P

HEAD_DIM = 128
MESH = pl.DeviceIdType.MESH
F32 = jnp.float32
BF16 = jnp.bfloat16
LOG2E = 1.4426950408889634
FAR = 1e30
GELU_C = 0.7978845608028654
GELU_A = 0.044715

norm_eps = 1e-05
masked_score = -1e30

NT = (((1,), (1,)), ((), ()))
TN = (((0,), (0,)), ((), ()))


def dot(a, b):
    return jnp.dot(a, b, preferred_element_type=F32)


def dot_nt(a, b):
    return lax.dot_general(a, b, NT, preferred_element_type=F32)


def dot_tn(a, b):
    return lax.dot_general(a, b, TN, preferred_element_type=F32)


def coords():
    dp = lax.axis_index("dp")
    return {
        "c": dp % 2,
        "x": (dp // 2) % 2,
        "a": (dp // 4) % 2,
        "b": dp // 8,
        "y": lax.axis_index("seq"),
    }


def partner(kind):
    dp = lax.axis_index("dp")
    if kind == "y":
        return {"seq": 1 - lax.axis_index("seq")}
    step = {"c": 1, "x": 2, "a": 4, "b": 8}[kind]
    bit = (dp // step) % 2
    return {"dp": dp + step - 2 * step * bit}


def greet(kinds):
    barrier = pltpu.get_barrier_semaphore()
    for kind in kinds:
        pl.semaphore_signal(barrier, inc=1, device_id=partner(kind), device_id_type=MESH)
    pl.semaphore_wait(barrier, len(kinds))


ORDERS = (("x", "a", "y", "b"), ("y", "a", "x", "b"))


def block_index(half, place):
    index = half * 16
    for kind, weight in zip(ORDERS[half], (8, 4, 2, 1)):
        index = index + place[kind] * weight
    return index


def dp_bits(dp):
    return {"c": dp % 2, "x": (dp // 2) % 2, "a": (dp // 4) % 2, "b": dp // 8}


class Scatter:
    def __init__(self, held, arrivals, send_sem, recv_sem):
        self.held, self.arrivals = held, arrivals
        self.send_sem, self.recv_sem = send_sem, recv_sem
        self.me = coords()

    def offset(self, half, stage, other):
        index = half * 16
        for k, weight in zip(range(stage + 1), (8, 4, 2, 1)):
            bit = self.me[ORDERS[half][k]]
            if other and k == stage:
                bit = 1 - bit
            index = index + bit * weight
        return index

    def copy(self, chunk, stage, half):
        size = 8 >> stage
        return pltpu.make_async_remote_copy(
            src_ref=self.held.at[chunk, pl.ds(self.offset(half, stage, True), size)],
            dst_ref=self.arrivals[stage].at[chunk, half],
            send_sem=self.send_sem.at[stage, chunk, half],
            recv_sem=self.recv_sem.at[stage, chunk, half],
            device_id=partner(ORDERS[half][stage]),
            device_id_type=MESH,
        )

    def start(self, chunk, stage):
        for half in range(2):
            self.copy(chunk, stage, half).start()

    def finish(self, chunk, stage):
        size = 8 >> stage
        for half in range(2):
            self.copy(chunk, stage, half).wait()
            mine = pl.ds(self.offset(half, stage, False), size)
            self.held[chunk, mine] = self.held[chunk, mine] + self.arrivals[stage][chunk, half]

    def result(self, chunk, half):
        return self.held[chunk, self.offset(half, 3, False)].astype(F32)


def arrival_shapes(chunks):
    return [pltpu.VMEM((chunks, 2, 8 >> k, 32, 256), BF16) for k in range(4)]


def when(cond, fn):
    if isinstance(cond, (bool, np.bool_)):
        if cond:
            fn()
    else:
        pl.when(cond)(fn)


def inside(value, low, high):
    if isinstance(value, int):
        return low <= value < high
    return (value >= low) & (value < high)


def kernel_one(
    halo, x_ref, doc_ref, slope_ref, bq_ref, bv_ref, bo_ref, g1_ref, s1_ref, g2_ref, s2_ref, wqkv_hbm, wout_hbm,
    act2_hbm, act2t_hbm, x2_hbm, qkv_hbm, ot_hbm, act1t_hbm, dist_hbm,
    act1, act1t, qkv, o_s, ot, act2, act2t, x2, dist, xh, doch, bias, wqkv, wout,
    wsem, osem, hs, hr,
):
    tokens, width = x_ref.shape
    heads = width // HEAD_DIM
    ext = tokens + halo
    seq = lax.axis_index("seq")

    wcopies = [
        pltpu.make_async_copy(
            wqkv_hbm.at[:, pl.ds(j * 512, 512)], wqkv.at[:, pl.ds(j * 512, 512)], wsem.at[j]
        )
        for j in range(6)
    ]
    wcopies.append(pltpu.make_async_copy(wout_hbm, wout, wsem.at[6]))
    for cp in wcopies:
        cp.start()
    greet(("y",))
    send_x = pltpu.make_async_remote_copy(
        src_ref=x_ref.at[pl.ds(tokens - halo, halo)], dst_ref=xh, send_sem=hs.at[0], recv_sem=hr.at[0],
        device_id=partner("y"), device_id_type=MESH,
    )
    send_doc = pltpu.make_async_remote_copy(
        src_ref=doc_ref, dst_ref=doch, send_sem=hs.at[1], recv_sem=hr.at[1],
        device_id=partner("y"), device_id_type=MESH,
    )

    @pl.when(seq == 0)
    def _():
        send_doc.start()
        send_x.start()

    gain1, shift1 = g1_ref[...].astype(F32), s1_ref[...].astype(F32)
    gain2, shift2 = g2_ref[...].astype(F32), s2_ref[...].astype(F32)

    def norm(v, gain, shift):
        center = v - jnp.mean(v, axis=-1, keepdims=True)
        inv = lax.rsqrt(jnp.mean(center * center, axis=-1, keepdims=True) + norm_eps)
        return center * inv * gain + shift

    bias[:, 0:width] = bq_ref[...].astype(F32)
    bias[:, width : 2 * width] = jnp.zeros((1, width), F32)
    bias[:, 2 * width :] = bv_ref[...].astype(F32)

    for r in range(tokens // 128):
        v = norm(x_ref[r * 128 : (r + 1) * 128].astype(F32), gain1, shift1).astype(BF16)
        act1[halo + r * 128 : halo + (r + 1) * 128] = v
        act1t[:, halo + r * 128 : halo + (r + 1) * 128] = v.T

    for j in range(6):
        wcopies[j].wait()
        cols = slice(j * 512, (j + 1) * 512)
        for m in range(tokens // 256):
            rows = slice(halo + m * 256, halo + (m + 1) * 256)
            qkv[rows, cols] = (dot(act1[rows], wqkv[:, cols]) + bias[:, cols]).astype(BF16)

    def distances(block):
        keys = doch_ext[block * 256 : block * 256 + 512]
        queries = doc_rows[:, block * 256 : block * 256 + 256]
        key_pos = lax.broadcasted_iota(jnp.int32, (512, 256), 0)
        query_pos = lax.broadcasted_iota(jnp.int32, (512, 256), 1) + 256
        gap = query_pos - key_pos
        allowed = (gap >= 0) & (keys == queries)
        dist[block] = jnp.where(allowed, gap.astype(F32), FAR)

    own_doc = doc_ref[...].astype(F32)[0:1]
    doc_rows = own_doc
    own_cols = jnp.transpose(jnp.broadcast_to(own_doc, (128, tokens)))[:, 0:1]

    def attend(block):
        def one_head(h, carry):
            c0 = pl.multiple_of(h * HEAD_DIM, HEAD_DIM)
            q = qkv[halo + block * 256 : halo + (block + 1) * 256, pl.ds(c0, HEAD_DIM)]
            k = qkv[block * 256 : block * 256 + 512, pl.ds(width + c0, HEAD_DIM)]
            v = qkv[block * 256 : block * 256 + 512, pl.ds(2 * width + c0, HEAD_DIM)]
            slope = slope_ref[pl.ds(h, 1), 0:1]
            s = dot_nt(k, q) * (LOG2E * HEAD_DIM**-0.5) - slope * dist[block]
            e = jnp.exp2(s - jnp.max(s, axis=0, keepdims=True))
            p = (e * (1.0 / jnp.sum(e, axis=0, keepdims=True))).astype(BF16)
            o_t = dot_tn(v, p)
            ot[pl.ds(c0, HEAD_DIM), block * 256 : (block + 1) * 256] = o_t.astype(BF16)
            o_s[block * 256 : (block + 1) * 256, pl.ds(c0, HEAD_DIM)] = o_t.T.astype(BF16)
            return carry

        lax.fori_loop(0, heads, one_head, 0)

    def project(block):
        for r in range(2):
            rows = slice(block * 256 + r * 128, block * 256 + (r + 1) * 128)
            second = x_ref[rows].astype(F32) + dot(o_s[rows], wout[...]) + bo_ref[...].astype(F32)
            x2[rows] = second
            v = norm(second, gain2, shift2).astype(BF16)
            act2[rows] = v
            act2t[:, rows] = v.T

    doch_ext = jnp.concatenate([jnp.full((halo, 1), -1.0, F32), own_cols], axis=0)
    distances(1)
    attend(1)
    wcopies[6].wait()
    project(1)

    @pl.when(seq == 0)
    def _():
        send_doc.wait_send()
        send_x.wait_send()
        doch[...] = jnp.full(doch.shape, -1, jnp.int32)
        xh[...] = jnp.zeros(xh.shape, BF16)
        act1[0:halo] = jnp.zeros((halo, width), BF16)
        act1t[:, 0:halo] = jnp.zeros((width, halo), BF16)
        qkv[0:halo] = jnp.zeros((halo, 3 * width), BF16)

    @pl.when(seq == 1)
    def _():
        send_doc.wait_recv()
        send_x.wait_recv()
        for r in range(halo // 128):
            v = norm(xh[r * 128 : (r + 1) * 128].astype(F32), gain1, shift1).astype(BF16)
            act1[r * 128 : (r + 1) * 128] = v
            act1t[:, r * 128 : (r + 1) * 128] = v.T
        for j in range(2, 6):
            cols = slice(j * 512, (j + 1) * 512)
            qkv[0:halo, cols] = (dot(act1[0:halo], wqkv[:, cols]) + bias[:, cols]).astype(BF16)

    halo_doc = doch[...].astype(F32)[0:1, tokens - halo :]
    halo_cols = jnp.transpose(jnp.broadcast_to(halo_doc, (128, halo)))[:, 0:1]
    doch_ext = jnp.concatenate([halo_cols, own_cols], axis=0)
    distances(0)
    attend(0)
    project(0)
    outs = [
        pltpu.make_async_copy(s, d, osem.at[i])
        for i, (s, d) in enumerate(
            (
                (act2, act2_hbm), (act2t, act2t_hbm), (x2, x2_hbm), (qkv, qkv_hbm), (ot, ot_hbm),
                (act1t, act1t_hbm), (dist, dist_hbm),
            )
        )
    ]
    for cp in outs:
        cp.start()
    for cp in outs:
        cp.wait()


def kernel_two(
    act2, act2t, cot, x2, g2_ref, bup_ref, bdown_ref, wup_hbm, wdown_hbm,
    out, gwu, dx2, ab, hd_hbm, vec,
    hid_t, hid, dpre, dn2, outacc, wu, wd, grad, came, held, r1, r2, r3, r4, gradd, camed,
    wsem, cs, cr, ss, rs, dcs, dcr, dsem,
):
    tokens, width = act2.shape
    ff = wup_hbm.shape[1]
    half = ff // 2
    steps = half // 256
    me = coords()

    def weights(f, slot):
        col = pl.multiple_of(f * 256, 256)
        return [
            pltpu.make_async_copy(wup_hbm.at[:, pl.ds(col, 256)], wu.at[slot, :, pl.ds(0, 256)], wsem.at[slot, 0]),
            pltpu.make_async_copy(
                wup_hbm.at[:, pl.ds(half + col, 256)], wu.at[slot, :, pl.ds(256, 256)], wsem.at[slot, 1]
            ),
            pltpu.make_async_copy(wdown_hbm.at[pl.ds(col, 256)], wd.at[slot, pl.ds(0, 256)], wsem.at[slot, 2]),
            pltpu.make_async_copy(
                wdown_hbm.at[pl.ds(half + col, 256)], wd.at[slot, pl.ds(256, 256)], wsem.at[slot, 3]
            ),
        ]

    for cp in weights(0, 0):
        cp.start()
    greet(("c", "x", "a", "b", "y"))
    scatter = Scatter(held, (r1, r2, r3, r4), ss, rs)

    def core_copy(f):
        slot = f % 2
        return pltpu.make_async_remote_copy(
            src_ref=grad.at[slot, 1 - me["c"]], dst_ref=came.at[f], send_sem=cs.at[slot], recv_sem=cr.at[f],
            device_id=partner("c"), device_id_type=MESH,
        )

    def finish_core(f):
        core_copy(f).wait()
        held[f] = grad[f % 2, me["c"]] + came[f]
        scatter.start(f, 0)

    def event(t):
        def last():
            scatter.finish(t - 5, 3)
            for h in range(2):
                gwu[pl.ds(h * 32, 32), pl.ds(pl.multiple_of((t - 5) * 256, 256), 256)] = scatter.result(t - 5, h)

        when(inside(t, 5, steps + 5), last)
        for stage in (2, 1, 0):
            lag = stage + 2

            def step(stage=stage, lag=lag):
                scatter.finish(t - lag, stage)
                scatter.start(t - lag, stage + 1)

            when(inside(t, lag, steps + lag), step)
        when(inside(t, 1, steps + 1), lambda: finish_core(t - 1))

    vec[...] = jnp.zeros(vec.shape, F32)
    vec[7:8] = jnp.sum(cot[...].astype(F32), axis=0, keepdims=True)
    dn2[...] = jnp.zeros(dn2.shape, F32)
    outacc[...] = x2[...] + bdown_ref[...].astype(F32)

    def body(f, carry):
        slot = f % 2
        for cp in weights(f, slot):
            cp.wait()

        @pl.when(f + 1 < steps)
        def _():
            for cp in weights(f + 1, 1 - slot):
                cp.start()

        event(f)
        for yy in range(2):
            cols = slice(yy * 256, (yy + 1) * 256)
            first = pl.multiple_of(yy * half + f * 256, 256)
            bias = bup_ref[:, pl.ds(first, 256)].astype(F32)
            sums = jnp.zeros((1, 256), F32)
            for m in range(tokens // 256):
                rows = slice(m * 256, (m + 1) * 256)
                u = dot(act2[rows], wu[slot, :, cols]) + bias
                dh = dot_nt(cot[rows], wd[slot, cols])
                uu = u * u
                th = jnp.tanh(GELU_C * u * (1.0 + GELU_A * uu))
                half_u = 0.5 * u
                hv = (half_u * (1.0 + th)).astype(BF16)
                slope = 0.5 * (1.0 + th) + half_u * (1.0 - th * th) * (GELU_C * (1.0 + 3.0 * GELU_A * uu))
                dv = (dh * slope).astype(BF16)
                hid[rows, cols] = hv
                dpre[rows, cols] = dv
                hid_t[pl.ds(first, 256), rows] = hv.T
                sums = sums + jnp.sum(dv.astype(F32), axis=0, keepdims=True)
            row = yy * (half // width) + f // (width // 256)
            vec[pl.ds(8 + row, 1), pl.ds(pl.multiple_of((f % (width // 256)) * 256, 256), 256)] = sums
        for yy in range(2):
            cols = slice(yy * 256, (yy + 1) * 256)
            for m in range(width // 256):
                tile = dot(act2t[m * 256 : (m + 1) * 256], dpre[:, cols])
                for q in range(4):
                    place = dp_bits(m * 4 + q)
                    place["y"] = yy
                    for h in range(2):
                        r0 = q * 64 + h * 32
                        grad[slot, place["c"], block_index(h, place)] = tile[r0 : r0 + 32].astype(BF16)
        core_copy(f).start()
        for m in range(tokens // 256):
            rows = slice(m * 256, (m + 1) * 256)
            dn2[rows] += dot_nt(dpre[rows], wu[slot])
            outacc[rows] += dot(hid[rows], wd[slot])
        return carry

    lax.fori_loop(0, steps, body, 0)
    out[...] = outacc[...].astype(BF16)

    def down_copy(kk):
        return pltpu.make_async_remote_copy(
            src_ref=gradd.at[kk, 1 - me["c"]], dst_ref=camed.at[kk], send_sem=dcs.at[kk], recv_sem=dcr.at[kk],
            device_id=partner("c"), device_id_type=MESH,
        )

    for kk in range(2):
        for yy in range(2):
            event(steps + kk * 2 + yy)

            def tiles(m, carry, kk=kk, yy=yy):
                tile = dot(hid_t[pl.ds(pl.multiple_of(m * 256, 256), 256)], cot[:, yy * 512 + kk * 256 : yy * 512 + kk * 256 + 256])
                place = dp_bits(m)
                place["y"] = yy
                for rr in range(4):
                    for h in range(2):
                        r0 = rr * 64 + h * 32
                        gradd[kk, place["c"], rr, block_index(h, place)] = tile[r0 : r0 + 32].astype(BF16)
                return carry

            lax.fori_loop(0, 16, tiles, 0)
        down_copy(kk).start()

    gain2 = g2_ref[...].astype(F32)

    def norm_rows(r, carry):
        rows = pl.ds(pl.multiple_of(r * 64, 64), 64)
        v = x2[rows]
        center = v - jnp.mean(v, axis=-1, keepdims=True)
        inv = lax.rsqrt(jnp.mean(center * center, axis=-1, keepdims=True) + norm_eps)
        normed = center * inv
        dn = dn2[rows]
        e = dn * gain2
        vec[5:6] += jnp.sum(dn * normed, axis=0, keepdims=True)
        vec[6:7] += jnp.sum(dn, axis=0, keepdims=True)
        dx = cot[rows].astype(F32) + inv * (
            e - jnp.mean(e, axis=-1, keepdims=True) - normed * jnp.mean(e * normed, axis=-1, keepdims=True)
        )
        dx2[rows] = dx
        low = dx.astype(BF16)
        ab[rows] = low
        vec[2:3] += jnp.sum(low.astype(F32), axis=0, keepdims=True)
        return carry

    lax.fori_loop(0, tokens // 64, norm_rows, 0)
    event(steps + 4)
    stores = []
    for kk in range(2):
        down_copy(kk).wait()

        def add(rr, carry, kk=kk):
            gradd[kk, me["c"], rr] = gradd[kk, me["c"], rr] + camed[kk, rr]
            return carry

        lax.fori_loop(0, 4, add, 0)
        cp = pltpu.make_async_copy(gradd.at[kk, me["c"]], hd_hbm.at[pl.ds(kk * 4, 4)], dsem.at[kk])
        cp.start()
        stores.append(cp)
    for cp in stores:
        cp.wait()


CHUNKS = 16


def kernel_three(
    halo, x_ref, slope_ref, g1_ref, ab, dx2, qkv, ot, act1t, dist, vec_in, hd_hbm, wqkv_hbm, wout_hbm,
    gin, gwd, gwo, gwqkv, vec,
    do, dqkv, dn1, dnh, dnc, wbuf, wout, grad, came, held, r1, r2, r3, r4, vin,
    wsem, cs, cr, ss, rs, hsem, hs, hr, vs, vr,
):
    tokens, width = ab.shape
    heads = width // HEAD_DIM
    seq = lax.axis_index("seq")
    me = coords()
    load_down = pltpu.make_async_copy(hd_hbm, held.at[pl.ds(0, 8)], hsem.at[0])
    load_down.start()
    load_out = pltpu.make_async_copy(wout_hbm, wout, wsem.at[2])
    load_out.start()
    greet(("c", "x", "a", "b", "y"))
    scatter = Scatter(held, (r1, r2, r3, r4), ss, rs)

    def core_copy(t):
        slot = (t - 8) % 8
        return pltpu.make_async_remote_copy(
            src_ref=grad.at[slot, 1 - me["c"]], dst_ref=came.at[slot], send_sem=cs.at[slot], recv_sem=cr.at[slot],
            device_id=partner("c"), device_id_type=MESH,
        )

    def begin(t):
        if t >= 8:
            core_copy(t).wait()
            held[t] = grad[t - 8, me["c"]] + came[t - 8]
        scatter.start(t, 0)

    def event(t):
        if 4 <= t < CHUNKS + 4:
            n = t - 4
            scatter.finish(n, 3)
            for h in range(2):
                block = scatter.result(n, h)
                if n < 8:
                    gwd[(n % 4) * 64 + h * 32 : (n % 4) * 64 + h * 32 + 32, (n // 4) * 256 : (n // 4) * 256 + 256] = block
                elif n < 10:
                    gwo[h * 32 : h * 32 + 32, (n - 8) * 256 : (n - 8) * 256 + 256] = block
                else:
                    gwqkv[h * 32 : h * 32 + 32, (n - 10) * 256 : (n - 10) * 256 + 256] = block
        for stage in (2, 1, 0):
            n = t - stage - 1
            if 0 <= n < CHUNKS:
                scatter.finish(n, stage)
                scatter.start(n, stage + 1)
        if t + 1 < CHUNKS:
            begin(t + 1)

    load_down.wait()
    begin(0)
    event(0)

    def put(slot, yy, m, tile):
        for q in range(4):
            place = dp_bits(m * 4 + q)
            place["y"] = yy
            for h in range(2):
                r0 = q * 64 + h * 32
                grad[slot, place["c"], block_index(h, place)] = tile[r0 : r0 + 32].astype(BF16)

    for j in range(2):
        for yy in range(2):
            c0 = yy * 512 + j * 256
            for m in range(width // 256):
                put(j, yy, m, dot(ot[m * 256 : (m + 1) * 256], ab[:, c0 : c0 + 256]))
        core_copy(8 + j).start()
    load_out.wait()
    for m in range(tokens // 256):
        rows = slice(m * 256, (m + 1) * 256)
        do[rows] = dot_nt(ab[rows], wout[...]).astype(BF16)
    event(1)

    scale = HEAD_DIM**-0.5
    dqkv[0:halo, 0:width] = jnp.zeros((halo, width), BF16)
    vec[...] = vec_in[...]

    def one_head(h, carry):
        c0 = pl.multiple_of(h * HEAD_DIM, HEAD_DIM)
        slope = slope_ref[pl.ds(h, 1), 0:1]
        parts = []
        for block in range(2):
            rows = slice(halo + block * 256, halo + (block + 1) * 256)
            krows = slice(block * 256, block * 256 + 512)
            q = qkv[rows, pl.ds(c0, HEAD_DIM)]
            k = qkv[krows, pl.ds(width + c0, HEAD_DIM)]
            v = qkv[krows, pl.ds(2 * width + c0, HEAD_DIM)]
            g = do[block * 256 : (block + 1) * 256, pl.ds(c0, HEAD_DIM)]
            s = dot_nt(k, q) * (LOG2E * scale) - slope * dist[block]
            e = jnp.exp2(s - jnp.max(s, axis=0, keepdims=True))
            p = e * (1.0 / jnp.sum(e, axis=0, keepdims=True))
            dp = dot_nt(v, g)
            delta = jnp.sum(p * dp, axis=0, keepdims=True)
            ds = (p * (dp - delta)).astype(BF16)
            dq = (dot_tn(ds, k) * scale).astype(BF16)
            dqkv[rows, pl.ds(c0, HEAD_DIM)] = dq
            dk = dot(ds, q) * scale
            dv = dot(p.astype(BF16), g)
            parts.append((dk, dv))
        for which in range(2):
            cols = pl.ds((1 + which) * width + c0, HEAD_DIM)
            first, second = parts[0][which], parts[1][which]
            dqkv[0:256, cols] = first[0:256].astype(BF16)
            dqkv[256:512, cols] = (first[256:512] + second[0:256]).astype(BF16)
            dqkv[512:768, cols] = second[256:512].astype(BF16)
        return carry

    for group in range(4):
        lax.fori_loop(group * 2, group * 2 + 2, one_head, 0)
        event(2 + group)

    vec[0:1] = jnp.sum(dqkv[halo:, 0:width].astype(F32), axis=0, keepdims=True)
    vec[1:2] = jnp.sum(dqkv[:, 2 * width :].astype(F32), axis=0, keepdims=True)

    for j in range(6):
        for yy in range(2):
            c0 = yy * (3 * width // 2) + j * 256
            for m in range(width // 256):
                put(2 + j, yy, m, dot(act1t[m * 256 : (m + 1) * 256], dqkv[:, c0 : c0 + 256]))
        core_copy(10 + j).start()
        if j % 2 == 1:
            event(6 + j // 2)

    def wload(j, slot):
        return pltpu.make_async_copy(wqkv_hbm.at[:, pl.ds(j * 512, 512)], wbuf.at[slot], wsem.at[slot])

    order = [2, 3, 4, 5, 0, 1]
    wload(order[0], 0).start()
    for i, j in enumerate(order):
        wload(j, i % 2).wait()
        if i + 1 < 6:
            wload(order[i + 1], (i + 1) % 2).start()
        cols = slice(j * 512, (j + 1) * 512)
        if i < 4:
            part = dot_nt(dqkv[0:halo, cols], wbuf[i % 2])
            if i == 0:
                dnh[...] = part
            else:
                dnh[...] += part
        for m in range(tokens // 256):
            part = dot_nt(dqkv[halo + m * 256 : halo + (m + 1) * 256, cols], wbuf[i % 2])
            if i == 0:
                dn1[m * 256 : (m + 1) * 256] = part
            else:
                dn1[m * 256 : (m + 1) * 256] += part
        if i == 3:
            dnc[0] = dnh[...].astype(BF16)

    back = pltpu.make_async_remote_copy(
        src_ref=dnc.at[0], dst_ref=dnc.at[1], send_sem=hs, recv_sem=hr, device_id=partner("y"), device_id_type=MESH,
    )

    @pl.when(seq == 1)
    def _():
        back.start()

    event(9)

    @pl.when(seq == 1)
    def _():
        back.wait_send()

    @pl.when(seq == 0)
    def _():
        back.wait_recv()
        dn1[tokens - halo :] += dnc[1].astype(F32)

    gain1 = g1_ref[...].astype(F32)

    def norm_rows(r, carry):
        rows = pl.ds(pl.multiple_of(r * 64, 64), 64)
        v = x_ref[rows].astype(F32)
        center = v - jnp.mean(v, axis=-1, keepdims=True)
        inv = lax.rsqrt(jnp.mean(center * center, axis=-1, keepdims=True) + norm_eps)
        normed = center * inv
        dn = dn1[rows]
        e = dn * gain1
        vec[3:4] += jnp.sum(dn * normed, axis=0, keepdims=True)
        vec[4:5] += jnp.sum(dn, axis=0, keepdims=True)
        gin[rows] = dx2[rows] + inv * (
            e - jnp.mean(e, axis=-1, keepdims=True) - normed * jnp.mean(e * normed, axis=-1, keepdims=True)
        )
        return carry

    lax.fori_loop(0, tokens // 64, norm_rows, 0)

    def vec_copy(i, kind):
        return pltpu.make_async_remote_copy(
            src_ref=vin.at[i, 0], dst_ref=vin.at[i, 1], send_sem=vs.at[i], recv_sem=vr.at[i],
            device_id=partner(kind), device_id_type=MESH,
        )

    vin[0, 0] = vec[...]
    kinds = ("c", "x", "y", "a", "b")
    for i, kind in enumerate(kinds):
        vec_copy(i, kind).start()
        event(10 + i)
        vec_copy(i, kind).wait()
        total = vin[i, 0] + vin[i, 1]
        if i < 4:
            vin[i + 1, 0] = total
        else:
            vec[...] = total
    for t in range(15, CHUNKS + 4):
        event(t)


def vmem():
    return pl.BlockSpec(memory_space=pltpu.VMEM)


def hbm():
    return pl.BlockSpec(memory_space=pl.ANY)


def shape(dims, dtype):
    return jax.ShapeDtypeStruct(dims, dtype)


DMA = pltpu.SemaphoreType.DMA


def params(cid):
    return pltpu.CompilerParams(collective_id=cid, has_side_effects=True, vmem_limit_bytes=63 * 2**20)


def fast_local(
    inputs, doc_ids, w_qkv, bias_q, bias_v, w_out, bias_out, norm1_gain, norm1_bias, norm2_gain, norm2_bias,
    w_up, bias_up, w_down, bias_down, cotangent,
):
    x = inputs[0]
    tokens, width = x.shape
    ff = w_up.shape[1]
    halo = 256
    ext = tokens + halo
    heads = width // HEAD_DIM
    row = lambda v: v.reshape(1, -1)
    docs = jnp.broadcast_to(doc_ids, (8, tokens))
    slopes = jnp.asarray(
        np.broadcast_to((2.0 ** -(np.arange(heads) + 1.0) * LOG2E)[:, None], (heads, 128)).astype(np.float32)
    )
    act2, act2t, x2, qkv, ot, act1t, dist = pl.pallas_call(
        functools.partial(kernel_one, halo),
        out_shape=(
            shape((tokens, width), BF16), shape((width, tokens), BF16), shape((tokens, width), F32),
            shape((ext, 3 * width), BF16), shape((width, tokens), BF16), shape((width, ext), BF16),
            shape((2, 512, 256), F32),
        ),
        in_specs=[vmem()] * 10 + [hbm()] * 2,
        out_specs=(hbm(),) * 7,
        scratch_shapes=[
            pltpu.VMEM((ext, width), BF16), pltpu.VMEM((width, ext), BF16), pltpu.VMEM((ext, 3 * width), BF16),
            pltpu.VMEM((tokens, width), BF16), pltpu.VMEM((width, tokens), BF16), pltpu.VMEM((tokens, width), BF16),
            pltpu.VMEM((width, tokens), BF16), pltpu.VMEM((tokens, width), F32), pltpu.VMEM((2, 512, 256), F32),
            pltpu.VMEM((halo, width), BF16), pltpu.VMEM((8, tokens), jnp.int32), pltpu.VMEM((1, 3 * width), F32),
            pltpu.VMEM((width, 3 * width), BF16), pltpu.VMEM((width, width), BF16),
            DMA((7,)), DMA((7,)), DMA((2,)), DMA((2,)),
        ],
        compiler_params=params(0),
        name="attention_forward",
    )(
        x, docs, slopes, row(bias_q), row(bias_v), row(bias_out), row(norm1_gain), row(norm1_bias), row(norm2_gain),
        row(norm2_bias), w_qkv, w_out,
    )
    cot = cotangent[0]
    steps = ff // 512
    out, g_w_up, dx2, ab, hd, vec = pl.pallas_call(
        kernel_two,
        out_shape=(
            shape((tokens, width), BF16), shape((width // 16, ff // 2), F32), shape((tokens, width), F32),
            shape((tokens, width), BF16), shape((8, 32, 32, 256), BF16), shape((16, width), F32),
        ),
        in_specs=[vmem()] * 7 + [hbm()] * 2,
        out_specs=(vmem(), vmem(), vmem(), vmem(), hbm(), vmem()),
        scratch_shapes=[
            pltpu.VMEM((ff, tokens), BF16), pltpu.VMEM((tokens, 512), BF16), pltpu.VMEM((tokens, 512), BF16),
            pltpu.VMEM((tokens, width), F32), pltpu.VMEM((tokens, width), F32),
            pltpu.VMEM((2, width, 512), BF16), pltpu.VMEM((2, 512, width), BF16),
            pltpu.VMEM((2, 2, 32, 32, 256), BF16), pltpu.VMEM((steps, 32, 32, 256), BF16),
            pltpu.VMEM((steps, 32, 32, 256), BF16),
        ]
        + arrival_shapes(steps)
        + [
            pltpu.VMEM((2, 2, 4, 32, 32, 256), BF16), pltpu.VMEM((2, 4, 32, 32, 256), BF16),
            DMA((2, 4)), DMA((2,)), DMA((steps,)), DMA((4, steps, 2)), DMA((4, steps, 2)), DMA((2,)), DMA((2,)),
            DMA((2,)),
        ],
        compiler_params=params(1),
        name="feed_forward",
    )(act2, act2t, cot, x2, row(norm2_gain), row(bias_up), row(bias_down), w_up, w_down)

    gin, g_w_down, g_w_out, g_w_qkv, vec = pl.pallas_call(
        functools.partial(kernel_three, halo),
        out_shape=(
            shape((tokens, width), F32), shape((ff // 16, width // 2), F32), shape((width // 16, width // 2), F32),
            shape((width // 16, 3 * width // 2), F32), shape((16, width), F32),
        ),
        in_specs=[vmem()] * 10 + [hbm()] * 3,
        out_specs=(vmem(),) * 5,
        scratch_shapes=[
            pltpu.VMEM((tokens, width), BF16), pltpu.VMEM((ext, 3 * width), BF16), pltpu.VMEM((tokens, width), F32),
            pltpu.VMEM((halo, width), F32), pltpu.VMEM((2, halo, width), BF16), pltpu.VMEM((2, width, 512), BF16),
            pltpu.VMEM((width, width), BF16),
            pltpu.VMEM((8, 2, 32, 32, 256), BF16), pltpu.VMEM((8, 32, 32, 256), BF16),
            pltpu.VMEM((CHUNKS, 32, 32, 256), BF16),
        ]
        + arrival_shapes(CHUNKS)
        + [
            pltpu.VMEM((5, 2, 16, width), F32),
            DMA((3,)), DMA((8,)), DMA((8,)), DMA((4, CHUNKS, 2)), DMA((4, CHUNKS, 2)), DMA((1,)), DMA, DMA,
            DMA((5,)), DMA((5,)),
        ],
        compiler_params=params(2),
        name="attention_backward",
    )(x, slopes, row(norm1_gain), ab, dx2, qkv, ot, act1t, dist, vec, hd, w_qkv, w_out)
    return (
        out[None], gin[None], g_w_qkv, vec[0], vec[1], g_w_out, vec[2], vec[3], vec[4], vec[5], vec[6], g_w_up,
        vec[8 : 8 + ff // width].reshape(ff), g_w_down, vec[7],
    )


def smooth_act(values):
    return jax.nn.gelu(values, approximate=True)


def layer_norm(values, norm_gain, norm_shift):
    center = values - jnp.mean(values, axis=-1, keepdims=True)
    inv_std = lax.rsqrt(jnp.mean(center * center, axis=-1, keepdims=True) + norm_eps)
    normed = center * inv_std
    return (normed * norm_gain + norm_shift, normed, inv_std)


def norm_back(grad_out, normed, inv_std, norm_gain):
    grad_gain = jnp.sum(grad_out * normed, axis=0)
    grad_shift = jnp.sum(grad_out, axis=0)
    inner_grad = grad_out * norm_gain
    grad_in = inv_std * (
        inner_grad
        - jnp.mean(inner_grad, axis=-1, keepdims=True)
        - normed * jnp.mean(inner_grad * normed, axis=-1, keepdims=True)
    )
    return (grad_in, grad_gain, grad_shift)


def block_scores(query_block, key_rows, first_row, head_slope, row_docs):
    block_rows = query_block.shape[0]
    length = key_rows.shape[0]
    raw_scores = lax.dot_general(
        query_block, key_rows, (((1,), (1,)), ((), ())), preferred_element_type=jnp.float32
    )
    query_pos = first_row + jnp.arange(block_rows, dtype=jnp.int32)
    key_pos = jnp.arange(length, dtype=jnp.int32)
    offset = query_pos[:, None] - key_pos[None, :]
    query_doc = lax.dynamic_slice_in_dim(row_docs, first_row, block_rows)
    allowed = (offset >= 0) & (query_doc[:, None] == row_docs[None, :])
    scores = raw_scores * key_rows.shape[1] ** (-0.5) - head_slope * offset.astype(jnp.float32)
    return jnp.where(allowed, scores, masked_score)


def head_forward(query_rows, key_rows, value_rows, head_slope, row_docs, block_rows):
    starts = jnp.arange(query_rows.shape[0] // block_rows, dtype=jnp.int32) * block_rows

    def one_block(first_row):
        query_block = lax.dynamic_slice_in_dim(query_rows, first_row, block_rows)
        scores = block_scores(query_block, key_rows, first_row, head_slope, row_docs)
        row_max = jnp.max(scores, axis=-1, keepdims=True)
        exponent = jnp.exp(scores - row_max)
        row_total = jnp.sum(exponent, axis=-1, keepdims=True)
        weights = (exponent / row_total).astype(jnp.bfloat16)
        block_out = jnp.dot(weights, value_rows, preferred_element_type=jnp.float32).astype(
            jnp.bfloat16
        )
        return (block_out, (row_max + jnp.log(row_total))[:, 0])

    block_outs, log_total = lax.map(one_block, starts)
    return (block_outs.reshape(-1, value_rows.shape[1]), log_total.reshape(-1))


def head_backward(
    query_rows, key_rows, value_rows, grad_rows, log_total, head_slope, row_docs, block_rows
):
    length, head_width = key_rows.shape
    inv_root = head_width ** (-0.5)
    starts = jnp.arange(length // block_rows, dtype=jnp.int32) * block_rows

    def one_block(running, first_row):
        grad_keys, grad_values = running
        query_block = lax.dynamic_slice_in_dim(query_rows, first_row, block_rows)
        grad_block = lax.dynamic_slice_in_dim(grad_rows, first_row, block_rows)
        total_block = lax.dynamic_slice_in_dim(log_total, first_row, block_rows)
        scores = block_scores(query_block, key_rows, first_row, head_slope, row_docs)
        weights = jnp.exp(scores - total_block[:, None])
        grad_weights = lax.dot_general(
            grad_block, value_rows, (((1,), (1,)), ((), ())), preferred_element_type=jnp.float32
        )
        inner_sum = jnp.sum(weights * grad_weights, axis=-1, keepdims=True)
        grad_scores = (weights * (grad_weights - inner_sum)).astype(jnp.bfloat16)
        grad_query = jnp.dot(grad_scores, key_rows, preferred_element_type=jnp.float32) * inv_root
        grad_keys = (
            grad_keys
            + lax.dot_general(
                grad_scores,
                query_block,
                (((0,), (0,)), ((), ())),
                preferred_element_type=jnp.float32,
            )
            * inv_root
        )
        grad_values = grad_values + lax.dot_general(
            weights.astype(jnp.bfloat16),
            grad_block,
            (((0,), (0,)), ((), ())),
            preferred_element_type=jnp.float32,
        )
        return ((grad_keys, grad_values), grad_query)

    zeros_block = jnp.zeros((length, head_width), jnp.float32)
    (grad_keys, grad_values), grad_query = lax.scan(one_block, (zeros_block, zeros_block), starts)
    return (
        grad_query.reshape(length, head_width).astype(jnp.bfloat16),
        grad_keys.astype(jnp.bfloat16),
        grad_values.astype(jnp.bfloat16),
    )


def local(
    inputs,
    doc_ids,
    w_qkv,
    bias_q,
    bias_v,
    w_out,
    bias_out,
    norm1_gain,
    norm1_bias,
    norm2_gain,
    norm2_bias,
    w_up,
    bias_up,
    w_down,
    bias_down,
    cotangent,
):
    model_width = w_out.shape[0]
    tokens = inputs.shape[1]
    head_count = model_width // HEAD_DIM
    float_inputs = inputs[0].astype(jnp.float32)
    gain_one = norm1_gain.astype(jnp.float32)
    gain_two = norm2_gain.astype(jnp.float32)
    normed_in, normed_one, inv_one = layer_norm(
        float_inputs, gain_one, norm1_bias.astype(jnp.float32)
    )
    act_one = normed_in.astype(jnp.bfloat16)
    projected = jnp.dot(act_one, w_qkv, preferred_element_type=jnp.float32)
    query_rows = (projected[:, :model_width] + bias_q.astype(jnp.float32)).astype(jnp.bfloat16)
    key_rows = projected[:, model_width : 2 * model_width].astype(jnp.bfloat16)
    value_rows = (projected[:, 2 * model_width :] + bias_v.astype(jnp.float32)).astype(jnp.bfloat16)
    query_rows = query_rows.reshape(tokens, head_count, HEAD_DIM)
    key_rows = key_rows.reshape(tokens, head_count, HEAD_DIM)
    value_rows = value_rows.reshape(tokens, head_count, HEAD_DIM)
    whole_q, whole_k, whole_v = (
        lax.all_to_all(query_rows, "seq", split_axis=1, concat_axis=0, tiled=True),
        lax.all_to_all(key_rows, "seq", split_axis=1, concat_axis=0, tiled=True),
        lax.all_to_all(value_rows, "seq", split_axis=1, concat_axis=0, tiled=True),
    )
    row_docs = lax.all_gather(doc_ids, "seq", axis=1, tiled=True)[0]
    local_heads = whole_q.shape[1]
    length = whole_q.shape[0]
    block_rows = min(512, length)
    first_head = lax.axis_index("seq") * local_heads
    slopes = jnp.exp2(
        -(first_head + 1 + jnp.arange(local_heads, dtype=jnp.int32)).astype(jnp.float32)
    )
    head_q = jnp.moveaxis(whole_q, 1, 0)
    head_k = jnp.moveaxis(whole_k, 1, 0)
    head_v = jnp.moveaxis(whole_v, 1, 0)

    def forward_head(operands):
        return head_forward(
            operands[0], operands[1], operands[2], operands[3], row_docs, block_rows
        )

    head_outs, head_totals = lax.map(forward_head, (head_q, head_k, head_v, slopes))
    mixed_heads = lax.all_to_all(
        jnp.moveaxis(head_outs, 0, 1), "seq", split_axis=0, concat_axis=1, tiled=True
    )
    mixed_flat = mixed_heads.reshape(tokens, model_width)
    second = (
        float_inputs
        + jnp.dot(mixed_flat, w_out, preferred_element_type=jnp.float32)
        + bias_out.astype(jnp.float32)
    )
    normed_mid, normed_two, inv_two = layer_norm(second, gain_two, norm2_bias.astype(jnp.float32))
    act_two = normed_mid.astype(jnp.bfloat16)
    pre_act = jnp.dot(act_two, w_up, preferred_element_type=jnp.float32) + bias_up.astype(
        jnp.float32
    )
    activated, act_pullback = jax.vjp(smooth_act, pre_act)
    hidden = activated.astype(jnp.bfloat16)
    result = (
        second
        + jnp.dot(hidden, w_down, preferred_element_type=jnp.float32)
        + bias_down.astype(jnp.float32)
    )
    grad_out = cotangent[0].astype(jnp.float32)
    grad_low = grad_out.astype(jnp.bfloat16)
    g_bias_down = jnp.sum(grad_low.astype(jnp.float32), axis=0)
    g_w_down = lax.dot_general(
        hidden, grad_low, (((0,), (0,)), ((), ())), preferred_element_type=jnp.float32
    )
    grad_hidden = lax.dot_general(
        grad_low, w_down, (((1,), (1,)), ((), ())), preferred_element_type=jnp.float32
    )
    grad_pre = act_pullback(grad_hidden)[0].astype(jnp.bfloat16)
    g_bias_up = jnp.sum(grad_pre.astype(jnp.float32), axis=0)
    g_w_up = lax.dot_general(
        act_two, grad_pre, (((0,), (0,)), ((), ())), preferred_element_type=jnp.float32
    )
    grad_norm_two = lax.dot_general(
        grad_pre, w_up, (((1,), (1,)), ((), ())), preferred_element_type=jnp.float32
    )
    grad_mid, g_gain_two, g_shift_two = norm_back(grad_norm_two, normed_two, inv_two, gain_two)
    grad_second = grad_out + grad_mid
    grad_branch = grad_second.astype(jnp.bfloat16)
    g_bias_out = jnp.sum(grad_branch.astype(jnp.float32), axis=0)
    g_w_out = lax.dot_general(
        mixed_flat, grad_branch, (((0,), (0,)), ((), ())), preferred_element_type=jnp.float32
    )
    grad_mixed = lax.dot_general(
        grad_branch, w_out, (((1,), (1,)), ((), ())), preferred_element_type=jnp.float32
    ).astype(jnp.bfloat16)
    grad_whole = lax.all_to_all(
        grad_mixed.reshape(tokens, head_count, HEAD_DIM),
        "seq",
        split_axis=1,
        concat_axis=0,
        tiled=True,
    )
    grad_heads = jnp.moveaxis(grad_whole, 1, 0)

    def backward_head(operands):
        return head_backward(
            operands[0],
            operands[1],
            operands[2],
            operands[3],
            operands[4],
            operands[5],
            row_docs,
            block_rows,
        )

    grad_q, grad_k, grad_v = lax.map(
        backward_head, (head_q, head_k, head_v, grad_heads, head_totals, slopes)
    )
    back_q, back_k, back_v = (
        lax.all_to_all(jnp.moveaxis(grad_q, 0, 1), "seq", split_axis=0, concat_axis=1, tiled=True),
        lax.all_to_all(jnp.moveaxis(grad_k, 0, 1), "seq", split_axis=0, concat_axis=1, tiled=True),
        lax.all_to_all(jnp.moveaxis(grad_v, 0, 1), "seq", split_axis=0, concat_axis=1, tiled=True),
    )
    back_q = back_q.reshape(tokens, model_width)
    back_k = back_k.reshape(tokens, model_width)
    back_v = back_v.reshape(tokens, model_width)
    g_bias_q = jnp.sum(back_q.astype(jnp.float32), axis=0)
    g_bias_v = jnp.sum(back_v.astype(jnp.float32), axis=0)
    grad_proj = jnp.concatenate([back_q, back_k, back_v], axis=1)
    g_w_qkv = lax.dot_general(
        act_one, grad_proj, (((0,), (0,)), ((), ())), preferred_element_type=jnp.float32
    )
    grad_norm_one = lax.dot_general(
        grad_proj, w_qkv, (((1,), (1,)), ((), ())), preferred_element_type=jnp.float32
    )
    grad_first, g_gain_one, g_shift_one = norm_back(grad_norm_one, normed_one, inv_one, gain_one)
    grad_inputs = grad_second + grad_first
    matrices = (g_w_qkv, g_w_out, g_w_up, g_w_down)
    partial_sums = (
        lax.psum_scatter(
            matrices[0].astype(jnp.bfloat16), "dp", scatter_dimension=0, tiled=True
        ).astype(jnp.float32),
        lax.psum_scatter(
            matrices[1].astype(jnp.bfloat16), "dp", scatter_dimension=0, tiled=True
        ).astype(jnp.float32),
        lax.psum_scatter(
            matrices[2].astype(jnp.bfloat16), "dp", scatter_dimension=0, tiled=True
        ).astype(jnp.float32),
        lax.psum_scatter(
            matrices[3].astype(jnp.bfloat16), "dp", scatter_dimension=0, tiled=True
        ).astype(jnp.float32),
    )
    summed = (
        lax.psum_scatter(
            partial_sums[0].astype(jnp.bfloat16), "seq", scatter_dimension=1, tiled=True
        ).astype(jnp.float32),
        lax.psum_scatter(
            partial_sums[1].astype(jnp.bfloat16), "seq", scatter_dimension=1, tiled=True
        ).astype(jnp.float32),
        lax.psum_scatter(
            partial_sums[2].astype(jnp.bfloat16), "seq", scatter_dimension=1, tiled=True
        ).astype(jnp.float32),
        lax.psum_scatter(
            partial_sums[3].astype(jnp.bfloat16), "seq", scatter_dimension=1, tiled=True
        ).astype(jnp.float32),
    )
    vectors = lax.psum(
        (
            g_bias_q,
            g_bias_v,
            g_bias_out,
            g_gain_one,
            g_shift_one,
            g_gain_two,
            g_shift_two,
            g_bias_up,
            g_bias_down,
        ),
        ("dp", "seq"),
    )
    return (
        result.astype(jnp.bfloat16)[None],
        grad_inputs[None],
        summed[0],
        vectors[0],
        vectors[1],
        summed[1],
        vectors[2],
        vectors[3],
        vectors[4],
        vectors[5],
        vectors[6],
        summed[2],
        vectors[7],
        summed[3],
        vectors[8],
    )


def solution(mesh):
    in_specs = (
        P("dp", "seq", None),
        P("dp", "seq"),
        P(),
        P(),
        P(),
        P(),
        P(),
        P(),
        P(),
        P(),
        P(),
        P(),
        P(),
        P(),
        P(),
        P("dp", "seq", None),
    )
    out_specs = (
        P("dp", "seq", None),
        P("dp", "seq", None),
        P("dp", "seq"),
        P(),
        P(),
        P("dp", "seq"),
        P(),
        P(),
        P(),
        P(),
        P(),
        P("dp", "seq"),
        P(),
        P("dp", "seq"),
        P(),
    )
    sizes = (mesh.shape["dp"], mesh.shape["seq"])
    chosen = fast_local if sizes == (16, 2) else local
    return jax.shard_map(chosen, mesh=mesh, in_specs=in_specs, out_specs=out_specs, check_vma=False)
```

```python
import functools

import jax
import jax.numpy as jnp
import numpy as np
from jax import lax
from jax.experimental import pallas as pl
from jax.experimental.pallas import tpu as pltpu
from jax.sharding import PartitionSpec as P

HEAD_DIM = 128
MESH = pl.DeviceIdType.MESH
F32 = jnp.float32
BF16 = jnp.bfloat16
LOG2E = 1.4426950408889634
FAR = 1e30
GELU_C = 0.7978845608028654
GELU_A = 0.044715

norm_eps = 1e-05
masked_score = -1e30

NT = (((1,), (1,)), ((), ()))
TN = (((0,), (0,)), ((), ()))


def dot(a, b):
    return jnp.dot(a, b, preferred_element_type=F32)


def dot_nt(a, b):
    return lax.dot_general(a, b, NT, preferred_element_type=F32)


def dot_tn(a, b):
    return lax.dot_general(a, b, TN, preferred_element_type=F32)


def coords():
    dp = lax.axis_index("dp")
    return {
        "c": dp % 2,
        "x": (dp // 2) % 2,
        "a": (dp // 4) % 2,
        "b": dp // 8,
        "y": lax.axis_index("seq"),
    }


def partner(kind):
    dp = lax.axis_index("dp")
    if kind == "y":
        return {"seq": 1 - lax.axis_index("seq")}
    step = {"c": 1, "x": 2, "a": 4, "b": 8}[kind]
    bit = (dp // step) % 2
    return {"dp": dp + step - 2 * step * bit}


def greet(kinds):
    barrier = pltpu.get_barrier_semaphore()
    for kind in kinds:
        pl.semaphore_signal(barrier, inc=1, device_id=partner(kind), device_id_type=MESH)
    pl.semaphore_wait(barrier, len(kinds))


ORDERS = (("x", "a", "y", "b"), ("y", "a", "x", "b"))


def block_index(half, place):
    index = half * 16
    for kind, weight in zip(ORDERS[half], (8, 4, 2, 1)):
        index = index + place[kind] * weight
    return index


def dp_bits(dp):
    return {"c": dp % 2, "x": (dp // 2) % 2, "a": (dp // 4) % 2, "b": dp // 8}


class Scatter:
    def __init__(self, held, arrivals, send_sem, recv_sem):
        self.held, self.arrivals = held, arrivals
        self.send_sem, self.recv_sem = send_sem, recv_sem
        self.me = coords()

    def offset(self, half, stage, other):
        index = half * 16
        for k, weight in zip(range(stage + 1), (8, 4, 2, 1)):
            bit = self.me[ORDERS[half][k]]
            if other and k == stage:
                bit = 1 - bit
            index = index + bit * weight
        return index

    def copy(self, chunk, stage, half):
        size = 8 >> stage
        return pltpu.make_async_remote_copy(
            src_ref=self.held.at[chunk, pl.ds(self.offset(half, stage, True), size)],
            dst_ref=self.arrivals[stage].at[chunk, half],
            send_sem=self.send_sem.at[stage, chunk, half],
            recv_sem=self.recv_sem.at[stage, chunk, half],
            device_id=partner(ORDERS[half][stage]),
            device_id_type=MESH,
        )

    def start(self, chunk, stage):
        for half in range(2):
            self.copy(chunk, stage, half).start()

    def finish(self, chunk, stage):
        size = 8 >> stage
        for half in range(2):
            self.copy(chunk, stage, half).wait()
            mine = pl.ds(self.offset(half, stage, False), size)
            self.held[chunk, mine] = self.held[chunk, mine] + self.arrivals[stage][chunk, half]

    def result(self, chunk, half):
        return self.held[chunk, self.offset(half, 3, False)]


def arrival_shapes(chunks):
    return [pltpu.VMEM((chunks, 2, 8 >> k, 32, 256), BF16) for k in range(4)]


def when(cond, fn):
    if isinstance(cond, (bool, np.bool_)):
        if cond:
            fn()
    else:
        pl.when(cond)(fn)


def inside(value, low, high):
    if isinstance(value, int):
        return low <= value < high
    return (value >= low) & (value < high)


RING = 3
AHEAD = 3


def row_of(ref):
    return ref[...].astype(F32).reshape(1, -1)


def layer_kernel(
    halo, x_ref, doc_ref, slope_ref, bq_ref, bv_ref, bo_ref, g1_ref, s1_ref, g2_ref, s2_ref, bup_ref, bdown_ref,
    cot_hbm, wqkv_hbm, wout_hbm, wup_hbm, wdown_hbm,
    out_hbm, gin_hbm, gup, gdown, gout, gqkv, vec,
    qkv, act1t, ot, dist, doch, x2, cot, act2, act2t, hid_t, dpre, dn2, dn1, dnh, dqkv, wu, wd, bias, bup,
    grad, held, r1, r2, r3, r4, vin,
    qsem, osem, wsem, csem, cs, cr, ss, rs, hs, hr, vs, vr, esem,
):
    tokens, width = x_ref.shape
    heads = width // HEAD_DIM
    ff = wup_hbm.shape[1]
    half_ff = ff // 2
    steps = half_ff // 256
    seq = lax.axis_index("seq")
    me = coords()
    first_down, first_out, first_qkv, chunks = steps, 2 * steps, 2 * steps + 2, 2 * steps + 8
    scale = HEAD_DIM**-0.5

    act1 = dqkv.at[:, pl.ds(0, width)]
    o_s = dqkv.at[pl.ds(halo, tokens), pl.ds(width, width)]
    xh = dqkv.at[pl.ds(0, halo), pl.ds(2 * width, width)]
    wout_low = dqkv.at[pl.ds(halo, 512), pl.ds(2 * width, width)]

    dn_come = qkv.at[pl.ds(0, halo), pl.ds(0, width)]
    dn_send = qkv.at[pl.ds(0, halo), pl.ds(width, width)]

    def wqkv_part(j):
        return wu.at[j] if j < 2 else hid_t.at[pl.ds((j - 2) * width, width)]

    qloads = [
        pltpu.make_async_copy(wqkv_hbm.at[:, pl.ds(j * 512, 512)], wqkv_part(j), qsem.at[j]) for j in range(6)
    ]
    oloads = [
        pltpu.make_async_copy(wout_hbm.at[pl.ds(0, 512)], wout_low, osem.at[0]),
        pltpu.make_async_copy(wout_hbm.at[pl.ds(512, 512)], wd.at[1], osem.at[1]),
    ]
    cload = pltpu.make_async_copy(cot_hbm, cot, csem)
    for cp in qloads + oloads + [cload]:
        cp.start()
    greet(("c", "x", "a", "b", "y"))
    send_x = pltpu.make_async_remote_copy(
        src_ref=x_ref.at[pl.ds(tokens - halo, halo)], dst_ref=xh, send_sem=hs.at[0], recv_sem=hr.at[0],
        device_id=partner("y"), device_id_type=MESH,
    )
    send_doc = pltpu.make_async_remote_copy(
        src_ref=doc_ref, dst_ref=doch, send_sem=hs.at[1], recv_sem=hr.at[1],
        device_id=partner("y"), device_id_type=MESH,
    )

    @pl.when(seq == 0)
    def _():
        send_doc.start()
        send_x.start()

    def weights(f, slot):
        col = pl.multiple_of(f * 256, 256)
        return [
            pltpu.make_async_copy(wup_hbm.at[:, pl.ds(col, 256)], wu.at[slot, :, pl.ds(0, 256)], wsem.at[slot, 0]),
            pltpu.make_async_copy(
                wup_hbm.at[:, pl.ds(half_ff + col, 256)], wu.at[slot, :, pl.ds(256, 256)], wsem.at[slot, 1]
            ),
            pltpu.make_async_copy(wdown_hbm.at[pl.ds(col, 256)], wd.at[slot, pl.ds(0, 256)], wsem.at[slot, 2]),
            pltpu.make_async_copy(
                wdown_hbm.at[pl.ds(half_ff + col, 256)], wd.at[slot, pl.ds(256, 256)], wsem.at[slot, 3]
            ),
        ]

    scatter = Scatter(held, (r1, r2, r3, r4), ss, rs)

    def core_copy(n):
        return pltpu.make_async_remote_copy(
            src_ref=grad.at[n % RING, 1 - me["c"]], dst_ref=held.at[n], send_sem=cs.at[n % RING], recv_sem=cr.at[n],
            device_id=partner("c"), device_id_type=MESH,
        )

    def join(n):
        core_copy(n).wait()
        held[n] = held[n] + grad[n % RING, me["c"]]

    def put(n, yy, m, tile):
        for q in range(4):
            place = dp_bits(m * 4 + q)
            place["y"] = yy
            for h in range(2):
                r0 = q * 64 + h * 32
                grad[n % RING, place["c"], block_index(h, place)] = tile[r0 : r0 + 32].astype(BF16)

    def store(n):
        for h in range(2):
            block = scatter.result(n, h)

            def up():
                gup[h * 32 : h * 32 + 32, pl.ds(pl.multiple_of(n * 256, 256), 256)] = block

            def down():
                i = n - first_down
                row = pl.multiple_of((i % 4) * 64 + h * 32, 32)
                gdown[pl.ds(row, 32), pl.ds(pl.multiple_of((i // 4) * 256, 256), 256)] = block

            def outp():
                gout[h * 32 : h * 32 + 32, pl.ds(pl.multiple_of((n - first_out) * 256, 256), 256)] = block

            def proj():
                gqkv[h * 32 : h * 32 + 32, pl.ds(pl.multiple_of((n - first_qkv) * 256, 256), 256)] = block

            when(inside(n, 0, first_down), up)
            when(inside(n, first_down, first_out), down)
            when(inside(n, first_out, first_qkv), outp)
            when(inside(n, first_qkv, chunks), proj)

    def service(t, ahead=True):
        if ahead:
            when(inside(t + AHEAD, 0, chunks), lambda: scatter.start(t + AHEAD, 0))

        def last():
            scatter.finish(t - 6, 3)
            store(t - 6)

        when(inside(t - 6, 0, chunks), last)
        for stage in (2, 1, 0):
            n = t - 2 * stage

            def step(stage=stage, n=n):
                scatter.finish(n, stage)
                scatter.start(n, stage + 1)

            when(inside(n, 0, chunks), step)

    gain1, shift1 = row_of(g1_ref), row_of(s1_ref)
    gain2, shift2 = row_of(g2_ref), row_of(s2_ref)

    def norm(v, gain, shift):
        center = v - jnp.mean(v, axis=-1, keepdims=True)
        inv = lax.rsqrt(jnp.mean(center * center, axis=-1, keepdims=True) + norm_eps)
        return center * inv * gain + shift

    bias[:, 0:width] = row_of(bq_ref)
    bias[:, width : 2 * width] = jnp.zeros((1, width), F32)
    bias[:, 2 * width :] = row_of(bv_ref)
    bup[...] = row_of(bup_ref)

    for r in range(tokens // 128):
        v = norm(x_ref[r * 128 : (r + 1) * 128].astype(F32), gain1, shift1).astype(BF16)
        act1[halo + r * 128 : halo + (r + 1) * 128] = v
        act1t[:, halo + r * 128 : halo + (r + 1) * 128] = v.T

    for j in range(6):
        qloads[j].wait()
        cols = slice(j * 512, (j + 1) * 512)
        for m in range(tokens // 256):
            rows = slice(halo + m * 256, halo + (m + 1) * 256)
            qkv[rows, cols] = (dot(act1[rows], wqkv_part(j)[...]) + bias[:, cols]).astype(BF16)
    for cp in weights(0, 0):
        cp.start()

    own_doc = doc_ref[...].astype(F32)
    own_cols = jnp.transpose(jnp.broadcast_to(own_doc, (128, tokens)))[:, 0:1]

    def distances(block, key_docs):
        keys = key_docs[block * 256 : block * 256 + 512]
        queries = own_doc[:, block * 256 : block * 256 + 256]
        key_pos = lax.broadcasted_iota(jnp.int32, (512, 256), 0)
        query_pos = lax.broadcasted_iota(jnp.int32, (512, 256), 1) + 256
        gap = query_pos - key_pos
        allowed = (gap >= 0) & (keys == queries)
        dist[block] = jnp.where(allowed, gap.astype(F32), FAR)

    def attend(block):
        def some_heads(i, carry):
            for u in range(FWD_HEADS):
                h = i * FWD_HEADS + u
                c0 = pl.multiple_of(h * HEAD_DIM, HEAD_DIM)
                q = qkv[halo + block * 256 : halo + (block + 1) * 256, pl.ds(c0, HEAD_DIM)]
                k = qkv[block * 256 : block * 256 + 512, pl.ds(width + c0, HEAD_DIM)]
                v = qkv[block * 256 : block * 256 + 512, pl.ds(2 * width + c0, HEAD_DIM)]
                slope = slope_ref[pl.ds(h, 1), 0:1]
                s = dot_nt(k, q) * (LOG2E * scale) - slope * dist[block]
                e = jnp.exp2(s - jnp.max(s, axis=0, keepdims=True))
                p = (e * (1.0 / jnp.sum(e, axis=0, keepdims=True))).astype(BF16)
                o_t = dot_tn(v, p)
                ot[pl.ds(c0, HEAD_DIM), block * 256 : (block + 1) * 256] = o_t.astype(BF16)
                o_s[block * 256 : (block + 1) * 256, pl.ds(c0, HEAD_DIM)] = o_t.T.astype(BF16)
            return carry

        lax.fori_loop(0, heads // FWD_HEADS, some_heads, 0)

    def project(block):
        for r in range(2):
            rows = slice(block * 256 + r * 128, block * 256 + (r + 1) * 128)
            second = (
                x_ref[rows].astype(F32) + dot(o_s[rows, 0:512], wout_low[...]) + dot(o_s[rows, 512:1024], wd[1])
            ) + row_of(bo_ref)
            x2[rows] = second
            v = norm(second, gain2, shift2).astype(BF16)
            act2[rows] = v
            act2t[:, rows] = v.T

    distances(1, jnp.concatenate([jnp.full((halo, 1), -1.0, F32), own_cols], axis=0))
    attend(1)
    for cp in oloads:
        cp.wait()
    project(1)

    @pl.when(seq == 0)
    def _():
        send_doc.wait_send()
        send_x.wait_send()
        doch[...] = jnp.full(doch.shape, -1, jnp.int32)
        act1t[:, 0:halo] = jnp.zeros((width, halo), BF16)
        qkv[0:halo, width:] = jnp.zeros((halo, 2 * width), BF16)

    @pl.when(seq == 1)
    def _():
        send_doc.wait_recv()
        send_x.wait_recv()
        for r in range(halo // 128):
            v = norm(xh[r * 128 : (r + 1) * 128].astype(F32), gain1, shift1).astype(BF16)
            act1[r * 128 : (r + 1) * 128] = v
            act1t[:, r * 128 : (r + 1) * 128] = v.T
        for j in range(2, 6):
            cols = slice(j * 512, (j + 1) * 512)
            qkv[0:halo, cols] = (dot(act1[0:halo], wqkv_part(j)[...]) + bias[:, cols]).astype(BF16)

    halo_doc = doch[...].astype(F32)[:, tokens - halo :]
    halo_cols = jnp.transpose(jnp.broadcast_to(halo_doc, (128, halo)))[:, 0:1]
    distances(0, jnp.concatenate([halo_cols, own_cols], axis=0))
    attend(0)
    project(0)

    cload.wait()
    vec[...] = jnp.zeros(vec.shape, F32)
    vec[7:8] = jnp.sum(cot[...].astype(F32), axis=0, keepdims=True)
    dn2[...] = jnp.zeros(dn2.shape, F32)

    def ff_step(f, carry):
        slot = f % 2
        for cp in weights(f, slot):
            cp.wait()

        @pl.when(f + 1 < steps)
        def _():
            for cp in weights(f + 1, 1 - slot):
                cp.start()

        for yy in range(2):
            cols = slice(yy * 256, (yy + 1) * 256)
            first = pl.multiple_of(yy * half_ff + f * 256, 256)
            shift = bup[:, pl.ds(first, 256)]
            sums = jnp.zeros((1, 256), F32)
            for m in range(tokens // 256):
                rows = slice(m * 256, (m + 1) * 256)
                u = dot(act2[rows], wu[slot, :, cols]) + shift
                dh = dot_nt(cot[rows], wd[slot, cols])
                uu = u * u
                th = jnp.tanh(GELU_C * u * (1.0 + GELU_A * uu))
                half_u = 0.5 * u
                hv = (half_u * (1.0 + th)).astype(BF16)
                slope = 0.5 * (1.0 + th) + half_u * (1.0 - th * th) * (GELU_C * (1.0 + 3.0 * GELU_A * uu))
                dv = (dh * slope).astype(BF16)
                dpre[rows, cols] = dv
                hid_t[pl.ds(first, 256), rows] = hv.T
                sums = sums + jnp.sum(dv.astype(F32), axis=0, keepdims=True)
            row = yy * (half_ff // width) + f // (width // 256)
            vec[pl.ds(8 + row, 1), pl.ds(pl.multiple_of((f % (width // 256)) * 256, 256), 256)] = sums

        @pl.when(f >= 1)
        def _():
            join(f - 1)
            scatter.start(f - 1, 0)

        for yy in range(2):
            cols = slice(yy * 256, (yy + 1) * 256)
            for m in range(width // 256):
                put(f, yy, m, dot(act2t[m * 256 : (m + 1) * 256], dpre[:, cols]))
        core_copy(f).start()
        for m in range(tokens // 256):
            rows = slice(m * 256, (m + 1) * 256)
            dn2[rows] += dot_nt(dpre[rows], wu[slot])
        service(f - 3, ahead=False)
        return carry

    lax.fori_loop(0, steps, ff_step, 0)
    join(steps - 1)
    scatter.start(steps - 1, 0)
    oloads = [pltpu.make_async_copy(wout_hbm.at[pl.ds(i * 512, 512)], wd.at[i], osem.at[i]) for i in range(2)]
    order = (2, 3, 4, 5, 0, 1)

    def qload(i):
        return pltpu.make_async_copy(wqkv_hbm.at[:, pl.ds(order[i] * 512, 512)], wu.at[i % 2], qsem.at[i % 2])

    for cp in oloads + [qload(0), qload(1)]:
        cp.start()

    def down_step(i, carry):
        n = first_down + i
        for yy in range(2):
            right = cot[:, pl.ds(pl.multiple_of(yy * 512 + (i // 4) * 256, 256), 256)]
            for m in range(4):
                left = jnp.concatenate(
                    [
                        hid_t[pl.ds(pl.multiple_of((m * 4 + q) * 256 + (i % 4) * 64, 64), 64)]
                        for q in range(4)
                    ],
                    axis=0,
                )
                put(n, yy, m, dot(left, right))
        core_copy(n).start()

        @pl.when(i >= 1)
        def _():
            join(n - 1)

        for at, t in ((2, steps - 3), (5, steps - 2), (7, steps - 1)):

            @pl.when(i == at)
            def _(t=t):
                service(t)

        return carry

    lax.fori_loop(0, steps, down_step, 0)
    join(first_out - 1)

    def norm_two(r, carry):
        rows = pl.ds(pl.multiple_of(r * 64, 64), 64)
        v = x2[rows]
        center = v - jnp.mean(v, axis=-1, keepdims=True)
        inv = lax.rsqrt(jnp.mean(center * center, axis=-1, keepdims=True) + norm_eps)
        normed = center * inv
        dn = dn2[rows]
        e = dn * gain2
        vec[5:6] += jnp.sum(dn * normed, axis=0, keepdims=True)
        vec[6:7] += jnp.sum(dn, axis=0, keepdims=True)
        dx = cot[rows].astype(F32) + inv * (
            e - jnp.mean(e, axis=-1, keepdims=True) - normed * jnp.mean(e * normed, axis=-1, keepdims=True)
        )
        dn2[rows] = dx
        low = dx.astype(BF16)
        cot[rows] = low
        vec[2:3] += jnp.sum(low.astype(F32), axis=0, keepdims=True)
        return carry

    lax.fori_loop(0, tokens // 64, norm_two, 0)
    dx2, ab, do = dn2, cot, act2
    service(steps)

    for j in range(2):
        for yy in range(2):
            c0 = yy * 512 + j * 256
            for m in range(width // 256):
                put(first_out + j, yy, m, dot(ot[m * 256 : (m + 1) * 256], ab[:, c0 : c0 + 256]))
        core_copy(first_out + j).start()
    service(steps + 1)
    for cp in oloads:
        cp.wait()
    for m in range(tokens // 256):
        rows = slice(m * 256, (m + 1) * 256)
        for i in range(2):
            do[rows, i * 512 : (i + 1) * 512] = dot_nt(ab[rows], wd[i]).astype(BF16)

    def dload(i):
        return pltpu.make_async_copy(wdown_hbm.at[pl.ds(i * 512, 512)], wd.at[i % 2], osem.at[i % 2])

    dload(0).start()
    dload(1).start()
    join(first_out)
    join(first_out + 1)
    service(steps + 2)

    dqkv[0:halo, 0:width] = jnp.zeros((halo, width), BF16)

    def head_back(h):
        c0 = pl.multiple_of(h * HEAD_DIM, HEAD_DIM)
        slope = slope_ref[pl.ds(h, 1), 0:1]
        parts = []
        for block in range(2):
            rows = slice(halo + block * 256, halo + (block + 1) * 256)
            krows = slice(block * 256, block * 256 + 512)
            q = qkv[rows, pl.ds(c0, HEAD_DIM)]
            k = qkv[krows, pl.ds(width + c0, HEAD_DIM)]
            v = qkv[krows, pl.ds(2 * width + c0, HEAD_DIM)]
            g = do[block * 256 : (block + 1) * 256, pl.ds(c0, HEAD_DIM)]
            s = dot_nt(k, q) * (LOG2E * scale) - slope * dist[block]
            e = jnp.exp2(s - jnp.max(s, axis=0, keepdims=True))
            p = e * (1.0 / jnp.sum(e, axis=0, keepdims=True))
            dp = dot_nt(v, g)
            delta = jnp.sum(p * dp, axis=0, keepdims=True)
            ds = (p * (dp - delta)).astype(BF16)
            dqkv[rows, pl.ds(c0, HEAD_DIM)] = (dot_tn(ds, k) * scale).astype(BF16)
            parts.append((dot(ds, q) * scale, dot(p.astype(BF16), g)))
        for which in range(2):
            cols = pl.ds((1 + which) * width + c0, HEAD_DIM)
            first, second = parts[0][which], parts[1][which]
            dqkv[0:256, cols] = first[0:256].astype(BF16)
            dqkv[256:512, cols] = (first[256:512] + second[0:256]).astype(BF16)
            dqkv[512:768, cols] = second[256:512].astype(BF16)

    def heads_back(i, carry):
        for u in range(2):
            head_back(i * 2 + u)
        service(steps + 3 + i)
        return carry

    lax.fori_loop(0, heads // 2, heads_back, 0)
    vec[0:1] = jnp.sum(dqkv[halo:, 0:width].astype(F32), axis=0, keepdims=True)
    vec[1:2] = jnp.sum(dqkv[:, 2 * width :].astype(F32), axis=0, keepdims=True)

    t0 = steps + 3 + heads // 2
    for j in range(6):
        n = first_qkv + j
        for yy in range(2):
            c0 = yy * (3 * width // 2) + j * 256
            for m in range(width // 256):
                put(n, yy, m, dot(act1t[m * 256 : (m + 1) * 256], dqkv[:, c0 : c0 + 256]))
        core_copy(n).start()
        if j >= 1:
            join(n - 1)
        if j % 2 == 1:
            service(t0)
            t0 += 1
    join(chunks - 1)

    for i, j in enumerate(order):
        qload(i).wait()
        cols = slice(j * 512, (j + 1) * 512)
        if i < 4:
            part = dot_nt(dqkv[0:halo, cols], wu[i % 2])
            if i == 0:
                dnh[...] = part
            else:
                dnh[...] += part
        for m in range(tokens // 256):
            part = dot_nt(dqkv[halo + m * 256 : halo + (m + 1) * 256, cols], wu[i % 2])
            if i == 0:
                dn1[m * 256 : (m + 1) * 256] = part
            else:
                dn1[m * 256 : (m + 1) * 256] += part
        if i + 2 < 6:
            qload(i + 2).start()
        if i == 3:
            dn_send[...] = dnh[...].astype(BF16)
            back = pltpu.make_async_remote_copy(
                src_ref=dn_send, dst_ref=dn_come, send_sem=hs.at[2], recv_sem=hr.at[2],
                device_id=partner("y"), device_id_type=MESH,
            )

            @pl.when(seq == 1)
            def _():
                back.start()

        if i % 2 == 1:
            service(t0)
            t0 += 1

    def out_part(i):
        dload(i).wait()
        for m in range(tokens // 256):
            rows = slice(m * 256, (m + 1) * 256)
            part = dot_tn(hid_t[i * 512 : (i + 1) * 512, rows], wd[i % 2])
            if i == 0:
                part = part + row_of(bdown_ref)
            if i < 7:
                x2[rows] += part
            else:
                act2[rows] = (x2[rows] + part).astype(BF16)
        if i + 2 < 8:
            dload(i + 2).start()

    for i in range(4):
        out_part(i)
    service(t0)
    t0 += 1

    @pl.when(seq == 1)
    def _():
        back.wait_send()

    @pl.when(seq == 0)
    def _():
        back.wait_recv()
        dn1[tokens - halo :] += dn_come[...].astype(F32)

    def norm_one(r, carry):
        rows = pl.ds(pl.multiple_of(r * 64, 64), 64)
        v = x_ref[rows].astype(F32)
        center = v - jnp.mean(v, axis=-1, keepdims=True)
        inv = lax.rsqrt(jnp.mean(center * center, axis=-1, keepdims=True) + norm_eps)
        normed = center * inv
        dn = dn1[rows]
        e = dn * gain1
        vec[3:4] += jnp.sum(dn * normed, axis=0, keepdims=True)
        vec[4:5] += jnp.sum(dn, axis=0, keepdims=True)
        dn1[rows] = dx2[rows] + inv * (
            e - jnp.mean(e, axis=-1, keepdims=True) - normed * jnp.mean(e * normed, axis=-1, keepdims=True)
        )
        return carry

    lax.fori_loop(0, tokens // 64, norm_one, 0)
    save_gin = pltpu.make_async_copy(dn1, gin_hbm, esem.at[0])
    save_gin.start()

    kinds = ("c", "x", "y", "a", "b")

    def vec_copy(i):
        return pltpu.make_async_remote_copy(
            src_ref=vin.at[i, 0], dst_ref=vin.at[i, 1], send_sem=vs.at[i], recv_sem=vr.at[i],
            device_id=partner(kinds[i]), device_id_type=MESH,
        )

    vin[0, 0] = vec[...]
    vec_copy(0).start()
    for i in range(5):
        if i < 4:
            out_part(4 + i)
        if t0 < chunks:
            service(t0)
            t0 += 1
        vec_copy(i).wait()
        total = vin[i, 0] + vin[i, 1]
        if i < 4:
            vin[i + 1, 0] = total
            vec_copy(i + 1).start()
        else:
            vec[...] = total
        if i == 3:
            save_out = pltpu.make_async_copy(act2, out_hbm, esem.at[1])
            save_out.start()
    for t in range(t0, chunks + 6):
        service(t)
    save_gin.wait()
    save_out.wait()


def finish_kernel(out_in, gin_in, gup, gdown, gout, gqkv, vec, *refs):
    out, gin, o_qkv, bq, bv, o_out, bo, g1, s1, g2, s2, o_up, b_up, o_down, b_down = refs
    out[...] = out_in[...]
    gin[...] = gin_in[...]
    o_qkv[...] = gqkv[...].astype(F32)
    o_out[...] = gout[...].astype(F32)
    o_up[...] = gup[...].astype(F32)
    o_down[...] = gdown[...].astype(F32)
    width = vec.shape[1]
    for i, ref in enumerate((bq, bv, bo, g1, s1, g2, s2, b_down)):
        ref[...] = vec[i]
    for i in range(b_up.shape[0] // width):
        b_up[i * width : (i + 1) * width] = vec[8 + i]


FWD_HEADS = 2


def vmem():
    return pl.BlockSpec(memory_space=pltpu.VMEM)


def hbm():
    return pl.BlockSpec(memory_space=pl.ANY)


def shape(dims, dtype):
    return jax.ShapeDtypeStruct(dims, dtype)


DMA = pltpu.SemaphoreType.DMA


def params(cid):
    return pltpu.CompilerParams(collective_id=cid, has_side_effects=True, vmem_limit_bytes=64 * 2**20 - 2**16)


def fast_local(
    inputs, doc_ids, w_qkv, bias_q, bias_v, w_out, bias_out, norm1_gain, norm1_bias, norm2_gain, norm2_bias,
    w_up, bias_up, w_down, bias_down, cotangent,
):
    x = inputs[0]
    tokens, width = x.shape
    ff = w_up.shape[1]
    halo = 256
    ext = tokens + halo
    heads = width // HEAD_DIM
    steps = ff // 512
    chunks = 2 * steps + 8
    slopes = jnp.asarray(
        np.broadcast_to((2.0 ** -(np.arange(heads) + 1.0) * LOG2E)[:, None], (heads, 128)).astype(np.float32)
    )
    shards = (
        (width // 16, ff // 2), (ff // 16, width // 2), (width // 16, width // 2), (width // 16, 3 * width // 2),
    )
    out, gin, g_up, g_down, g_out, g_qkv, vec = pl.pallas_call(
        functools.partial(layer_kernel, halo),
        out_shape=(shape((tokens, width), BF16), shape((tokens, width), F32))
        + tuple(shape(dims, BF16) for dims in shards)
        + (shape((16, width), F32),),
        in_specs=[vmem()] * 12 + [hbm()] * 5,
        out_specs=(hbm(),) * 2 + (vmem(),) * 5,
        scratch_shapes=[
            pltpu.VMEM((ext, 3 * width), BF16),
            pltpu.VMEM((width, ext), BF16),
            pltpu.VMEM((width, tokens), BF16),
            pltpu.VMEM((2, 512, 256), F32),
            pltpu.VMEM((1, tokens), jnp.int32),
            pltpu.VMEM((tokens, width), F32),
            pltpu.VMEM((tokens, width), BF16),
            pltpu.VMEM((tokens, width), BF16),
            pltpu.VMEM((width, tokens), BF16),
            pltpu.VMEM((ff, tokens), BF16),
            pltpu.VMEM((tokens, 512), BF16),
            pltpu.VMEM((tokens, width), F32),
            pltpu.VMEM((tokens, width), F32),
            pltpu.VMEM((halo, width), F32),
            pltpu.VMEM((ext, 3 * width), BF16),
            pltpu.VMEM((2, width, 512), BF16),
            pltpu.VMEM((2, 512, width), BF16),
            pltpu.VMEM((1, 3 * width), F32),
            pltpu.VMEM((1, ff), F32),
            pltpu.VMEM((RING, 2, 32, 32, 256), BF16),
            pltpu.VMEM((chunks, 32, 32, 256), BF16),
        ]
        + arrival_shapes(chunks)
        + [
            pltpu.VMEM((5, 2, 16, width), F32),
            DMA((6,)), DMA((2,)), DMA((2, 4)), DMA, DMA((RING,)), DMA((chunks,)), DMA((4, chunks, 2)),
            DMA((4, chunks, 2)), DMA((3,)), DMA((3,)), DMA((5,)), DMA((5,)), DMA((2,)),
        ],
        compiler_params=params(0),
        name="layer",
    )(
        x, doc_ids, slopes, bias_q, bias_v, bias_out, norm1_gain, norm1_bias, norm2_gain, norm2_bias, bias_up, bias_down,
        cotangent[0], w_qkv, w_out, w_up, w_down,
    )
    row = shape((width,), F32)
    return_shapes = (
        shape((tokens, width), BF16), shape((tokens, width), F32), shape(shards[3], F32), row, row, shape(shards[2], F32),
        row, row, row, row, row, shape(shards[0], F32), shape((ff,), F32), shape(shards[1], F32), row,
    )
    results = pl.pallas_call(
        finish_kernel,
        out_shape=return_shapes,
        in_specs=[vmem()] * 7,
        out_specs=(vmem(),) * 15,
        name="hand_over",
    )(out, gin, g_up, g_down, g_out, g_qkv, vec)
    return (results[0][None], results[1][None]) + tuple(results[2:])


def smooth_act(values):
    return jax.nn.gelu(values, approximate=True)


def layer_norm(values, norm_gain, norm_shift):
    center = values - jnp.mean(values, axis=-1, keepdims=True)
    inv_std = lax.rsqrt(jnp.mean(center * center, axis=-1, keepdims=True) + norm_eps)
    normed = center * inv_std
    return (normed * norm_gain + norm_shift, normed, inv_std)


def norm_back(grad_out, normed, inv_std, norm_gain):
    grad_gain = jnp.sum(grad_out * normed, axis=0)
    grad_shift = jnp.sum(grad_out, axis=0)
    inner_grad = grad_out * norm_gain
    grad_in = inv_std * (
        inner_grad
        - jnp.mean(inner_grad, axis=-1, keepdims=True)
        - normed * jnp.mean(inner_grad * normed, axis=-1, keepdims=True)
    )
    return (grad_in, grad_gain, grad_shift)


def block_scores(query_block, key_rows, first_row, head_slope, row_docs):
    block_rows = query_block.shape[0]
    length = key_rows.shape[0]
    raw_scores = lax.dot_general(
        query_block, key_rows, (((1,), (1,)), ((), ())), preferred_element_type=jnp.float32
    )
    query_pos = first_row + jnp.arange(block_rows, dtype=jnp.int32)
    key_pos = jnp.arange(length, dtype=jnp.int32)
    offset = query_pos[:, None] - key_pos[None, :]
    query_doc = lax.dynamic_slice_in_dim(row_docs, first_row, block_rows)
    allowed = (offset >= 0) & (query_doc[:, None] == row_docs[None, :])
    scores = raw_scores * key_rows.shape[1] ** (-0.5) - head_slope * offset.astype(jnp.float32)
    return jnp.where(allowed, scores, masked_score)


def head_forward(query_rows, key_rows, value_rows, head_slope, row_docs, block_rows):
    starts = jnp.arange(query_rows.shape[0] // block_rows, dtype=jnp.int32) * block_rows

    def one_block(first_row):
        query_block = lax.dynamic_slice_in_dim(query_rows, first_row, block_rows)
        scores = block_scores(query_block, key_rows, first_row, head_slope, row_docs)
        row_max = jnp.max(scores, axis=-1, keepdims=True)
        exponent = jnp.exp(scores - row_max)
        row_total = jnp.sum(exponent, axis=-1, keepdims=True)
        weights = (exponent / row_total).astype(jnp.bfloat16)
        block_out = jnp.dot(weights, value_rows, preferred_element_type=jnp.float32).astype(
            jnp.bfloat16
        )
        return (block_out, (row_max + jnp.log(row_total))[:, 0])

    block_outs, log_total = lax.map(one_block, starts)
    return (block_outs.reshape(-1, value_rows.shape[1]), log_total.reshape(-1))


def head_backward(
    query_rows, key_rows, value_rows, grad_rows, log_total, head_slope, row_docs, block_rows
):
    length, head_width = key_rows.shape
    inv_root = head_width ** (-0.5)
    starts = jnp.arange(length // block_rows, dtype=jnp.int32) * block_rows

    def one_block(running, first_row):
        grad_keys, grad_values = running
        query_block = lax.dynamic_slice_in_dim(query_rows, first_row, block_rows)
        grad_block = lax.dynamic_slice_in_dim(grad_rows, first_row, block_rows)
        total_block = lax.dynamic_slice_in_dim(log_total, first_row, block_rows)
        scores = block_scores(query_block, key_rows, first_row, head_slope, row_docs)
        weights = jnp.exp(scores - total_block[:, None])
        grad_weights = lax.dot_general(
            grad_block, value_rows, (((1,), (1,)), ((), ())), preferred_element_type=jnp.float32
        )
        inner_sum = jnp.sum(weights * grad_weights, axis=-1, keepdims=True)
        grad_scores = (weights * (grad_weights - inner_sum)).astype(jnp.bfloat16)
        grad_query = jnp.dot(grad_scores, key_rows, preferred_element_type=jnp.float32) * inv_root
        grad_keys = (
            grad_keys
            + lax.dot_general(
                grad_scores,
                query_block,
                (((0,), (0,)), ((), ())),
                preferred_element_type=jnp.float32,
            )
            * inv_root
        )
        grad_values = grad_values + lax.dot_general(
            weights.astype(jnp.bfloat16),
            grad_block,
            (((0,), (0,)), ((), ())),
            preferred_element_type=jnp.float32,
        )
        return ((grad_keys, grad_values), grad_query)

    zeros_block = jnp.zeros((length, head_width), jnp.float32)
    (grad_keys, grad_values), grad_query = lax.scan(one_block, (zeros_block, zeros_block), starts)
    return (
        grad_query.reshape(length, head_width).astype(jnp.bfloat16),
        grad_keys.astype(jnp.bfloat16),
        grad_values.astype(jnp.bfloat16),
    )


def local(
    inputs,
    doc_ids,
    w_qkv,
    bias_q,
    bias_v,
    w_out,
    bias_out,
    norm1_gain,
    norm1_bias,
    norm2_gain,
    norm2_bias,
    w_up,
    bias_up,
    w_down,
    bias_down,
    cotangent,
):
    model_width = w_out.shape[0]
    tokens = inputs.shape[1]
    head_count = model_width // HEAD_DIM
    float_inputs = inputs[0].astype(jnp.float32)
    gain_one = norm1_gain.astype(jnp.float32)
    gain_two = norm2_gain.astype(jnp.float32)
    normed_in, normed_one, inv_one = layer_norm(
        float_inputs, gain_one, norm1_bias.astype(jnp.float32)
    )
    act_one = normed_in.astype(jnp.bfloat16)
    projected = jnp.dot(act_one, w_qkv, preferred_element_type=jnp.float32)
    query_rows = (projected[:, :model_width] + bias_q.astype(jnp.float32)).astype(jnp.bfloat16)
    key_rows = projected[:, model_width : 2 * model_width].astype(jnp.bfloat16)
    value_rows = (projected[:, 2 * model_width :] + bias_v.astype(jnp.float32)).astype(jnp.bfloat16)
    query_rows = query_rows.reshape(tokens, head_count, HEAD_DIM)
    key_rows = key_rows.reshape(tokens, head_count, HEAD_DIM)
    value_rows = value_rows.reshape(tokens, head_count, HEAD_DIM)
    whole_q, whole_k, whole_v = (
        lax.all_to_all(query_rows, "seq", split_axis=1, concat_axis=0, tiled=True),
        lax.all_to_all(key_rows, "seq", split_axis=1, concat_axis=0, tiled=True),
        lax.all_to_all(value_rows, "seq", split_axis=1, concat_axis=0, tiled=True),
    )
    row_docs = lax.all_gather(doc_ids, "seq", axis=1, tiled=True)[0]
    local_heads = whole_q.shape[1]
    length = whole_q.shape[0]
    block_rows = min(512, length)
    first_head = lax.axis_index("seq") * local_heads
    slopes = jnp.exp2(
        -(first_head + 1 + jnp.arange(local_heads, dtype=jnp.int32)).astype(jnp.float32)
    )
    head_q = jnp.moveaxis(whole_q, 1, 0)
    head_k = jnp.moveaxis(whole_k, 1, 0)
    head_v = jnp.moveaxis(whole_v, 1, 0)

    def forward_head(operands):
        return head_forward(
            operands[0], operands[1], operands[2], operands[3], row_docs, block_rows
        )

    head_outs, head_totals = lax.map(forward_head, (head_q, head_k, head_v, slopes))
    mixed_heads = lax.all_to_all(
        jnp.moveaxis(head_outs, 0, 1), "seq", split_axis=0, concat_axis=1, tiled=True
    )
    mixed_flat = mixed_heads.reshape(tokens, model_width)
    second = (
        float_inputs
        + jnp.dot(mixed_flat, w_out, preferred_element_type=jnp.float32)
        + bias_out.astype(jnp.float32)
    )
    normed_mid, normed_two, inv_two = layer_norm(second, gain_two, norm2_bias.astype(jnp.float32))
    act_two = normed_mid.astype(jnp.bfloat16)
    pre_act = jnp.dot(act_two, w_up, preferred_element_type=jnp.float32) + bias_up.astype(
        jnp.float32
    )
    activated, act_pullback = jax.vjp(smooth_act, pre_act)
    hidden = activated.astype(jnp.bfloat16)
    result = (
        second
        + jnp.dot(hidden, w_down, preferred_element_type=jnp.float32)
        + bias_down.astype(jnp.float32)
    )
    grad_out = cotangent[0].astype(jnp.float32)
    grad_low = grad_out.astype(jnp.bfloat16)
    g_bias_down = jnp.sum(grad_low.astype(jnp.float32), axis=0)
    g_w_down = lax.dot_general(
        hidden, grad_low, (((0,), (0,)), ((), ())), preferred_element_type=jnp.float32
    )
    grad_hidden = lax.dot_general(
        grad_low, w_down, (((1,), (1,)), ((), ())), preferred_element_type=jnp.float32
    )
    grad_pre = act_pullback(grad_hidden)[0].astype(jnp.bfloat16)
    g_bias_up = jnp.sum(grad_pre.astype(jnp.float32), axis=0)
    g_w_up = lax.dot_general(
        act_two, grad_pre, (((0,), (0,)), ((), ())), preferred_element_type=jnp.float32
    )
    grad_norm_two = lax.dot_general(
        grad_pre, w_up, (((1,), (1,)), ((), ())), preferred_element_type=jnp.float32
    )
    grad_mid, g_gain_two, g_shift_two = norm_back(grad_norm_two, normed_two, inv_two, gain_two)
    grad_second = grad_out + grad_mid
    grad_branch = grad_second.astype(jnp.bfloat16)
    g_bias_out = jnp.sum(grad_branch.astype(jnp.float32), axis=0)
    g_w_out = lax.dot_general(
        mixed_flat, grad_branch, (((0,), (0,)), ((), ())), preferred_element_type=jnp.float32
    )
    grad_mixed = lax.dot_general(
        grad_branch, w_out, (((1,), (1,)), ((), ())), preferred_element_type=jnp.float32
    ).astype(jnp.bfloat16)
    grad_whole = lax.all_to_all(
        grad_mixed.reshape(tokens, head_count, HEAD_DIM),
        "seq",
        split_axis=1,
        concat_axis=0,
        tiled=True,
    )
    grad_heads = jnp.moveaxis(grad_whole, 1, 0)

    def backward_head(operands):
        return head_backward(
            operands[0],
            operands[1],
            operands[2],
            operands[3],
            operands[4],
            operands[5],
            row_docs,
            block_rows,
        )

    grad_q, grad_k, grad_v = lax.map(
        backward_head, (head_q, head_k, head_v, grad_heads, head_totals, slopes)
    )
    back_q, back_k, back_v = (
        lax.all_to_all(jnp.moveaxis(grad_q, 0, 1), "seq", split_axis=0, concat_axis=1, tiled=True),
        lax.all_to_all(jnp.moveaxis(grad_k, 0, 1), "seq", split_axis=0, concat_axis=1, tiled=True),
        lax.all_to_all(jnp.moveaxis(grad_v, 0, 1), "seq", split_axis=0, concat_axis=1, tiled=True),
    )
    back_q = back_q.reshape(tokens, model_width)
    back_k = back_k.reshape(tokens, model_width)
    back_v = back_v.reshape(tokens, model_width)
    g_bias_q = jnp.sum(back_q.astype(jnp.float32), axis=0)
    g_bias_v = jnp.sum(back_v.astype(jnp.float32), axis=0)
    grad_proj = jnp.concatenate([back_q, back_k, back_v], axis=1)
    g_w_qkv = lax.dot_general(
        act_one, grad_proj, (((0,), (0,)), ((), ())), preferred_element_type=jnp.float32
    )
    grad_norm_one = lax.dot_general(
        grad_proj, w_qkv, (((1,), (1,)), ((), ())), preferred_element_type=jnp.float32
    )
    grad_first, g_gain_one, g_shift_one = norm_back(grad_norm_one, normed_one, inv_one, gain_one)
    grad_inputs = grad_second + grad_first
    matrices = (g_w_qkv, g_w_out, g_w_up, g_w_down)
    partial_sums = (
        lax.psum_scatter(
            matrices[0].astype(jnp.bfloat16), "dp", scatter_dimension=0, tiled=True
        ).astype(jnp.float32),
        lax.psum_scatter(
            matrices[1].astype(jnp.bfloat16), "dp", scatter_dimension=0, tiled=True
        ).astype(jnp.float32),
        lax.psum_scatter(
            matrices[2].astype(jnp.bfloat16), "dp", scatter_dimension=0, tiled=True
        ).astype(jnp.float32),
        lax.psum_scatter(
            matrices[3].astype(jnp.bfloat16), "dp", scatter_dimension=0, tiled=True
        ).astype(jnp.float32),
    )
    summed = (
        lax.psum_scatter(
            partial_sums[0].astype(jnp.bfloat16), "seq", scatter_dimension=1, tiled=True
        ).astype(jnp.float32),
        lax.psum_scatter(
            partial_sums[1].astype(jnp.bfloat16), "seq", scatter_dimension=1, tiled=True
        ).astype(jnp.float32),
        lax.psum_scatter(
            partial_sums[2].astype(jnp.bfloat16), "seq", scatter_dimension=1, tiled=True
        ).astype(jnp.float32),
        lax.psum_scatter(
            partial_sums[3].astype(jnp.bfloat16), "seq", scatter_dimension=1, tiled=True
        ).astype(jnp.float32),
    )
    vectors = lax.psum(
        (
            g_bias_q,
            g_bias_v,
            g_bias_out,
            g_gain_one,
            g_shift_one,
            g_gain_two,
            g_shift_two,
            g_bias_up,
            g_bias_down,
        ),
        ("dp", "seq"),
    )
    return (
        result.astype(jnp.bfloat16)[None],
        grad_inputs[None],
        summed[0],
        vectors[0],
        vectors[1],
        summed[1],
        vectors[2],
        vectors[3],
        vectors[4],
        vectors[5],
        vectors[6],
        summed[2],
        vectors[7],
        summed[3],
        vectors[8],
    )


def solution(mesh):
    in_specs = (
        P("dp", "seq", None),
        P("dp", "seq"),
        P(),
        P(),
        P(),
        P(),
        P(),
        P(),
        P(),
        P(),
        P(),
        P(),
        P(),
        P(),
        P(),
        P("dp", "seq", None),
    )
    out_specs = (
        P("dp", "seq", None),
        P("dp", "seq", None),
        P("dp", "seq"),
        P(),
        P(),
        P("dp", "seq"),
        P(),
        P(),
        P(),
        P(),
        P(),
        P("dp", "seq"),
        P(),
        P("dp", "seq"),
        P(),
    )
    sizes = (mesh.shape["dp"], mesh.shape["seq"])
    chosen = fast_local if sizes == (16, 2) else local
    return jax.shard_map(chosen, mesh=mesh, in_specs=in_specs, out_specs=out_specs, check_vma=False)
```

```python
import functools

import jax
import jax.numpy as jnp
import numpy as np
from jax import lax
from jax.experimental import pallas as pl
from jax.experimental.pallas import tpu as pltpu
from jax.sharding import PartitionSpec as P

HEAD_DIM = 128
MESH = pl.DeviceIdType.MESH
F32 = jnp.float32
BF16 = jnp.bfloat16
LOG2E = 1.4426950408889634
FAR = 1e30
GELU_C = 0.7978845608028654
GELU_A = 0.044715

norm_eps = 1e-05
masked_score = -1e30

NT = (((1,), (1,)), ((), ()))
TN = (((0,), (0,)), ((), ()))


def dot(a, b):
    return jnp.dot(a, b, preferred_element_type=F32)


def dot_nt(a, b):
    return lax.dot_general(a, b, NT, preferred_element_type=F32)


def dot_tn(a, b):
    return lax.dot_general(a, b, TN, preferred_element_type=F32)


def coords():
    dp = lax.axis_index("dp")
    return {
        "c": dp % 2,
        "x": (dp // 2) % 2,
        "a": (dp // 4) % 2,
        "b": dp // 8,
        "y": lax.axis_index("seq"),
    }


def partner(kind):
    dp = lax.axis_index("dp")
    if kind == "y":
        return {"seq": 1 - lax.axis_index("seq")}
    step = {"c": 1, "x": 2, "a": 4, "b": 8}[kind]
    bit = (dp // step) % 2
    return {"dp": dp + step - 2 * step * bit}


def greet(kinds):
    barrier = pltpu.get_barrier_semaphore()
    for kind in kinds:
        pl.semaphore_signal(barrier, inc=1, device_id=partner(kind), device_id_type=MESH)
    pl.semaphore_wait(barrier, len(kinds))


ORDERS = (("x", "a", "y", "b"), ("y", "a", "x", "b"))


ALONG_X = (18, 20, 22)


def order_of(chunk, half):
    return ORDERS[0 if isinstance(chunk, int) and chunk in ALONG_X else half]


def block_index(chunk, half, place):
    index = half * 16
    for kind, weight in zip(order_of(chunk, half), (8, 4, 2, 1)):
        index = index + place[kind] * weight
    return index


def dp_bits(dp):
    return {"c": dp % 2, "x": (dp // 2) % 2, "a": (dp // 4) % 2, "b": dp // 8}


class Scatter:
    def __init__(self, held, arrivals, send_sem, recv_sem):
        self.held, self.arrivals = held, arrivals
        self.send_sem, self.recv_sem = send_sem, recv_sem
        self.me = coords()

    def offset(self, chunk, half, stage, other):
        index = half * 16
        for k, weight in zip(range(stage + 1), (8, 4, 2, 1)):
            bit = self.me[order_of(chunk, half)[k]]
            if other and k == stage:
                bit = 1 - bit
            index = index + bit * weight
        return index

    def copy(self, chunk, stage, half):
        size = 8 >> stage
        return pltpu.make_async_remote_copy(
            src_ref=self.held.at[chunk, pl.ds(self.offset(chunk, half, stage, True), size)],
            dst_ref=self.arrivals[stage].at[chunk, half],
            send_sem=self.send_sem.at[stage, chunk, half],
            recv_sem=self.recv_sem.at[stage, chunk, half],
            device_id=partner(order_of(chunk, half)[stage]),
            device_id_type=MESH,
        )

    def start(self, chunk, stage):
        for half in range(2):
            self.copy(chunk, stage, half).start()

    def finish(self, chunk, stage):
        size = 8 >> stage
        for half in range(2):
            self.copy(chunk, stage, half).wait()
            mine = pl.ds(self.offset(chunk, half, stage, False), size)
            self.held[chunk, mine] = self.held[chunk, mine] + self.arrivals[stage][chunk, half]

    def result(self, chunk, half):
        return self.held[chunk, self.offset(chunk, half, 3, False)]


def arrival_shapes(chunks):
    return [pltpu.VMEM((chunks, 2, 8 >> k, 32, 256), BF16) for k in range(4)]


def when(cond, fn):
    if isinstance(cond, (bool, np.bool_)):
        if cond:
            fn()
    else:
        pl.when(cond)(fn)


def inside(value, low, high):
    if isinstance(value, int):
        return low <= value < high
    return (value >= low) & (value < high)


RING = 3
AHEAD = 2


def row_of(ref):
    return ref[...].astype(F32).reshape(1, -1)


def layer_kernel(
    halo, x_ref, doc_ref, slope_ref, bq_ref, bv_ref, bo_ref, g1_ref, s1_ref, g2_ref, s2_ref, bup_ref, bdown_ref,
    cot_hbm, wqkv_hbm, wout_hbm, wup_hbm, wdown_hbm,
    out_hbm, gin_hbm, gup, gdown, gout, gqkv, vec,
    qkv, act1t, ot, dist, doch, x2, cot, act2, act2t, hid_t, dpre, dn2, dn1, dnh, dqkv, wu, wd, bias, bup,
    grad, held, r1, r2, r3, r4, vin,
    qsem, osem, wsem, csem, cs, cr, ss, rs, hs, hr, vs, vr, esem,
):
    tokens, width = x_ref.shape
    heads = width // HEAD_DIM
    ff = wup_hbm.shape[1]
    half_ff = ff // 2
    steps = half_ff // 256
    seq = lax.axis_index("seq")
    me = coords()
    first_down, first_out, first_qkv, chunks = steps, 2 * steps, 2 * steps + 2, 2 * steps + 8
    scale = HEAD_DIM**-0.5

    act1 = dqkv.at[:, pl.ds(0, width)]
    o_s = dqkv.at[pl.ds(halo, tokens), pl.ds(width, width)]
    xh = dqkv.at[pl.ds(0, halo), pl.ds(2 * width, width)]
    wout_low = dqkv.at[pl.ds(halo, 512), pl.ds(2 * width, width)]

    dn_come = qkv.at[pl.ds(0, halo), pl.ds(0, width)]
    dn_send = qkv.at[pl.ds(0, halo), pl.ds(width, width)]

    def wqkv_part(j):
        return wu.at[j] if j < 2 else hid_t.at[pl.ds((j - 2) * width, width)]

    qloads = [
        pltpu.make_async_copy(wqkv_hbm.at[:, pl.ds(j * 512, 512)], wqkv_part(j), qsem.at[j]) for j in range(6)
    ]
    oloads = [
        pltpu.make_async_copy(wout_hbm.at[pl.ds(0, 512)], wout_low, osem.at[0]),
        pltpu.make_async_copy(wout_hbm.at[pl.ds(512, 512)], wd.at[1], osem.at[1]),
    ]
    cload = pltpu.make_async_copy(cot_hbm, cot, csem)
    for cp in qloads + oloads + [cload]:
        cp.start()
    greet(("c", "x", "a", "b", "y"))
    send_x = pltpu.make_async_remote_copy(
        src_ref=x_ref.at[pl.ds(tokens - halo, halo)], dst_ref=xh, send_sem=hs.at[0], recv_sem=hr.at[0],
        device_id=partner("y"), device_id_type=MESH,
    )
    send_doc = pltpu.make_async_remote_copy(
        src_ref=doc_ref, dst_ref=doch, send_sem=hs.at[1], recv_sem=hr.at[1],
        device_id=partner("y"), device_id_type=MESH,
    )

    @pl.when(seq == 0)
    def _():
        send_doc.start()
        send_x.start()

    def weights(f, slot):
        col = pl.multiple_of(f * 256, 256)
        return [
            pltpu.make_async_copy(wup_hbm.at[:, pl.ds(col, 256)], wu.at[slot, :, pl.ds(0, 256)], wsem.at[slot, 0]),
            pltpu.make_async_copy(
                wup_hbm.at[:, pl.ds(half_ff + col, 256)], wu.at[slot, :, pl.ds(256, 256)], wsem.at[slot, 1]
            ),
            pltpu.make_async_copy(wdown_hbm.at[pl.ds(col, 256)], wd.at[slot, pl.ds(0, 256)], wsem.at[slot, 2]),
            pltpu.make_async_copy(
                wdown_hbm.at[pl.ds(half_ff + col, 256)], wd.at[slot, pl.ds(256, 256)], wsem.at[slot, 3]
            ),
        ]

    scatter = Scatter(held, (r1, r2, r3, r4), ss, rs)

    def core_copy(n):
        return pltpu.make_async_remote_copy(
            src_ref=grad.at[n % RING, 1 - me["c"]], dst_ref=held.at[n], send_sem=cs.at[n % RING], recv_sem=cr.at[n],
            device_id=partner("c"), device_id_type=MESH,
        )

    def join(n):
        core_copy(n).wait()
        held[n] = held[n] + grad[n % RING, me["c"]]

    def put(n, yy, m, tile):
        for q in range(4):
            place = dp_bits(m * 4 + q)
            place["y"] = yy
            for h in range(2):
                r0 = q * 64 + h * 32
                grad[n % RING, place["c"], block_index(n, h, place)] = tile[r0 : r0 + 32].astype(BF16)

    def store(n):
        for h in range(2):
            block = scatter.result(n, h)

            def up():
                gup[h * 32 : h * 32 + 32, pl.ds(pl.multiple_of(n * 256, 256), 256)] = block

            def down():
                i = n - first_down
                row = pl.multiple_of((i % 4) * 64 + h * 32, 32)
                gdown[pl.ds(row, 32), pl.ds(pl.multiple_of((i // 4) * 256, 256), 256)] = block

            def outp():
                gout[h * 32 : h * 32 + 32, pl.ds(pl.multiple_of((n - first_out) * 256, 256), 256)] = block

            def proj():
                gqkv[h * 32 : h * 32 + 32, pl.ds(pl.multiple_of((n - first_qkv) * 256, 256), 256)] = block

            when(inside(n, 0, first_down), up)
            when(inside(n, first_down, first_out), down)
            when(inside(n, first_out, first_qkv), outp)
            when(inside(n, first_qkv, chunks), proj)

    def service(t, ahead=True):
        if ahead:
            when(inside(t + AHEAD, 0, chunks), lambda: scatter.start(t + AHEAD, 0))

        def last():
            scatter.finish(t - 6, 3)
            store(t - 6)

        when(inside(t - 6, 0, chunks), last)
        for stage in (2, 1, 0):
            n = t - 2 * stage

            def step(stage=stage, n=n):
                scatter.finish(n, stage)
                scatter.start(n, stage + 1)

            when(inside(n, 0, chunks), step)

    gain1, shift1 = row_of(g1_ref), row_of(s1_ref)
    gain2, shift2 = row_of(g2_ref), row_of(s2_ref)

    def norm(v, gain, shift):
        center = v - jnp.mean(v, axis=-1, keepdims=True)
        inv = lax.rsqrt(jnp.mean(center * center, axis=-1, keepdims=True) + norm_eps)
        return center * inv * gain + shift

    bias[:, 0:width] = row_of(bq_ref)
    bias[:, width : 2 * width] = jnp.zeros((1, width), F32)
    bias[:, 2 * width :] = row_of(bv_ref)
    bup[...] = row_of(bup_ref)

    for r in range(tokens // 128):
        v = norm(x_ref[r * 128 : (r + 1) * 128].astype(F32), gain1, shift1).astype(BF16)
        act1[halo + r * 128 : halo + (r + 1) * 128] = v
        act1t[:, halo + r * 128 : halo + (r + 1) * 128] = v.T

    for j in range(6):
        qloads[j].wait()
        cols = slice(j * 512, (j + 1) * 512)
        for m in range(tokens // 256):
            rows = slice(halo + m * 256, halo + (m + 1) * 256)
            qkv[rows, cols] = (dot(act1[rows], wqkv_part(j)[...]) + bias[:, cols]).astype(BF16)
    for cp in weights(0, 0):
        cp.start()

    own_doc = doc_ref[...].astype(F32)
    own_cols = jnp.transpose(jnp.broadcast_to(own_doc, (128, tokens)))[:, 0:1]

    def distances(block, key_docs):
        keys = key_docs[block * 256 : block * 256 + 512]
        queries = own_doc[:, block * 256 : block * 256 + 256]
        key_pos = lax.broadcasted_iota(jnp.int32, (512, 256), 0)
        query_pos = lax.broadcasted_iota(jnp.int32, (512, 256), 1) + 256
        gap = query_pos - key_pos
        allowed = (gap >= 0) & (keys == queries)
        dist[block] = jnp.where(allowed, gap.astype(F32), FAR)

    def attend(block):
        def some_heads(i, carry):
            for u in range(FWD_HEADS):
                h = i * FWD_HEADS + u
                c0 = pl.multiple_of(h * HEAD_DIM, HEAD_DIM)
                slope = slope_ref[pl.ds(h, 1), 0:1]
                for t in range(2):
                    row = block * 256 + t * 128
                    q = qkv[halo + row : halo + row + 128, pl.ds(c0, HEAD_DIM)]
                    k = qkv[row : row + 384, pl.ds(width + c0, HEAD_DIM)]
                    v = qkv[row : row + 384, pl.ds(2 * width + c0, HEAD_DIM)]
                    far = dist[block, t * 128 : t * 128 + 384, t * 128 : t * 128 + 128]
                    s = dot_nt(k, q) * (LOG2E * scale) - slope * far
                    e = jnp.exp2(s - jnp.max(s, axis=0, keepdims=True))
                    p = (e * (1.0 / jnp.sum(e, axis=0, keepdims=True))).astype(BF16)
                    o_t = dot_tn(v, p)
                    ot[pl.ds(c0, HEAD_DIM), row : row + 128] = o_t.astype(BF16)
                    o_s[row : row + 128, pl.ds(c0, HEAD_DIM)] = o_t.T.astype(BF16)
            return carry

        lax.fori_loop(0, heads // FWD_HEADS, some_heads, 0)

    def project(block):
        for r in range(2):
            rows = slice(block * 256 + r * 128, block * 256 + (r + 1) * 128)
            second = (
                x_ref[rows].astype(F32) + dot(o_s[rows, 0:512], wout_low[...]) + dot(o_s[rows, 512:1024], wd[1])
            ) + row_of(bo_ref)
            x2[rows] = second
            v = norm(second, gain2, shift2).astype(BF16)
            act2[rows] = v
            act2t[:, rows] = v.T

    distances(1, jnp.concatenate([jnp.full((halo, 1), -1.0, F32), own_cols], axis=0))
    attend(1)
    for cp in oloads:
        cp.wait()
    project(1)

    @pl.when(seq == 0)
    def _():
        send_doc.wait_send()
        send_x.wait_send()
        doch[...] = jnp.full(doch.shape, -1, jnp.int32)
        act1t[:, 0:halo] = jnp.zeros((width, halo), BF16)
        qkv[0:halo, width:] = jnp.zeros((halo, 2 * width), BF16)

    @pl.when(seq == 1)
    def _():
        send_doc.wait_recv()
        send_x.wait_recv()
        for r in range(halo // 128):
            v = norm(xh[r * 128 : (r + 1) * 128].astype(F32), gain1, shift1).astype(BF16)
            act1[r * 128 : (r + 1) * 128] = v
            act1t[:, r * 128 : (r + 1) * 128] = v.T
        for j in range(2, 6):
            cols = slice(j * 512, (j + 1) * 512)
            qkv[0:halo, cols] = (dot(act1[0:halo], wqkv_part(j)[...]) + bias[:, cols]).astype(BF16)

    halo_doc = doch[...].astype(F32)[:, tokens - halo :]
    halo_cols = jnp.transpose(jnp.broadcast_to(halo_doc, (128, halo)))[:, 0:1]
    distances(0, jnp.concatenate([halo_cols, own_cols], axis=0))
    attend(0)
    project(0)

    cload.wait()
    vec[...] = jnp.zeros(vec.shape, F32)
    vec[7:8] = jnp.sum(cot[...].astype(F32), axis=0, keepdims=True)
    dn2[...] = jnp.zeros(dn2.shape, F32)

    def ff_step(f, carry):
        slot = f % 2
        for cp in weights(f, slot):
            cp.wait()

        @pl.when(f + 1 < steps)
        def _():
            for cp in weights(f + 1, 1 - slot):
                cp.start()

        for yy in range(2):
            if yy == 1:

                @pl.when(f >= 1)
                def _():
                    join(f - 1)
                    scatter.start(f - 1, 0)

            cols = slice(yy * 256, (yy + 1) * 256)
            first = pl.multiple_of(yy * half_ff + f * 256, 256)
            shift = bup[:, pl.ds(first, 256)]
            sums = jnp.zeros((1, 256), F32)
            for m in range(tokens // 256):
                rows = slice(m * 256, (m + 1) * 256)
                u = dot(act2[rows], wu[slot, :, cols]) + shift
                dh = dot_nt(cot[rows], wd[slot, cols])
                uu = u * u
                gate = 0.5 * jnp.tanh(u * (GELU_C + GELU_C * GELU_A * uu)) + 0.5
                act = u * gate
                hv = act.astype(BF16)
                slope = gate + act * (1.0 - gate) * (2.0 * GELU_C + 6.0 * GELU_C * GELU_A * uu)
                dv = (dh * slope).astype(BF16)
                dpre[rows, cols] = dv
                hid_t[pl.ds(first, 256), rows] = hv.T
                sums = sums + jnp.sum(dv.astype(F32), axis=0, keepdims=True)
            row = yy * (half_ff // width) + f // (width // 256)
            vec[pl.ds(8 + row, 1), pl.ds(pl.multiple_of((f % (width // 256)) * 256, 256), 256)] = sums

        for yy in range(2):
            cols = slice(yy * 256, (yy + 1) * 256)
            for m in range(width // 256):
                put(f, yy, m, dot(act2t[m * 256 : (m + 1) * 256], dpre[:, cols]))
        core_copy(f).start()
        for m in range(tokens // 256):
            rows = slice(m * 256, (m + 1) * 256)
            dn2[rows] += dot_nt(dpre[rows], wu[slot])
        service(f - 2, ahead=False)
        return carry

    lax.fori_loop(0, steps, ff_step, 0)
    join(steps - 1)
    scatter.start(steps - 1, 0)
    oloads = [pltpu.make_async_copy(wout_hbm.at[pl.ds(i * 512, 512)], wd.at[i], osem.at[i]) for i in range(2)]
    order = (2, 3, 4, 5, 0, 1)

    def qload(i):
        return pltpu.make_async_copy(wqkv_hbm.at[:, pl.ds(order[i] * 512, 512)], wu.at[i % 2], qsem.at[i % 2])

    for cp in oloads + [qload(0), qload(1)]:
        cp.start()

    def down_step(i, carry):
        n = first_down + i
        for yy in range(2):
            right = cot[:, pl.ds(pl.multiple_of(yy * 512 + (i // 4) * 256, 256), 256)]
            for m in range(4):
                left = jnp.concatenate(
                    [
                        hid_t[pl.ds(pl.multiple_of((m * 4 + q) * 256 + (i % 4) * 64, 64), 64)]
                        for q in range(4)
                    ],
                    axis=0,
                )
                put(n, yy, m, dot(left, right))
        core_copy(n).start()

        @pl.when(i >= 1)
        def _():
            join(n - 1)

        for at, t in ((2, steps - 2), (5, steps - 1), (7, steps)):

            @pl.when(i == at)
            def _(t=t):
                service(t)

        return carry

    lax.fori_loop(0, steps, down_step, 0)
    join(first_out - 1)

    def norm_two(r, carry):
        rows = pl.ds(pl.multiple_of(r * 64, 64), 64)
        v = x2[rows]
        center = v - jnp.mean(v, axis=-1, keepdims=True)
        inv = lax.rsqrt(jnp.mean(center * center, axis=-1, keepdims=True) + norm_eps)
        normed = center * inv
        dn = dn2[rows]
        e = dn * gain2
        vec[5:6] += jnp.sum(dn * normed, axis=0, keepdims=True)
        vec[6:7] += jnp.sum(dn, axis=0, keepdims=True)
        dx = cot[rows].astype(F32) + inv * (
            e - jnp.mean(e, axis=-1, keepdims=True) - normed * jnp.mean(e * normed, axis=-1, keepdims=True)
        )
        dn2[rows] = dx
        low = dx.astype(BF16)
        cot[rows] = low
        vec[2:3] += jnp.sum(low.astype(F32), axis=0, keepdims=True)
        return carry

    lax.fori_loop(0, tokens // 64, norm_two, 0)
    dx2, ab, do = dn2, cot, act2
    service(steps + 1)

    for j in range(2):
        for yy in range(2):
            c0 = yy * 512 + j * 256
            for m in range(width // 256):
                put(first_out + j, yy, m, dot(ot[m * 256 : (m + 1) * 256], ab[:, c0 : c0 + 256]))
        core_copy(first_out + j).start()
    service(steps + 2)
    for cp in oloads:
        cp.wait()
    for m in range(tokens // 256):
        rows = slice(m * 256, (m + 1) * 256)
        for i in range(2):
            do[rows, i * 512 : (i + 1) * 512] = dot_nt(ab[rows], wd[i]).astype(BF16)

    def dload(i):
        return pltpu.make_async_copy(wdown_hbm.at[pl.ds(i * 512, 512)], wd.at[i % 2], osem.at[i % 2])

    dload(0).start()
    dload(1).start()
    join(first_out)
    join(first_out + 1)
    service(steps + 3)

    dqkv[0:halo, 0:width] = jnp.zeros((halo, width), BF16)
    act2t[...] = jnp.zeros(act2t.shape, BF16)

    def head_back(h):
        c0 = pl.multiple_of(h * HEAD_DIM, HEAD_DIM)
        slope = slope_ref[pl.ds(h, 1), 0:1]
        parts = []
        for block in range(2):
            rows = slice(halo + block * 256, halo + (block + 1) * 256)
            krows = slice(block * 256, block * 256 + 512)
            q = qkv[rows, pl.ds(c0, HEAD_DIM)]
            k = qkv[krows, pl.ds(width + c0, HEAD_DIM)]
            g = do[block * 256 : (block + 1) * 256, pl.ds(c0, HEAD_DIM)]
            for t in range(2):
                row = block * 256 + t * 128
                keys, cols = slice(t * 128, t * 128 + 384), slice(t * 128, t * 128 + 128)
                qs = qkv[halo + row : halo + row + 128, pl.ds(c0, HEAD_DIM)]
                ks = qkv[row : row + 384, pl.ds(width + c0, HEAD_DIM)]
                vs = qkv[row : row + 384, pl.ds(2 * width + c0, HEAD_DIM)]
                s = dot_nt(ks, qs) * (LOG2E * scale) - slope * dist[block, keys, cols]
                e = jnp.exp2(s - jnp.max(s, axis=0, keepdims=True))
                p = e * (1.0 / jnp.sum(e, axis=0, keepdims=True))
                dp = dot_nt(vs, do[row : row + 128, pl.ds(c0, HEAD_DIM)])
                delta = jnp.sum(p * dp, axis=0, keepdims=True)
                keys = slice(block * 512 + t * 128, block * 512 + t * 128 + 384)
                act2t[keys, cols] = p.astype(BF16)
                act2t[keys, 256 + t * 128 : 384 + t * 128] = (p * (dp - delta)).astype(BF16)
            both = slice(block * 512, (block + 1) * 512)
            pb, ds = act2t[both, 0:256], act2t[both, 256:512]
            dqkv[rows, pl.ds(c0, HEAD_DIM)] = (dot_tn(k, ds) * scale).T.astype(BF16)
            parts.append((dot(ds, q) * scale, dot(pb, g)))
        for which in range(2):
            cols = pl.ds((1 + which) * width + c0, HEAD_DIM)
            first, second = parts[0][which], parts[1][which]
            dqkv[0:256, cols] = first[0:256].astype(BF16)
            dqkv[256:512, cols] = (first[256:512] + second[0:256]).astype(BF16)
            dqkv[512:768, cols] = second[256:512].astype(BF16)

    def heads_back(i, carry):
        for u in range(2):
            head_back(i * 2 + u)
        service(steps + 4 + i)
        return carry

    lax.fori_loop(0, heads // 2, heads_back, 0)
    vec[0:1] = jnp.sum(dqkv[halo:, 0:width].astype(F32), axis=0, keepdims=True)
    vec[1:2] = jnp.sum(dqkv[:, 2 * width :].astype(F32), axis=0, keepdims=True)

    state = {"t": steps + 4 + heads // 2}

    def serve():
        if state["t"] < chunks + 6:
            service(state["t"])
            state["t"] += 1

    back = pltpu.make_async_remote_copy(
        src_ref=dn_send, dst_ref=dn_come, send_sem=hs.at[2], recv_sem=hr.at[2],
        device_id=partner("y"), device_id_type=MESH,
    )

    def dn_part(i):
        cols = slice(order[i] * 512, (order[i] + 1) * 512)
        qload(i).wait()
        if i < 4:
            part = dot_nt(dqkv[0:halo, cols], wu[i % 2])
            if i == 0:
                dnh[...] = part
            elif i < 3:
                dnh[...] += part
            else:
                dn_send[...] = (dnh[...] + part).astype(BF16)
        for m in range(tokens // 256):
            rows = slice(m * 256, (m + 1) * 256)
            part = dot_nt(dqkv[halo + m * 256 : halo + (m + 1) * 256, cols], wu[i % 2])
            if i == 0:
                dn1[rows] = part
            else:
                dn1[rows] += part
        if i + 2 < 6:
            qload(i + 2).start()

    for j in range(6):
        n = first_qkv + j
        for yy in range(2):
            c0 = yy * (3 * width // 2) + j * 256
            for m in range(width // 256):
                put(n, yy, m, dot(act1t[m * 256 : (m + 1) * 256], dqkv[:, c0 : c0 + 256]))
        core_copy(n).start()
        if j >= 1:
            join(n - 1)
        if j % 2 == 1:
            serve()
        if j == 3:
            for i in range(4):
                dn_part(i)

            @pl.when(seq == 1)
            def _():
                back.start()

            serve()
    join(chunks - 1)
    for i in (4, 5):
        dn_part(i)
    serve()

    def out_part(i):
        dload(i).wait()
        for m in range(tokens // 256):
            rows = slice(m * 256, (m + 1) * 256)
            part = dot_tn(hid_t[i * 512 : (i + 1) * 512, rows], wd[i % 2])
            if i == 0:
                part = part + row_of(bdown_ref)
            if i < 7:
                x2[rows] += part
            else:
                act2[rows] = (x2[rows] + part).astype(BF16)
        if i + 2 < 8:
            dload(i + 2).start()

    for i in range(3):
        out_part(i)
    serve()

    @pl.when(seq == 1)
    def _():
        back.wait_send()

    @pl.when(seq == 0)
    def _():
        back.wait_recv()
        dn1[tokens - halo :] += dn_come[...].astype(F32)

    def norm_one(r, carry):
        rows = pl.ds(pl.multiple_of(r * 64, 64), 64)
        v = x_ref[rows].astype(F32)
        center = v - jnp.mean(v, axis=-1, keepdims=True)
        inv = lax.rsqrt(jnp.mean(center * center, axis=-1, keepdims=True) + norm_eps)
        normed = center * inv
        dn = dn1[rows]
        e = dn * gain1
        vec[3:4] += jnp.sum(dn * normed, axis=0, keepdims=True)
        vec[4:5] += jnp.sum(dn, axis=0, keepdims=True)
        dn1[rows] = dx2[rows] + inv * (
            e - jnp.mean(e, axis=-1, keepdims=True) - normed * jnp.mean(e * normed, axis=-1, keepdims=True)
        )
        return carry

    lax.fori_loop(0, tokens // 64, norm_one, 0)
    save_gin = pltpu.make_async_copy(dn1, gin_hbm, esem.at[0])
    save_gin.start()

    kinds = ("c", "x", "y", "a", "b")

    def vec_copy(i):
        return pltpu.make_async_remote_copy(
            src_ref=vin.at[i, 0], dst_ref=vin.at[i, 1], send_sem=vs.at[i], recv_sem=vr.at[i],
            device_id=partner(kinds[i]), device_id_type=MESH,
        )

    vin[0, 0] = vec[...]
    vec_copy(0).start()
    save_out = pltpu.make_async_copy(act2, out_hbm, esem.at[1])
    for i in range(5):
        serve()
        if i == 0:
            out_part(3)
            out_part(4)
            out_part(5)
        if i == 1:
            out_part(6)
            out_part(7)
            save_out.start()
        vec_copy(i).wait()
        total = vin[i, 0] + vin[i, 1]
        if i < 4:
            vin[i + 1, 0] = total
            vec_copy(i + 1).start()
        else:
            vec[...] = total
    while state["t"] < chunks + 6:
        serve()
    save_gin.wait()
    save_out.wait()


def finish_kernel(out_in, gin_in, gup, gdown, gout, gqkv, vec, *refs):
    out, gin, o_qkv, bq, bv, o_out, bo, g1, s1, g2, s2, o_up, b_up, o_down, b_down = refs
    out[...] = out_in[...]
    gin[...] = gin_in[...]
    o_qkv[...] = gqkv[...].astype(F32)
    o_out[...] = gout[...].astype(F32)
    o_up[...] = gup[...].astype(F32)
    o_down[...] = gdown[...].astype(F32)
    width = vec.shape[1]
    for i, ref in enumerate((bq, bv, bo, g1, s1, g2, s2, b_down)):
        ref[...] = vec[i]
    for i in range(b_up.shape[0] // width):
        b_up[i * width : (i + 1) * width] = vec[8 + i]


FWD_HEADS = 2


def vmem():
    return pl.BlockSpec(memory_space=pltpu.VMEM)


def hbm():
    return pl.BlockSpec(memory_space=pl.ANY)


def shape(dims, dtype):
    return jax.ShapeDtypeStruct(dims, dtype)


DMA = pltpu.SemaphoreType.DMA


def params(cid):
    return pltpu.CompilerParams(collective_id=cid, has_side_effects=True, vmem_limit_bytes=64 * 2**20 - 2**16)


def fast_local(
    inputs, doc_ids, w_qkv, bias_q, bias_v, w_out, bias_out, norm1_gain, norm1_bias, norm2_gain, norm2_bias,
    w_up, bias_up, w_down, bias_down, cotangent,
):
    x = inputs[0]
    tokens, width = x.shape
    ff = w_up.shape[1]
    halo = 256
    ext = tokens + halo
    heads = width // HEAD_DIM
    steps = ff // 512
    chunks = 2 * steps + 8
    slopes = jnp.asarray(
        np.broadcast_to((2.0 ** -(np.arange(heads) + 1.0) * LOG2E)[:, None], (heads, 128)).astype(np.float32)
    )
    shards = (
        (width // 16, ff // 2), (ff // 16, width // 2), (width // 16, width // 2), (width // 16, 3 * width // 2),
    )
    out, gin, g_up, g_down, g_out, g_qkv, vec = pl.pallas_call(
        functools.partial(layer_kernel, halo),
        out_shape=(shape((tokens, width), BF16), shape((tokens, width), F32))
        + tuple(shape(dims, BF16) for dims in shards)
        + (shape((16, width), F32),),
        in_specs=[vmem()] * 12 + [hbm()] * 5,
        out_specs=(hbm(),) * 2 + (vmem(),) * 5,
        scratch_shapes=[
            pltpu.VMEM((ext, 3 * width), BF16),
            pltpu.VMEM((width, ext), BF16),
            pltpu.VMEM((width, tokens), BF16),
            pltpu.VMEM((2, 512, 256), F32),
            pltpu.VMEM((1, tokens), jnp.int32),
            pltpu.VMEM((tokens, width), F32),
            pltpu.VMEM((tokens, width), BF16),
            pltpu.VMEM((tokens, width), BF16),
            pltpu.VMEM((width, tokens), BF16),
            pltpu.VMEM((ff, tokens), BF16),
            pltpu.VMEM((tokens, 512), BF16),
            pltpu.VMEM((tokens, width), F32),
            pltpu.VMEM((tokens, width), F32),
            pltpu.VMEM((halo, width), F32),
            pltpu.VMEM((ext, 3 * width), BF16),
            pltpu.VMEM((2, width, 512), BF16),
            pltpu.VMEM((2, 512, width), BF16),
            pltpu.VMEM((1, 3 * width), F32),
            pltpu.VMEM((1, ff), F32),
            pltpu.VMEM((RING, 2, 32, 32, 256), BF16),
            pltpu.VMEM((chunks, 32, 32, 256), BF16),
        ]
        + arrival_shapes(chunks)
        + [
            pltpu.VMEM((5, 2, 16, width), F32),
            DMA((6,)), DMA((2,)), DMA((2, 4)), DMA, DMA((RING,)), DMA((chunks,)), DMA((4, chunks, 2)),
            DMA((4, chunks, 2)), DMA((3,)), DMA((3,)), DMA((5,)), DMA((5,)), DMA((2,)),
        ],
        compiler_params=params(0),
        name="layer",
    )(
        x, doc_ids, slopes, bias_q, bias_v, bias_out, norm1_gain, norm1_bias, norm2_gain, norm2_bias, bias_up, bias_down,
        cotangent[0], w_qkv, w_out, w_up, w_down,
    )
    row = shape((width,), F32)
    return_shapes = (
        shape((tokens, width), BF16), shape((tokens, width), F32), shape(shards[3], F32), row, row, shape(shards[2], F32),
        row, row, row, row, row, shape(shards[0], F32), shape((ff,), F32), shape(shards[1], F32), row,
    )
    results = pl.pallas_call(
        finish_kernel,
        out_shape=return_shapes,
        in_specs=[vmem()] * 7,
        out_specs=(vmem(),) * 15,
        name="hand_over",
    )(out, gin, g_up, g_down, g_out, g_qkv, vec)
    return (results[0][None], results[1][None]) + tuple(results[2:])


def smooth_act(values):
    return jax.nn.gelu(values, approximate=True)


def layer_norm(values, norm_gain, norm_shift):
    center = values - jnp.mean(values, axis=-1, keepdims=True)
    inv_std = lax.rsqrt(jnp.mean(center * center, axis=-1, keepdims=True) + norm_eps)
    normed = center * inv_std
    return (normed * norm_gain + norm_shift, normed, inv_std)


def norm_back(grad_out, normed, inv_std, norm_gain):
    grad_gain = jnp.sum(grad_out * normed, axis=0)
    grad_shift = jnp.sum(grad_out, axis=0)
    inner_grad = grad_out * norm_gain
    grad_in = inv_std * (
        inner_grad
        - jnp.mean(inner_grad, axis=-1, keepdims=True)
        - normed * jnp.mean(inner_grad * normed, axis=-1, keepdims=True)
    )
    return (grad_in, grad_gain, grad_shift)


def block_scores(query_block, key_rows, first_row, head_slope, row_docs):
    block_rows = query_block.shape[0]
    length = key_rows.shape[0]
    raw_scores = lax.dot_general(
        query_block, key_rows, (((1,), (1,)), ((), ())), preferred_element_type=jnp.float32
    )
    query_pos = first_row + jnp.arange(block_rows, dtype=jnp.int32)
    key_pos = jnp.arange(length, dtype=jnp.int32)
    offset = query_pos[:, None] - key_pos[None, :]
    query_doc = lax.dynamic_slice_in_dim(row_docs, first_row, block_rows)
    allowed = (offset >= 0) & (query_doc[:, None] == row_docs[None, :])
    scores = raw_scores * key_rows.shape[1] ** (-0.5) - head_slope * offset.astype(jnp.float32)
    return jnp.where(allowed, scores, masked_score)


def head_forward(query_rows, key_rows, value_rows, head_slope, row_docs, block_rows):
    starts = jnp.arange(query_rows.shape[0] // block_rows, dtype=jnp.int32) * block_rows

    def one_block(first_row):
        query_block = lax.dynamic_slice_in_dim(query_rows, first_row, block_rows)
        scores = block_scores(query_block, key_rows, first_row, head_slope, row_docs)
        row_max = jnp.max(scores, axis=-1, keepdims=True)
        exponent = jnp.exp(scores - row_max)
        row_total = jnp.sum(exponent, axis=-1, keepdims=True)
        weights = (exponent / row_total).astype(jnp.bfloat16)
        block_out = jnp.dot(weights, value_rows, preferred_element_type=jnp.float32).astype(
            jnp.bfloat16
        )
        return (block_out, (row_max + jnp.log(row_total))[:, 0])

    block_outs, log_total = lax.map(one_block, starts)
    return (block_outs.reshape(-1, value_rows.shape[1]), log_total.reshape(-1))


def head_backward(
    query_rows, key_rows, value_rows, grad_rows, log_total, head_slope, row_docs, block_rows
):
    length, head_width = key_rows.shape
    inv_root = head_width ** (-0.5)
    starts = jnp.arange(length // block_rows, dtype=jnp.int32) * block_rows

    def one_block(running, first_row):
        grad_keys, grad_values = running
        query_block = lax.dynamic_slice_in_dim(query_rows, first_row, block_rows)
        grad_block = lax.dynamic_slice_in_dim(grad_rows, first_row, block_rows)
        total_block = lax.dynamic_slice_in_dim(log_total, first_row, block_rows)
        scores = block_scores(query_block, key_rows, first_row, head_slope, row_docs)
        weights = jnp.exp(scores - total_block[:, None])
        grad_weights = lax.dot_general(
            grad_block, value_rows, (((1,), (1,)), ((), ())), preferred_element_type=jnp.float32
        )
        inner_sum = jnp.sum(weights * grad_weights, axis=-1, keepdims=True)
        grad_scores = (weights * (grad_weights - inner_sum)).astype(jnp.bfloat16)
        grad_query = jnp.dot(grad_scores, key_rows, preferred_element_type=jnp.float32) * inv_root
        grad_keys = (
            grad_keys
            + lax.dot_general(
                grad_scores,
                query_block,
                (((0,), (0,)), ((), ())),
                preferred_element_type=jnp.float32,
            )
            * inv_root
        )
        grad_values = grad_values + lax.dot_general(
            weights.astype(jnp.bfloat16),
            grad_block,
            (((0,), (0,)), ((), ())),
            preferred_element_type=jnp.float32,
        )
        return ((grad_keys, grad_values), grad_query)

    zeros_block = jnp.zeros((length, head_width), jnp.float32)
    (grad_keys, grad_values), grad_query = lax.scan(one_block, (zeros_block, zeros_block), starts)
    return (
        grad_query.reshape(length, head_width).astype(jnp.bfloat16),
        grad_keys.astype(jnp.bfloat16),
        grad_values.astype(jnp.bfloat16),
    )


def local(
    inputs,
    doc_ids,
    w_qkv,
    bias_q,
    bias_v,
    w_out,
    bias_out,
    norm1_gain,
    norm1_bias,
    norm2_gain,
    norm2_bias,
    w_up,
    bias_up,
    w_down,
    bias_down,
    cotangent,
):
    model_width = w_out.shape[0]
    tokens = inputs.shape[1]
    head_count = model_width // HEAD_DIM
    float_inputs = inputs[0].astype(jnp.float32)
    gain_one = norm1_gain.astype(jnp.float32)
    gain_two = norm2_gain.astype(jnp.float32)
    normed_in, normed_one, inv_one = layer_norm(
        float_inputs, gain_one, norm1_bias.astype(jnp.float32)
    )
    act_one = normed_in.astype(jnp.bfloat16)
    projected = jnp.dot(act_one, w_qkv, preferred_element_type=jnp.float32)
    query_rows = (projected[:, :model_width] + bias_q.astype(jnp.float32)).astype(jnp.bfloat16)
    key_rows = projected[:, model_width : 2 * model_width].astype(jnp.bfloat16)
    value_rows = (projected[:, 2 * model_width :] + bias_v.astype(jnp.float32)).astype(jnp.bfloat16)
    query_rows = query_rows.reshape(tokens, head_count, HEAD_DIM)
    key_rows = key_rows.reshape(tokens, head_count, HEAD_DIM)
    value_rows = value_rows.reshape(tokens, head_count, HEAD_DIM)
    whole_q, whole_k, whole_v = (
        lax.all_to_all(query_rows, "seq", split_axis=1, concat_axis=0, tiled=True),
        lax.all_to_all(key_rows, "seq", split_axis=1, concat_axis=0, tiled=True),
        lax.all_to_all(value_rows, "seq", split_axis=1, concat_axis=0, tiled=True),
    )
    row_docs = lax.all_gather(doc_ids, "seq", axis=1, tiled=True)[0]
    local_heads = whole_q.shape[1]
    length = whole_q.shape[0]
    block_rows = min(512, length)
    first_head = lax.axis_index("seq") * local_heads
    slopes = jnp.exp2(
        -(first_head + 1 + jnp.arange(local_heads, dtype=jnp.int32)).astype(jnp.float32)
    )
    head_q = jnp.moveaxis(whole_q, 1, 0)
    head_k = jnp.moveaxis(whole_k, 1, 0)
    head_v = jnp.moveaxis(whole_v, 1, 0)

    def forward_head(operands):
        return head_forward(
            operands[0], operands[1], operands[2], operands[3], row_docs, block_rows
        )

    head_outs, head_totals = lax.map(forward_head, (head_q, head_k, head_v, slopes))
    mixed_heads = lax.all_to_all(
        jnp.moveaxis(head_outs, 0, 1), "seq", split_axis=0, concat_axis=1, tiled=True
    )
    mixed_flat = mixed_heads.reshape(tokens, model_width)
    second = (
        float_inputs
        + jnp.dot(mixed_flat, w_out, preferred_element_type=jnp.float32)
        + bias_out.astype(jnp.float32)
    )
    normed_mid, normed_two, inv_two = layer_norm(second, gain_two, norm2_bias.astype(jnp.float32))
    act_two = normed_mid.astype(jnp.bfloat16)
    pre_act = jnp.dot(act_two, w_up, preferred_element_type=jnp.float32) + bias_up.astype(
        jnp.float32
    )
    activated, act_pullback = jax.vjp(smooth_act, pre_act)
    hidden = activated.astype(jnp.bfloat16)
    result = (
        second
        + jnp.dot(hidden, w_down, preferred_element_type=jnp.float32)
        + bias_down.astype(jnp.float32)
    )
    grad_out = cotangent[0].astype(jnp.float32)
    grad_low = grad_out.astype(jnp.bfloat16)
    g_bias_down = jnp.sum(grad_low.astype(jnp.float32), axis=0)
    g_w_down = lax.dot_general(
        hidden, grad_low, (((0,), (0,)), ((), ())), preferred_element_type=jnp.float32
    )
    grad_hidden = lax.dot_general(
        grad_low, w_down, (((1,), (1,)), ((), ())), preferred_element_type=jnp.float32
    )
    grad_pre = act_pullback(grad_hidden)[0].astype(jnp.bfloat16)
    g_bias_up = jnp.sum(grad_pre.astype(jnp.float32), axis=0)
    g_w_up = lax.dot_general(
        act_two, grad_pre, (((0,), (0,)), ((), ())), preferred_element_type=jnp.float32
    )
    grad_norm_two = lax.dot_general(
        grad_pre, w_up, (((1,), (1,)), ((), ())), preferred_element_type=jnp.float32
    )
    grad_mid, g_gain_two, g_shift_two = norm_back(grad_norm_two, normed_two, inv_two, gain_two)
    grad_second = grad_out + grad_mid
    grad_branch = grad_second.astype(jnp.bfloat16)
    g_bias_out = jnp.sum(grad_branch.astype(jnp.float32), axis=0)
    g_w_out = lax.dot_general(
        mixed_flat, grad_branch, (((0,), (0,)), ((), ())), preferred_element_type=jnp.float32
    )
    grad_mixed = lax.dot_general(
        grad_branch, w_out, (((1,), (1,)), ((), ())), preferred_element_type=jnp.float32
    ).astype(jnp.bfloat16)
    grad_whole = lax.all_to_all(
        grad_mixed.reshape(tokens, head_count, HEAD_DIM),
        "seq",
        split_axis=1,
        concat_axis=0,
        tiled=True,
    )
    grad_heads = jnp.moveaxis(grad_whole, 1, 0)

    def backward_head(operands):
        return head_backward(
            operands[0],
            operands[1],
            operands[2],
            operands[3],
            operands[4],
            operands[5],
            row_docs,
            block_rows,
        )

    grad_q, grad_k, grad_v = lax.map(
        backward_head, (head_q, head_k, head_v, grad_heads, head_totals, slopes)
    )
    back_q, back_k, back_v = (
        lax.all_to_all(jnp.moveaxis(grad_q, 0, 1), "seq", split_axis=0, concat_axis=1, tiled=True),
        lax.all_to_all(jnp.moveaxis(grad_k, 0, 1), "seq", split_axis=0, concat_axis=1, tiled=True),
        lax.all_to_all(jnp.moveaxis(grad_v, 0, 1), "seq", split_axis=0, concat_axis=1, tiled=True),
    )
    back_q = back_q.reshape(tokens, model_width)
    back_k = back_k.reshape(tokens, model_width)
    back_v = back_v.reshape(tokens, model_width)
    g_bias_q = jnp.sum(back_q.astype(jnp.float32), axis=0)
    g_bias_v = jnp.sum(back_v.astype(jnp.float32), axis=0)
    grad_proj = jnp.concatenate([back_q, back_k, back_v], axis=1)
    g_w_qkv = lax.dot_general(
        act_one, grad_proj, (((0,), (0,)), ((), ())), preferred_element_type=jnp.float32
    )
    grad_norm_one = lax.dot_general(
        grad_proj, w_qkv, (((1,), (1,)), ((), ())), preferred_element_type=jnp.float32
    )
    grad_first, g_gain_one, g_shift_one = norm_back(grad_norm_one, normed_one, inv_one, gain_one)
    grad_inputs = grad_second + grad_first
    matrices = (g_w_qkv, g_w_out, g_w_up, g_w_down)
    partial_sums = (
        lax.psum_scatter(
            matrices[0].astype(jnp.bfloat16), "dp", scatter_dimension=0, tiled=True
        ).astype(jnp.float32),
        lax.psum_scatter(
            matrices[1].astype(jnp.bfloat16), "dp", scatter_dimension=0, tiled=True
        ).astype(jnp.float32),
        lax.psum_scatter(
            matrices[2].astype(jnp.bfloat16), "dp", scatter_dimension=0, tiled=True
        ).astype(jnp.float32),
        lax.psum_scatter(
            matrices[3].astype(jnp.bfloat16), "dp", scatter_dimension=0, tiled=True
        ).astype(jnp.float32),
    )
    summed = (
        lax.psum_scatter(
            partial_sums[0].astype(jnp.bfloat16), "seq", scatter_dimension=1, tiled=True
        ).astype(jnp.float32),
        lax.psum_scatter(
            partial_sums[1].astype(jnp.bfloat16), "seq", scatter_dimension=1, tiled=True
        ).astype(jnp.float32),
        lax.psum_scatter(
            partial_sums[2].astype(jnp.bfloat16), "seq", scatter_dimension=1, tiled=True
        ).astype(jnp.float32),
        lax.psum_scatter(
            partial_sums[3].astype(jnp.bfloat16), "seq", scatter_dimension=1, tiled=True
        ).astype(jnp.float32),
    )
    vectors = lax.psum(
        (
            g_bias_q,
            g_bias_v,
            g_bias_out,
            g_gain_one,
            g_shift_one,
            g_gain_two,
            g_shift_two,
            g_bias_up,
            g_bias_down,
        ),
        ("dp", "seq"),
    )
    return (
        result.astype(jnp.bfloat16)[None],
        grad_inputs[None],
        summed[0],
        vectors[0],
        vectors[1],
        summed[1],
        vectors[2],
        vectors[3],
        vectors[4],
        vectors[5],
        vectors[6],
        summed[2],
        vectors[7],
        summed[3],
        vectors[8],
    )


def solution(mesh):
    in_specs = (
        P("dp", "seq", None),
        P("dp", "seq"),
        P(),
        P(),
        P(),
        P(),
        P(),
        P(),
        P(),
        P(),
        P(),
        P(),
        P(),
        P(),
        P(),
        P("dp", "seq", None),
    )
    out_specs = (
        P("dp", "seq", None),
        P("dp", "seq", None),
        P("dp", "seq"),
        P(),
        P(),
        P("dp", "seq"),
        P(),
        P(),
        P(),
        P(),
        P(),
        P("dp", "seq"),
        P(),
        P("dp", "seq"),
        P(),
    )
    sizes = (mesh.shape["dp"], mesh.shape["seq"])
    chosen = fast_local if sizes == (16, 2) else local
    return jax.shard_map(chosen, mesh=mesh, in_specs=in_specs, out_specs=out_specs, check_vma=False)
```

```python
import functools

import jax
import jax.numpy as jnp
import numpy as np
from jax import lax
from jax.experimental import pallas as pl
from jax.experimental.pallas import tpu as pltpu
from jax.sharding import PartitionSpec as P

HEAD_DIM = 128
MESH = pl.DeviceIdType.MESH
F32 = jnp.float32
BF16 = jnp.bfloat16
LOG2E = 1.4426950408889634
FAR = 1e30
GELU_C = 0.7978845608028654
GELU_A = 0.044715

norm_eps = 1e-05
masked_score = -1e30

NT = (((1,), (1,)), ((), ()))
TN = (((0,), (0,)), ((), ()))


def dot(a, b):
    return jnp.dot(a, b, preferred_element_type=F32)


def dot_nt(a, b):
    return lax.dot_general(a, b, NT, preferred_element_type=F32)


def dot_tn(a, b):
    return lax.dot_general(a, b, TN, preferred_element_type=F32)


def coords():
    dp = lax.axis_index("dp")
    return {
        "c": dp % 2,
        "x": (dp // 2) % 2,
        "a": (dp // 4) % 2,
        "b": dp // 8,
        "y": lax.axis_index("seq"),
    }


def partner(kind):
    dp = lax.axis_index("dp")
    if kind == "y":
        return {"seq": 1 - lax.axis_index("seq")}
    step = {"c": 1, "x": 2, "a": 4, "b": 8}[kind]
    bit = (dp // step) % 2
    return {"dp": dp + step - 2 * step * bit}


def greet(kinds):
    barrier = pltpu.get_barrier_semaphore()
    for kind in kinds:
        pl.semaphore_signal(barrier, inc=1, device_id=partner(kind), device_id_type=MESH)
    pl.semaphore_wait(barrier, len(kinds))


ORDERS = (("x", "a", "y", "b"), ("y", "a", "x", "b"))


ALONG_X = (18, 20, 22)


def order_of(chunk, half):
    return ORDERS[0 if isinstance(chunk, int) and chunk in ALONG_X else half]


def block_index(chunk, half, place):
    index = half * 16
    for kind, weight in zip(order_of(chunk, half), (8, 4, 2, 1)):
        index = index + place[kind] * weight
    return index


def dp_bits(dp):
    return {"c": dp % 2, "x": (dp // 2) % 2, "a": (dp // 4) % 2, "b": dp // 8}


class Scatter:
    def __init__(self, held, arrivals, send_sem, recv_sem):
        self.held, self.arrivals = held, arrivals
        self.send_sem, self.recv_sem = send_sem, recv_sem
        self.me = coords()

    def offset(self, chunk, half, stage, other):
        index = half * 16
        for k, weight in zip(range(stage + 1), (8, 4, 2, 1)):
            bit = self.me[order_of(chunk, half)[k]]
            if other and k == stage:
                bit = 1 - bit
            index = index + bit * weight
        return index

    def copy(self, chunk, stage, half):
        size = 8 >> stage
        return pltpu.make_async_remote_copy(
            src_ref=self.held.at[chunk, pl.ds(self.offset(chunk, half, stage, True), size)],
            dst_ref=self.arrivals[stage].at[chunk, half],
            send_sem=self.send_sem.at[stage],
            recv_sem=self.recv_sem.at[stage, chunk],
            device_id=partner(order_of(chunk, half)[stage]),
            device_id_type=MESH,
        )

    def start(self, chunk, stage):
        for half in range(2):
            self.copy(chunk, stage, half).start()

    def whole(self, stage, ref, at):
        return pltpu.make_async_remote_copy(
            src_ref=ref, dst_ref=ref, send_sem=self.send_sem.at[stage], recv_sem=self.recv_sem.at[stage, at],
            device_id=partner("x"), device_id_type=MESH,
        )

    def sent(self):
        for stage in range(4):
            self.whole(stage, self.arrivals[stage], 0).wait_send()

    def finish(self, chunk, stage):
        size = 8 >> stage
        self.whole(stage, self.arrivals[stage].at[chunk], chunk).wait_recv()
        for half in range(2):
            mine = pl.ds(self.offset(chunk, half, stage, False), size)
            self.held[chunk, mine] = self.held[chunk, mine] + self.arrivals[stage][chunk, half]

    def result(self, chunk, half):
        return self.held[chunk, self.offset(chunk, half, 3, False)]


def arrival_shapes(chunks):
    return [pltpu.VMEM((chunks, 2, 8 >> k, 32, 256), BF16) for k in range(4)]


def when(cond, fn):
    if isinstance(cond, (bool, np.bool_)):
        if cond:
            fn()
    else:
        pl.when(cond)(fn)


def inside(value, low, high):
    if isinstance(value, int):
        return low <= value < high
    return (value >= low) & (value < high)


RING = 3
AHEAD = 2


def row_of(ref):
    return ref[...].astype(F32).reshape(1, -1)


def layer_kernel(
    halo, x_ref, doc_ref, slope_ref, bq_ref, bv_ref, bo_ref, g1_ref, s1_ref, g2_ref, s2_ref, bup_ref, bdown_ref,
    cot_hbm, wqkv_hbm, wout_hbm, wup_hbm, wdown_hbm,
    out_hbm, gin_hbm, gup, gdown, gout, gqkv, vec,
    qkv, act1t, ot, dist, doch, x2, cot, act2, act2t, hid_t, dpre, dn2, dn1, dnh, dqkv, wu, wd, bias, bup,
    grad, held, r1, r2, r3, r4, vin,
    qsem, osem, wsem, csem, cs, cr, ss, rs, hs, hr, vs, vr, esem,
):
    tokens, width = x_ref.shape
    heads = width // HEAD_DIM
    ff = wup_hbm.shape[1]
    half_ff = ff // 2
    steps = half_ff // 256
    seq = lax.axis_index("seq")
    me = coords()
    first_down, first_out, first_qkv, chunks = steps, 2 * steps, 2 * steps + 2, 2 * steps + 8
    scale = HEAD_DIM**-0.5

    act1 = dqkv.at[:, pl.ds(0, width)]
    o_s = dqkv.at[pl.ds(halo, tokens), pl.ds(width, width)]
    xh = dqkv.at[pl.ds(0, halo), pl.ds(2 * width, width)]
    wout_low = dqkv.at[pl.ds(halo, 512), pl.ds(2 * width, width)]

    dn_come = qkv.at[pl.ds(0, halo), pl.ds(0, width)]
    dn_send = qkv.at[pl.ds(0, halo), pl.ds(width, width)]

    def wqkv_part(j):
        return wu.at[j] if j < 2 else hid_t.at[pl.ds((j - 2) * width, width)]

    qloads = [
        pltpu.make_async_copy(wqkv_hbm.at[:, pl.ds(j * 512, 512)], wqkv_part(j), qsem.at[j]) for j in range(6)
    ]
    oloads = [
        pltpu.make_async_copy(wout_hbm.at[pl.ds(0, 512)], wout_low, osem.at[0]),
        pltpu.make_async_copy(wout_hbm.at[pl.ds(512, 512)], wd.at[1], osem.at[1]),
    ]
    cload = pltpu.make_async_copy(cot_hbm, cot, csem)
    for cp in qloads + oloads + [cload]:
        cp.start()
    greet(("c", "x", "a", "b", "y"))
    send_x = pltpu.make_async_remote_copy(
        src_ref=x_ref.at[pl.ds(tokens - halo, halo)], dst_ref=xh, send_sem=hs.at[0], recv_sem=hr.at[0],
        device_id=partner("y"), device_id_type=MESH,
    )
    send_doc = pltpu.make_async_remote_copy(
        src_ref=doc_ref, dst_ref=doch, send_sem=hs.at[1], recv_sem=hr.at[1],
        device_id=partner("y"), device_id_type=MESH,
    )

    @pl.when(seq == 0)
    def _():
        send_doc.start()
        send_x.start()

    def weights(f, slot):
        col = pl.multiple_of(f * 256, 256)
        return [
            pltpu.make_async_copy(wup_hbm.at[:, pl.ds(col, 256)], wu.at[slot, :, pl.ds(0, 256)], wsem.at[slot, 0]),
            pltpu.make_async_copy(
                wup_hbm.at[:, pl.ds(half_ff + col, 256)], wu.at[slot, :, pl.ds(256, 256)], wsem.at[slot, 1]
            ),
            pltpu.make_async_copy(wdown_hbm.at[pl.ds(col, 256)], wd.at[slot, pl.ds(0, 256)], wsem.at[slot, 2]),
            pltpu.make_async_copy(
                wdown_hbm.at[pl.ds(half_ff + col, 256)], wd.at[slot, pl.ds(256, 256)], wsem.at[slot, 3]
            ),
        ]

    scatter = Scatter(held, (r1, r2, r3, r4), ss, rs)

    def core_copy(n):
        return pltpu.make_async_remote_copy(
            src_ref=grad.at[n % RING, 1 - me["c"]], dst_ref=held.at[n], send_sem=cs.at[n % RING], recv_sem=cr.at[n],
            device_id=partner("c"), device_id_type=MESH,
        )

    def join(n):
        core_copy(n).wait()
        held[n] = held[n] + grad[n % RING, me["c"]]

    def put(n, yy, m, tile):
        for q in range(4):
            place = dp_bits(m * 4 + q)
            place["y"] = yy
            for h in range(2):
                r0 = q * 64 + h * 32
                grad[n % RING, place["c"], block_index(n, h, place)] = tile[r0 : r0 + 32].astype(BF16)

    def store(n):
        for h in range(2):
            block = scatter.result(n, h)

            def up():
                gup[h * 32 : h * 32 + 32, pl.ds(pl.multiple_of(n * 256, 256), 256)] = block

            def down():
                i = n - first_down
                row = pl.multiple_of((i % 4) * 64 + h * 32, 32)
                gdown[pl.ds(row, 32), pl.ds(pl.multiple_of((i // 4) * 256, 256), 256)] = block

            def outp():
                gout[h * 32 : h * 32 + 32, pl.ds(pl.multiple_of((n - first_out) * 256, 256), 256)] = block

            def proj():
                gqkv[h * 32 : h * 32 + 32, pl.ds(pl.multiple_of((n - first_qkv) * 256, 256), 256)] = block

            when(inside(n, 0, first_down), up)
            when(inside(n, first_down, first_out), down)
            when(inside(n, first_out, first_qkv), outp)
            when(inside(n, first_qkv, chunks), proj)

    def service(t, ahead=True):
        if ahead:
            when(inside(t + AHEAD, 0, chunks), lambda: scatter.start(t + AHEAD, 0))

        def last():
            scatter.finish(t - 6, 3)
            store(t - 6)

        when(inside(t - 6, 0, chunks), last)
        for stage in (2, 1, 0):
            n = t - 2 * stage

            def step(stage=stage, n=n):
                scatter.finish(n, stage)
                scatter.start(n, stage + 1)

            when(inside(n, 0, chunks), step)

    gain1, shift1 = row_of(g1_ref), row_of(s1_ref)
    gain2, shift2 = row_of(g2_ref), row_of(s2_ref)

    def norm(v, gain, shift):
        center = v - jnp.mean(v, axis=-1, keepdims=True)
        inv = lax.rsqrt(jnp.mean(center * center, axis=-1, keepdims=True) + norm_eps)
        return center * inv * gain + shift

    bias[:, 0:width] = row_of(bq_ref)
    bias[:, width : 2 * width] = jnp.zeros((1, width), F32)
    bias[:, 2 * width :] = row_of(bv_ref)
    bup[...] = row_of(bup_ref)

    def norm_rows(m):
        for r in range(2 * m, 2 * m + 2):
            v = norm(x_ref[r * 128 : (r + 1) * 128].astype(F32), gain1, shift1).astype(BF16)
            act1[halo + r * 128 : halo + (r + 1) * 128] = v
            act1t[:, halo + r * 128 : halo + (r + 1) * 128] = v.T

    norm_rows(0)
    for cp in qloads:
        cp.wait()
    for m in range(tokens // 256):
        rows = slice(halo + m * 256, halo + (m + 1) * 256)
        for j in range(6):
            cols = slice(j * 512, (j + 1) * 512)
            qkv[rows, cols] = (dot(act1[rows], wqkv_part(j)[...]) + bias[:, cols]).astype(BF16)
            if m == 0 and j == 0:
                norm_rows(1)
    for cp in weights(0, 0):
        cp.start()

    own_doc = doc_ref[...].astype(F32)
    own_cols = jnp.transpose(jnp.broadcast_to(own_doc, (128, tokens)))[:, 0:1]

    def distances(block, key_docs):
        keys = key_docs[block * 256 : block * 256 + 512]
        queries = own_doc[:, block * 256 : block * 256 + 256]
        key_pos = lax.broadcasted_iota(jnp.int32, (512, 256), 0)
        query_pos = lax.broadcasted_iota(jnp.int32, (512, 256), 1) + 256
        gap = query_pos - key_pos
        allowed = (gap >= 0) & (keys == queries)
        dist[block] = jnp.where(allowed, gap.astype(F32), FAR)

    def attend(block):
        def some_heads(i, carry):
            for u in range(FWD_HEADS):
                h = i * FWD_HEADS + u
                c0 = pl.multiple_of(h * HEAD_DIM, HEAD_DIM)
                slope = slope_ref[pl.ds(h, 1), 0:1]
                for t in range(2):
                    row = block * 256 + t * 128
                    q = qkv[halo + row : halo + row + 128, pl.ds(c0, HEAD_DIM)]
                    k = qkv[row : row + 384, pl.ds(width + c0, HEAD_DIM)]
                    v = qkv[row : row + 384, pl.ds(2 * width + c0, HEAD_DIM)]
                    far = dist[block, t * 128 : t * 128 + 384, t * 128 : t * 128 + 128]
                    s = dot_nt(k, q) * (LOG2E * scale) - slope * far
                    e = jnp.exp2(s - jnp.max(s, axis=0, keepdims=True))
                    p = (e * (1.0 / jnp.sum(e, axis=0, keepdims=True))).astype(BF16)
                    o_t = dot_tn(v, p)
                    ot[pl.ds(c0, HEAD_DIM), row : row + 128] = o_t.astype(BF16)
                    o_s[row : row + 128, pl.ds(c0, HEAD_DIM)] = o_t.T.astype(BF16)
            return carry

        lax.fori_loop(0, heads // FWD_HEADS, some_heads, 0)

    def project(block):
        for r in range(2):
            rows = slice(block * 256 + r * 128, block * 256 + (r + 1) * 128)
            second = (
                x_ref[rows].astype(F32) + dot(o_s[rows, 0:512], wout_low[...]) + dot(o_s[rows, 512:1024], wd[1])
            ) + row_of(bo_ref)
            x2[rows] = second
            v = norm(second, gain2, shift2).astype(BF16)
            act2[rows] = v
            act2t[:, rows] = v.T

    distances(1, jnp.concatenate([jnp.full((halo, 1), -1.0, F32), own_cols], axis=0))
    attend(1)
    for cp in oloads:
        cp.wait()
    project(1)

    @pl.when(seq == 0)
    def _():
        send_doc.wait_send()
        send_x.wait_send()
        doch[...] = jnp.full(doch.shape, -1, jnp.int32)
        act1t[:, 0:halo] = jnp.zeros((width, halo), BF16)
        qkv[0:halo, width:] = jnp.zeros((halo, 2 * width), BF16)

    @pl.when(seq == 1)
    def _():
        send_doc.wait_recv()
        send_x.wait_recv()
        for r in range(halo // 128):
            v = norm(xh[r * 128 : (r + 1) * 128].astype(F32), gain1, shift1).astype(BF16)
            act1[r * 128 : (r + 1) * 128] = v
            act1t[:, r * 128 : (r + 1) * 128] = v.T
        for j in range(2, 6):
            cols = slice(j * 512, (j + 1) * 512)
            qkv[0:halo, cols] = (dot(act1[0:halo], wqkv_part(j)[...]) + bias[:, cols]).astype(BF16)

    halo_doc = doch[...].astype(F32)[:, tokens - halo :]
    halo_cols = jnp.transpose(jnp.broadcast_to(halo_doc, (128, halo)))[:, 0:1]
    distances(0, jnp.concatenate([halo_cols, own_cols], axis=0))
    attend(0)
    project(0)

    cload.wait()
    vec[...] = jnp.zeros(vec.shape, F32)
    vec[7:8] = jnp.sum(cot[...].astype(F32), axis=0, keepdims=True)
    dn2[...] = jnp.zeros(dn2.shape, F32)

    def ff_step(f, carry):
        slot = f % 2
        for cp in weights(f, slot):
            cp.wait()

        @pl.when(f + 1 < steps)
        def _():
            for cp in weights(f + 1, 1 - slot):
                cp.start()

        for yy in range(2):
            if yy == 1:

                @pl.when(f >= 1)
                def _():
                    join(f - 1)
                    scatter.start(f - 1, 0)

            cols = slice(yy * 256, (yy + 1) * 256)
            first = pl.multiple_of(yy * half_ff + f * 256, 256)
            shift = bup[:, pl.ds(first, 256)]
            sums = jnp.zeros((1, 256), F32)
            for m in range(tokens // 256):
                rows = slice(m * 256, (m + 1) * 256)
                u = dot(act2[rows], wu[slot, :, cols]) + shift
                dh = dot_nt(cot[rows], wd[slot, cols])
                uu = u * u
                gate = 0.5 * jnp.tanh(u * (GELU_C + GELU_C * GELU_A * uu)) + 0.5
                act = u * gate
                hv = act.astype(BF16)
                slope = gate + act * (1.0 - gate) * (2.0 * GELU_C + 6.0 * GELU_C * GELU_A * uu)
                dv = (dh * slope).astype(BF16)
                dpre[rows, cols] = dv
                hid_t[pl.ds(first, 256), rows] = hv.T
                sums = sums + jnp.sum(dv.astype(F32), axis=0, keepdims=True)
            row = yy * (half_ff // width) + f // (width // 256)
            vec[pl.ds(8 + row, 1), pl.ds(pl.multiple_of((f % (width // 256)) * 256, 256), 256)] = sums

        for yy in range(2):
            cols = slice(yy * 256, (yy + 1) * 256)
            for m in range(width // 256):
                put(f, yy, m, dot(act2t[m * 256 : (m + 1) * 256], dpre[:, cols]))
        core_copy(f).start()
        for m in range(tokens // 256):
            rows = slice(m * 256, (m + 1) * 256)
            dn2[rows] += dot_nt(dpre[rows], wu[slot])
        service(f - 2, ahead=False)
        return carry

    lax.fori_loop(0, steps, ff_step, 0)
    join(steps - 1)
    scatter.start(steps - 1, 0)
    oloads = [pltpu.make_async_copy(wout_hbm.at[pl.ds(i * 512, 512)], wd.at[i], osem.at[i]) for i in range(2)]
    order = (2, 3, 4, 5, 0, 1)

    def qload(i):
        return pltpu.make_async_copy(wqkv_hbm.at[:, pl.ds(order[i] * 512, 512)], wu.at[i % 2], qsem.at[i % 2])

    for cp in oloads + [qload(0), qload(1)]:
        cp.start()

    def down_step(i, carry):
        n = first_down + i
        for yy in range(2):
            right = cot[:, pl.ds(pl.multiple_of(yy * 512 + (i // 4) * 256, 256), 256)]
            for m in range(4):
                left = jnp.concatenate(
                    [
                        hid_t[pl.ds(pl.multiple_of((m * 4 + q) * 256 + (i % 4) * 64, 64), 64)]
                        for q in range(4)
                    ],
                    axis=0,
                )
                put(n, yy, m, dot(left, right))
        core_copy(n).start()

        @pl.when(i >= 1)
        def _():
            join(n - 1)

        for at, t in ((2, steps - 2), (5, steps - 1), (7, steps)):

            @pl.when(i == at)
            def _(t=t):
                service(t)

        return carry

    lax.fori_loop(0, steps, down_step, 0)
    join(first_out - 1)

    def norm_two(r, carry):
        rows = pl.ds(pl.multiple_of(r * 64, 64), 64)
        v = x2[rows]
        center = v - jnp.mean(v, axis=-1, keepdims=True)
        inv = lax.rsqrt(jnp.mean(center * center, axis=-1, keepdims=True) + norm_eps)
        normed = center * inv
        dn = dn2[rows]
        e = dn * gain2
        vec[5:6] += jnp.sum(dn * normed, axis=0, keepdims=True)
        vec[6:7] += jnp.sum(dn, axis=0, keepdims=True)
        dx = cot[rows].astype(F32) + inv * (
            e - jnp.mean(e, axis=-1, keepdims=True) - normed * jnp.mean(e * normed, axis=-1, keepdims=True)
        )
        dn2[rows] = dx
        low = dx.astype(BF16)
        cot[rows] = low
        vec[2:3] += jnp.sum(low.astype(F32), axis=0, keepdims=True)
        return carry

    lax.fori_loop(0, tokens // 64, norm_two, 0)
    dx2, ab, do = dn2, cot, act2
    service(steps + 1)

    for j in range(2):
        for yy in range(2):
            c0 = yy * 512 + j * 256
            for m in range(width // 256):
                put(first_out + j, yy, m, dot(ot[m * 256 : (m + 1) * 256], ab[:, c0 : c0 + 256]))
        core_copy(first_out + j).start()
    service(steps + 2)
    for cp in oloads:
        cp.wait()
    for m in range(tokens // 256):
        rows = slice(m * 256, (m + 1) * 256)
        for i in range(2):
            do[rows, i * 512 : (i + 1) * 512] = dot_nt(ab[rows], wd[i]).astype(BF16)

    def dload(i):
        return pltpu.make_async_copy(wdown_hbm.at[pl.ds(i * 512, 512)], wd.at[i % 2], osem.at[i % 2])

    dload(0).start()
    dload(1).start()
    join(first_out)
    join(first_out + 1)
    service(steps + 3)

    dqkv[0:halo, 0:width] = jnp.zeros((halo, width), BF16)
    act2t[...] = jnp.zeros(act2t.shape, BF16)

    def head_back(h):
        c0 = pl.multiple_of(h * HEAD_DIM, HEAD_DIM)
        slope = slope_ref[pl.ds(h, 1), 0:1]
        parts = []
        for block in range(2):
            rows = slice(halo + block * 256, halo + (block + 1) * 256)
            krows = slice(block * 256, block * 256 + 512)
            q = qkv[rows, pl.ds(c0, HEAD_DIM)]
            k = qkv[krows, pl.ds(width + c0, HEAD_DIM)]
            g = do[block * 256 : (block + 1) * 256, pl.ds(c0, HEAD_DIM)]
            for t in range(2):
                row = block * 256 + t * 128
                keys, cols = slice(t * 128, t * 128 + 384), slice(t * 128, t * 128 + 128)
                qs = qkv[halo + row : halo + row + 128, pl.ds(c0, HEAD_DIM)]
                ks = qkv[row : row + 384, pl.ds(width + c0, HEAD_DIM)]
                vs = qkv[row : row + 384, pl.ds(2 * width + c0, HEAD_DIM)]
                s = dot_nt(ks, qs) * (LOG2E * scale) - slope * dist[block, keys, cols]
                e = jnp.exp2(s - jnp.max(s, axis=0, keepdims=True))
                p = e * (1.0 / jnp.sum(e, axis=0, keepdims=True))
                dp = dot_nt(vs, do[row : row + 128, pl.ds(c0, HEAD_DIM)])
                delta = jnp.sum(p * dp, axis=0, keepdims=True)
                keys = slice(block * 512 + t * 128, block * 512 + t * 128 + 384)
                act2t[keys, cols] = p.astype(BF16)
                act2t[keys, 256 + t * 128 : 384 + t * 128] = (p * (dp - delta)).astype(BF16)
            both = slice(block * 512, (block + 1) * 512)
            pb, ds = act2t[both, 0:256], act2t[both, 256:512]
            dqkv[rows, pl.ds(c0, HEAD_DIM)] = (dot_tn(k, ds) * scale).T.astype(BF16)
            parts.append((dot(ds, q) * scale, dot(pb, g)))
        for which in range(2):
            cols = pl.ds((1 + which) * width + c0, HEAD_DIM)
            first, second = parts[0][which], parts[1][which]
            dqkv[0:256, cols] = first[0:256].astype(BF16)
            dqkv[256:512, cols] = (first[256:512] + second[0:256]).astype(BF16)
            dqkv[512:768, cols] = second[256:512].astype(BF16)

    def heads_back(i, carry):
        for u in range(2):
            head_back(i * 2 + u)
        service(steps + 4 + i)
        return carry

    lax.fori_loop(0, heads // 2, heads_back, 0)
    vec[0:1] = jnp.sum(dqkv[halo:, 0:width].astype(F32), axis=0, keepdims=True)
    vec[1:2] = jnp.sum(dqkv[:, 2 * width :].astype(F32), axis=0, keepdims=True)

    state = {"t": steps + 4 + heads // 2}

    def serve():
        if state["t"] < chunks + 6:
            service(state["t"])
            state["t"] += 1

    back = pltpu.make_async_remote_copy(
        src_ref=dn_send, dst_ref=dn_come, send_sem=hs.at[2], recv_sem=hr.at[2],
        device_id=partner("y"), device_id_type=MESH,
    )

    def dn_part(i):
        cols = slice(order[i] * 512, (order[i] + 1) * 512)
        qload(i).wait()
        if i < 4:
            part = dot_nt(dqkv[0:halo, cols], wu[i % 2])
            if i == 0:
                dnh[...] = part
            elif i < 3:
                dnh[...] += part
            else:
                dn_send[...] = (dnh[...] + part).astype(BF16)
        for m in range(tokens // 256):
            rows = slice(m * 256, (m + 1) * 256)
            part = dot_nt(dqkv[halo + m * 256 : halo + (m + 1) * 256, cols], wu[i % 2])
            if i == 0:
                dn1[rows] = part
            else:
                dn1[rows] += part
        if i + 2 < 6:
            qload(i + 2).start()

    for j in range(6):
        n = first_qkv + j
        for yy in range(2):
            c0 = yy * (3 * width // 2) + j * 256
            for m in range(width // 256):
                put(n, yy, m, dot(act1t[m * 256 : (m + 1) * 256], dqkv[:, c0 : c0 + 256]))
        core_copy(n).start()
        if j >= 1:
            join(n - 1)
        if j % 2 == 1:
            serve()
        if j == 3:
            for i in range(4):
                dn_part(i)

            @pl.when(seq == 1)
            def _():
                back.start()

            serve()
    join(chunks - 1)
    for i in (4, 5):
        dn_part(i)
    serve()

    def out_part(i):
        dload(i).wait()
        for m in range(tokens // 256):
            rows = slice(m * 256, (m + 1) * 256)
            part = dot_tn(hid_t[i * 512 : (i + 1) * 512, rows], wd[i % 2])
            if i == 0:
                part = part + row_of(bdown_ref)
            if i < 7:
                x2[rows] += part
            else:
                act2[rows] = (x2[rows] + part).astype(BF16)
        if i + 2 < 8:
            dload(i + 2).start()

    for i in range(3):
        out_part(i)
    serve()

    @pl.when(seq == 1)
    def _():
        back.wait_send()

    @pl.when(seq == 0)
    def _():
        back.wait_recv()
        dn1[tokens - halo :] += dn_come[...].astype(F32)

    def norm_one(r, carry):
        rows = pl.ds(pl.multiple_of(r * 64, 64), 64)
        v = x_ref[rows].astype(F32)
        center = v - jnp.mean(v, axis=-1, keepdims=True)
        inv = lax.rsqrt(jnp.mean(center * center, axis=-1, keepdims=True) + norm_eps)
        normed = center * inv
        dn = dn1[rows]
        e = dn * gain1
        vec[3:4] += jnp.sum(dn * normed, axis=0, keepdims=True)
        vec[4:5] += jnp.sum(dn, axis=0, keepdims=True)
        dn1[rows] = dx2[rows] + inv * (
            e - jnp.mean(e, axis=-1, keepdims=True) - normed * jnp.mean(e * normed, axis=-1, keepdims=True)
        )
        return carry

    lax.fori_loop(0, tokens // 64, norm_one, 0)
    save_gin = pltpu.make_async_copy(dn1, gin_hbm, esem.at[0])
    save_gin.start()

    kinds = ("c", "x", "y", "a", "b")

    def vec_copy(i):
        return pltpu.make_async_remote_copy(
            src_ref=vin.at[i, 0], dst_ref=vin.at[i, 1], send_sem=vs.at[i], recv_sem=vr.at[i],
            device_id=partner(kinds[i]), device_id_type=MESH,
        )

    vin[0, 0] = vec[...]
    vec_copy(0).start()
    save_out = pltpu.make_async_copy(act2, out_hbm, esem.at[1])
    for i in range(5):
        serve()
        if i == 0:
            out_part(3)
            out_part(4)
            out_part(5)
        if i == 1:
            out_part(6)
            out_part(7)
            save_out.start()
        vec_copy(i).wait()
        total = vin[i, 0] + vin[i, 1]
        if i < 4:
            vin[i + 1, 0] = total
            vec_copy(i + 1).start()
        else:
            vec[...] = total
    while state["t"] < chunks + 6:
        serve()
    scatter.sent()
    save_gin.wait()
    save_out.wait()


def finish_kernel(out_in, gin_in, gup, gdown, gout, gqkv, vec, *refs):
    out, gin, o_qkv, bq, bv, o_out, bo, g1, s1, g2, s2, o_up, b_up, o_down, b_down = refs
    out[...] = out_in[...]
    gin[...] = gin_in[...]
    o_qkv[...] = gqkv[...].astype(F32)
    o_out[...] = gout[...].astype(F32)
    o_up[...] = gup[...].astype(F32)
    o_down[...] = gdown[...].astype(F32)
    width = vec.shape[1]
    for i, ref in enumerate((bq, bv, bo, g1, s1, g2, s2, b_down)):
        ref[...] = vec[i]
    for i in range(b_up.shape[0] // width):
        b_up[i * width : (i + 1) * width] = vec[8 + i]


FWD_HEADS = 4


def vmem():
    return pl.BlockSpec(memory_space=pltpu.VMEM)


def hbm():
    return pl.BlockSpec(memory_space=pl.ANY)


def shape(dims, dtype):
    return jax.ShapeDtypeStruct(dims, dtype)


DMA = pltpu.SemaphoreType.DMA


def params(cid):
    return pltpu.CompilerParams(collective_id=cid, has_side_effects=True, vmem_limit_bytes=64 * 2**20 - 2**16)


def fast_local(
    inputs, doc_ids, w_qkv, bias_q, bias_v, w_out, bias_out, norm1_gain, norm1_bias, norm2_gain, norm2_bias,
    w_up, bias_up, w_down, bias_down, cotangent,
):
    x = inputs[0]
    tokens, width = x.shape
    ff = w_up.shape[1]
    halo = 256
    ext = tokens + halo
    heads = width // HEAD_DIM
    steps = ff // 512
    chunks = 2 * steps + 8
    slopes = jnp.asarray(
        np.broadcast_to((2.0 ** -(np.arange(heads) + 1.0) * LOG2E)[:, None], (heads, 128)).astype(np.float32)
    )
    shards = (
        (width // 16, ff // 2), (ff // 16, width // 2), (width // 16, width // 2), (width // 16, 3 * width // 2),
    )
    out, gin, g_up, g_down, g_out, g_qkv, vec = pl.pallas_call(
        functools.partial(layer_kernel, halo),
        out_shape=(shape((tokens, width), BF16), shape((tokens, width), F32))
        + tuple(shape(dims, BF16) for dims in shards)
        + (shape((16, width), F32),),
        in_specs=[vmem()] * 12 + [hbm()] * 5,
        out_specs=(hbm(),) * 2 + (vmem(),) * 5,
        scratch_shapes=[
            pltpu.VMEM((ext, 3 * width), BF16),
            pltpu.VMEM((width, ext), BF16),
            pltpu.VMEM((width, tokens), BF16),
            pltpu.VMEM((2, 512, 256), F32),
            pltpu.VMEM((1, tokens), jnp.int32),
            pltpu.VMEM((tokens, width), F32),
            pltpu.VMEM((tokens, width), BF16),
            pltpu.VMEM((tokens, width), BF16),
            pltpu.VMEM((width, tokens), BF16),
            pltpu.VMEM((ff, tokens), BF16),
            pltpu.VMEM((tokens, 512), BF16),
            pltpu.VMEM((tokens, width), F32),
            pltpu.VMEM((tokens, width), F32),
            pltpu.VMEM((halo, width), F32),
            pltpu.VMEM((ext, 3 * width), BF16),
            pltpu.VMEM((2, width, 512), BF16),
            pltpu.VMEM((2, 512, width), BF16),
            pltpu.VMEM((1, 3 * width), F32),
            pltpu.VMEM((1, ff), F32),
            pltpu.VMEM((RING, 2, 32, 32, 256), BF16),
            pltpu.VMEM((chunks, 32, 32, 256), BF16),
        ]
        + arrival_shapes(chunks)
        + [
            pltpu.VMEM((5, 2, 16, width), F32),
            DMA((6,)), DMA((2,)), DMA((2, 4)), DMA, DMA((RING,)), DMA((chunks,)), DMA((4,)),
            DMA((4, chunks)), DMA((3,)), DMA((3,)), DMA((5,)), DMA((5,)), DMA((2,)),
        ],
        compiler_params=params(0),
        name="layer",
    )(
        x, doc_ids, slopes, bias_q, bias_v, bias_out, norm1_gain, norm1_bias, norm2_gain, norm2_bias, bias_up, bias_down,
        cotangent[0], w_qkv, w_out, w_up, w_down,
    )
    row = shape((width,), F32)
    return_shapes = (
        shape((tokens, width), BF16), shape((tokens, width), F32), shape(shards[3], F32), row, row, shape(shards[2], F32),
        row, row, row, row, row, shape(shards[0], F32), shape((ff,), F32), shape(shards[1], F32), row,
    )
    results = pl.pallas_call(
        finish_kernel,
        out_shape=return_shapes,
        in_specs=[vmem()] * 7,
        out_specs=(vmem(),) * 15,
        name="hand_over",
    )(out, gin, g_up, g_down, g_out, g_qkv, vec)
    return (results[0][None], results[1][None]) + tuple(results[2:])


def smooth_act(values):
    return jax.nn.gelu(values, approximate=True)


def layer_norm(values, norm_gain, norm_shift):
    center = values - jnp.mean(values, axis=-1, keepdims=True)
    inv_std = lax.rsqrt(jnp.mean(center * center, axis=-1, keepdims=True) + norm_eps)
    normed = center * inv_std
    return (normed * norm_gain + norm_shift, normed, inv_std)


def norm_back(grad_out, normed, inv_std, norm_gain):
    grad_gain = jnp.sum(grad_out * normed, axis=0)
    grad_shift = jnp.sum(grad_out, axis=0)
    inner_grad = grad_out * norm_gain
    grad_in = inv_std * (
        inner_grad
        - jnp.mean(inner_grad, axis=-1, keepdims=True)
        - normed * jnp.mean(inner_grad * normed, axis=-1, keepdims=True)
    )
    return (grad_in, grad_gain, grad_shift)


def block_scores(query_block, key_rows, first_row, head_slope, row_docs):
    block_rows = query_block.shape[0]
    length = key_rows.shape[0]
    raw_scores = lax.dot_general(
        query_block, key_rows, (((1,), (1,)), ((), ())), preferred_element_type=jnp.float32
    )
    query_pos = first_row + jnp.arange(block_rows, dtype=jnp.int32)
    key_pos = jnp.arange(length, dtype=jnp.int32)
    offset = query_pos[:, None] - key_pos[None, :]
    query_doc = lax.dynamic_slice_in_dim(row_docs, first_row, block_rows)
    allowed = (offset >= 0) & (query_doc[:, None] == row_docs[None, :])
    scores = raw_scores * key_rows.shape[1] ** (-0.5) - head_slope * offset.astype(jnp.float32)
    return jnp.where(allowed, scores, masked_score)


def head_forward(query_rows, key_rows, value_rows, head_slope, row_docs, block_rows):
    starts = jnp.arange(query_rows.shape[0] // block_rows, dtype=jnp.int32) * block_rows

    def one_block(first_row):
        query_block = lax.dynamic_slice_in_dim(query_rows, first_row, block_rows)
        scores = block_scores(query_block, key_rows, first_row, head_slope, row_docs)
        row_max = jnp.max(scores, axis=-1, keepdims=True)
        exponent = jnp.exp(scores - row_max)
        row_total = jnp.sum(exponent, axis=-1, keepdims=True)
        weights = (exponent / row_total).astype(jnp.bfloat16)
        block_out = jnp.dot(weights, value_rows, preferred_element_type=jnp.float32).astype(
            jnp.bfloat16
        )
        return (block_out, (row_max + jnp.log(row_total))[:, 0])

    block_outs, log_total = lax.map(one_block, starts)
    return (block_outs.reshape(-1, value_rows.shape[1]), log_total.reshape(-1))


def head_backward(
    query_rows, key_rows, value_rows, grad_rows, log_total, head_slope, row_docs, block_rows
):
    length, head_width = key_rows.shape
    inv_root = head_width ** (-0.5)
    starts = jnp.arange(length // block_rows, dtype=jnp.int32) * block_rows

    def one_block(running, first_row):
        grad_keys, grad_values = running
        query_block = lax.dynamic_slice_in_dim(query_rows, first_row, block_rows)
        grad_block = lax.dynamic_slice_in_dim(grad_rows, first_row, block_rows)
        total_block = lax.dynamic_slice_in_dim(log_total, first_row, block_rows)
        scores = block_scores(query_block, key_rows, first_row, head_slope, row_docs)
        weights = jnp.exp(scores - total_block[:, None])
        grad_weights = lax.dot_general(
            grad_block, value_rows, (((1,), (1,)), ((), ())), preferred_element_type=jnp.float32
        )
        inner_sum = jnp.sum(weights * grad_weights, axis=-1, keepdims=True)
        grad_scores = (weights * (grad_weights - inner_sum)).astype(jnp.bfloat16)
        grad_query = jnp.dot(grad_scores, key_rows, preferred_element_type=jnp.float32) * inv_root
        grad_keys = (
            grad_keys
            + lax.dot_general(
                grad_scores,
                query_block,
                (((0,), (0,)), ((), ())),
                preferred_element_type=jnp.float32,
            )
            * inv_root
        )
        grad_values = grad_values + lax.dot_general(
            weights.astype(jnp.bfloat16),
            grad_block,
            (((0,), (0,)), ((), ())),
            preferred_element_type=jnp.float32,
        )
        return ((grad_keys, grad_values), grad_query)

    zeros_block = jnp.zeros((length, head_width), jnp.float32)
    (grad_keys, grad_values), grad_query = lax.scan(one_block, (zeros_block, zeros_block), starts)
    return (
        grad_query.reshape(length, head_width).astype(jnp.bfloat16),
        grad_keys.astype(jnp.bfloat16),
        grad_values.astype(jnp.bfloat16),
    )


def local(
    inputs,
    doc_ids,
    w_qkv,
    bias_q,
    bias_v,
    w_out,
    bias_out,
    norm1_gain,
    norm1_bias,
    norm2_gain,
    norm2_bias,
    w_up,
    bias_up,
    w_down,
    bias_down,
    cotangent,
):
    model_width = w_out.shape[0]
    tokens = inputs.shape[1]
    head_count = model_width // HEAD_DIM
    float_inputs = inputs[0].astype(jnp.float32)
    gain_one = norm1_gain.astype(jnp.float32)
    gain_two = norm2_gain.astype(jnp.float32)
    normed_in, normed_one, inv_one = layer_norm(
        float_inputs, gain_one, norm1_bias.astype(jnp.float32)
    )
    act_one = normed_in.astype(jnp.bfloat16)
    projected = jnp.dot(act_one, w_qkv, preferred_element_type=jnp.float32)
    query_rows = (projected[:, :model_width] + bias_q.astype(jnp.float32)).astype(jnp.bfloat16)
    key_rows = projected[:, model_width : 2 * model_width].astype(jnp.bfloat16)
    value_rows = (projected[:, 2 * model_width :] + bias_v.astype(jnp.float32)).astype(jnp.bfloat16)
    query_rows = query_rows.reshape(tokens, head_count, HEAD_DIM)
    key_rows = key_rows.reshape(tokens, head_count, HEAD_DIM)
    value_rows = value_rows.reshape(tokens, head_count, HEAD_DIM)
    whole_q, whole_k, whole_v = (
        lax.all_to_all(query_rows, "seq", split_axis=1, concat_axis=0, tiled=True),
        lax.all_to_all(key_rows, "seq", split_axis=1, concat_axis=0, tiled=True),
        lax.all_to_all(value_rows, "seq", split_axis=1, concat_axis=0, tiled=True),
    )
    row_docs = lax.all_gather(doc_ids, "seq", axis=1, tiled=True)[0]
    local_heads = whole_q.shape[1]
    length = whole_q.shape[0]
    block_rows = min(512, length)
    first_head = lax.axis_index("seq") * local_heads
    slopes = jnp.exp2(
        -(first_head + 1 + jnp.arange(local_heads, dtype=jnp.int32)).astype(jnp.float32)
    )
    head_q = jnp.moveaxis(whole_q, 1, 0)
    head_k = jnp.moveaxis(whole_k, 1, 0)
    head_v = jnp.moveaxis(whole_v, 1, 0)

    def forward_head(operands):
        return head_forward(
            operands[0], operands[1], operands[2], operands[3], row_docs, block_rows
        )

    head_outs, head_totals = lax.map(forward_head, (head_q, head_k, head_v, slopes))
    mixed_heads = lax.all_to_all(
        jnp.moveaxis(head_outs, 0, 1), "seq", split_axis=0, concat_axis=1, tiled=True
    )
    mixed_flat = mixed_heads.reshape(tokens, model_width)
    second = (
        float_inputs
        + jnp.dot(mixed_flat, w_out, preferred_element_type=jnp.float32)
        + bias_out.astype(jnp.float32)
    )
    normed_mid, normed_two, inv_two = layer_norm(second, gain_two, norm2_bias.astype(jnp.float32))
    act_two = normed_mid.astype(jnp.bfloat16)
    pre_act = jnp.dot(act_two, w_up, preferred_element_type=jnp.float32) + bias_up.astype(
        jnp.float32
    )
    activated, act_pullback = jax.vjp(smooth_act, pre_act)
    hidden = activated.astype(jnp.bfloat16)
    result = (
        second
        + jnp.dot(hidden, w_down, preferred_element_type=jnp.float32)
        + bias_down.astype(jnp.float32)
    )
    grad_out = cotangent[0].astype(jnp.float32)
    grad_low = grad_out.astype(jnp.bfloat16)
    g_bias_down = jnp.sum(grad_low.astype(jnp.float32), axis=0)
    g_w_down = lax.dot_general(
        hidden, grad_low, (((0,), (0,)), ((), ())), preferred_element_type=jnp.float32
    )
    grad_hidden = lax.dot_general(
        grad_low, w_down, (((1,), (1,)), ((), ())), preferred_element_type=jnp.float32
    )
    grad_pre = act_pullback(grad_hidden)[0].astype(jnp.bfloat16)
    g_bias_up = jnp.sum(grad_pre.astype(jnp.float32), axis=0)
    g_w_up = lax.dot_general(
        act_two, grad_pre, (((0,), (0,)), ((), ())), preferred_element_type=jnp.float32
    )
    grad_norm_two = lax.dot_general(
        grad_pre, w_up, (((1,), (1,)), ((), ())), preferred_element_type=jnp.float32
    )
    grad_mid, g_gain_two, g_shift_two = norm_back(grad_norm_two, normed_two, inv_two, gain_two)
    grad_second = grad_out + grad_mid
    grad_branch = grad_second.astype(jnp.bfloat16)
    g_bias_out = jnp.sum(grad_branch.astype(jnp.float32), axis=0)
    g_w_out = lax.dot_general(
        mixed_flat, grad_branch, (((0,), (0,)), ((), ())), preferred_element_type=jnp.float32
    )
    grad_mixed = lax.dot_general(
        grad_branch, w_out, (((1,), (1,)), ((), ())), preferred_element_type=jnp.float32
    ).astype(jnp.bfloat16)
    grad_whole = lax.all_to_all(
        grad_mixed.reshape(tokens, head_count, HEAD_DIM),
        "seq",
        split_axis=1,
        concat_axis=0,
        tiled=True,
    )
    grad_heads = jnp.moveaxis(grad_whole, 1, 0)

    def backward_head(operands):
        return head_backward(
            operands[0],
            operands[1],
            operands[2],
            operands[3],
            operands[4],
            operands[5],
            row_docs,
            block_rows,
        )

    grad_q, grad_k, grad_v = lax.map(
        backward_head, (head_q, head_k, head_v, grad_heads, head_totals, slopes)
    )
    back_q, back_k, back_v = (
        lax.all_to_all(jnp.moveaxis(grad_q, 0, 1), "seq", split_axis=0, concat_axis=1, tiled=True),
        lax.all_to_all(jnp.moveaxis(grad_k, 0, 1), "seq", split_axis=0, concat_axis=1, tiled=True),
        lax.all_to_all(jnp.moveaxis(grad_v, 0, 1), "seq", split_axis=0, concat_axis=1, tiled=True),
    )
    back_q = back_q.reshape(tokens, model_width)
    back_k = back_k.reshape(tokens, model_width)
    back_v = back_v.reshape(tokens, model_width)
    g_bias_q = jnp.sum(back_q.astype(jnp.float32), axis=0)
    g_bias_v = jnp.sum(back_v.astype(jnp.float32), axis=0)
    grad_proj = jnp.concatenate([back_q, back_k, back_v], axis=1)
    g_w_qkv = lax.dot_general(
        act_one, grad_proj, (((0,), (0,)), ((), ())), preferred_element_type=jnp.float32
    )
    grad_norm_one = lax.dot_general(
        grad_proj, w_qkv, (((1,), (1,)), ((), ())), preferred_element_type=jnp.float32
    )
    grad_first, g_gain_one, g_shift_one = norm_back(grad_norm_one, normed_one, inv_one, gain_one)
    grad_inputs = grad_second + grad_first
    matrices = (g_w_qkv, g_w_out, g_w_up, g_w_down)
    partial_sums = (
        lax.psum_scatter(
            matrices[0].astype(jnp.bfloat16), "dp", scatter_dimension=0, tiled=True
        ).astype(jnp.float32),
        lax.psum_scatter(
            matrices[1].astype(jnp.bfloat16), "dp", scatter_dimension=0, tiled=True
        ).astype(jnp.float32),
        lax.psum_scatter(
            matrices[2].astype(jnp.bfloat16), "dp", scatter_dimension=0, tiled=True
        ).astype(jnp.float32),
        lax.psum_scatter(
            matrices[3].astype(jnp.bfloat16), "dp", scatter_dimension=0, tiled=True
        ).astype(jnp.float32),
    )
    summed = (
        lax.psum_scatter(
            partial_sums[0].astype(jnp.bfloat16), "seq", scatter_dimension=1, tiled=True
        ).astype(jnp.float32),
        lax.psum_scatter(
            partial_sums[1].astype(jnp.bfloat16), "seq", scatter_dimension=1, tiled=True
        ).astype(jnp.float32),
        lax.psum_scatter(
            partial_sums[2].astype(jnp.bfloat16), "seq", scatter_dimension=1, tiled=True
        ).astype(jnp.float32),
        lax.psum_scatter(
            partial_sums[3].astype(jnp.bfloat16), "seq", scatter_dimension=1, tiled=True
        ).astype(jnp.float32),
    )
    vectors = lax.psum(
        (
            g_bias_q,
            g_bias_v,
            g_bias_out,
            g_gain_one,
            g_shift_one,
            g_gain_two,
            g_shift_two,
            g_bias_up,
            g_bias_down,
        ),
        ("dp", "seq"),
    )
    return (
        result.astype(jnp.bfloat16)[None],
        grad_inputs[None],
        summed[0],
        vectors[0],
        vectors[1],
        summed[1],
        vectors[2],
        vectors[3],
        vectors[4],
        vectors[5],
        vectors[6],
        summed[2],
        vectors[7],
        summed[3],
        vectors[8],
    )


def solution(mesh):
    in_specs = (
        P("dp", "seq", None),
        P("dp", "seq"),
        P(),
        P(),
        P(),
        P(),
        P(),
        P(),
        P(),
        P(),
        P(),
        P(),
        P(),
        P(),
        P(),
        P("dp", "seq", None),
    )
    out_specs = (
        P("dp", "seq", None),
        P("dp", "seq", None),
        P("dp", "seq"),
        P(),
        P(),
        P("dp", "seq"),
        P(),
        P(),
        P(),
        P(),
        P(),
        P("dp", "seq"),
        P(),
        P("dp", "seq"),
        P(),
    )
    sizes = (mesh.shape["dp"], mesh.shape["seq"])
    chosen = fast_local if sizes == (16, 2) else local
    return jax.shard_map(chosen, mesh=mesh, in_specs=in_specs, out_specs=out_specs, check_vma=False)
```

```python
import functools

import jax
import jax.numpy as jnp
import numpy as np
from jax import lax
from jax.experimental import pallas as pl
from jax.experimental.pallas import tpu as pltpu
from jax.sharding import PartitionSpec as P

HEAD_DIM = 128
MESH = pl.DeviceIdType.MESH
F32 = jnp.float32
BF16 = jnp.bfloat16
LOG2E = 1.4426950408889634
FAR = 1e30
GELU_C = 0.7978845608028654
GELU_A = 0.044715

norm_eps = 1e-05
masked_score = -1e30

NT = (((1,), (1,)), ((), ()))
TN = (((0,), (0,)), ((), ()))


def dot(a, b):
    return jnp.dot(a, b, preferred_element_type=F32)


def dot_nt(a, b):
    return lax.dot_general(a, b, NT, preferred_element_type=F32)


def dot_tn(a, b):
    return lax.dot_general(a, b, TN, preferred_element_type=F32)


def coords():
    dp = lax.axis_index("dp")
    return {
        "c": dp % 2,
        "x": (dp // 2) % 2,
        "a": (dp // 4) % 2,
        "b": dp // 8,
        "y": lax.axis_index("seq"),
    }


def partner(kind):
    dp = lax.axis_index("dp")
    if kind == "y":
        return {"seq": 1 - lax.axis_index("seq")}
    step = {"c": 1, "x": 2, "a": 4, "b": 8}[kind]
    bit = (dp // step) % 2
    return {"dp": dp + step - 2 * step * bit}


def greet(kinds):
    barrier = pltpu.get_barrier_semaphore()
    for kind in kinds:
        pl.semaphore_signal(barrier, inc=1, device_id=partner(kind), device_id_type=MESH)
    pl.semaphore_wait(barrier, len(kinds))


ORDERS = (("x", "a", "y", "b"), ("y", "a", "x", "b"))


ALONG_X = (18, 20, 22)


def order_of(chunk, half):
    return ORDERS[0 if isinstance(chunk, int) and chunk in ALONG_X else half]


def block_index(chunk, half, place):
    index = half * 16
    for kind, weight in zip(order_of(chunk, half), (8, 4, 2, 1)):
        index = index + place[kind] * weight
    return index


def dp_bits(dp):
    return {"c": dp % 2, "x": (dp // 2) % 2, "a": (dp // 4) % 2, "b": dp // 8}


class Scatter:
    def __init__(self, held, arrivals, send_sem, recv_sem):
        self.held, self.arrivals = held, arrivals
        self.send_sem, self.recv_sem = send_sem, recv_sem
        self.me = coords()

    def offset(self, chunk, half, stage, other):
        index = half * 16
        for k, weight in zip(range(stage + 1), (8, 4, 2, 1)):
            bit = self.me[order_of(chunk, half)[k]]
            if other and k == stage:
                bit = 1 - bit
            index = index + bit * weight
        return index

    def copy(self, chunk, stage, half):
        size = 8 >> stage
        return pltpu.make_async_remote_copy(
            src_ref=self.held.at[chunk, pl.ds(self.offset(chunk, half, stage, True), size)],
            dst_ref=self.arrivals[stage].at[chunk, half],
            send_sem=self.send_sem.at[stage],
            recv_sem=self.recv_sem.at[stage, chunk],
            device_id=partner(order_of(chunk, half)[stage]),
            device_id_type=MESH,
        )

    def start(self, chunk, stage):
        for half in range(2):
            self.copy(chunk, stage, half).start()

    def whole(self, stage, ref, at):
        return pltpu.make_async_remote_copy(
            src_ref=ref, dst_ref=ref, send_sem=self.send_sem.at[stage], recv_sem=self.recv_sem.at[stage, at],
            device_id=partner("x"), device_id_type=MESH,
        )

    def sent(self):
        for stage in range(4):
            self.whole(stage, self.arrivals[stage], 0).wait_send()

    def finish(self, chunk, stage):
        size = 8 >> stage
        self.whole(stage, self.arrivals[stage].at[chunk], chunk).wait_recv()
        for half in range(2):
            mine = pl.ds(self.offset(chunk, half, stage, False), size)
            self.held[chunk, mine] = self.held[chunk, mine] + self.arrivals[stage][chunk, half]

    def result(self, chunk, half):
        return self.held[chunk, self.offset(chunk, half, 3, False)]


def arrival_shapes(chunks):
    return [pltpu.VMEM((chunks, 2, 8 >> k, 32, 256), BF16) for k in range(4)]


def when(cond, fn):
    if isinstance(cond, (bool, np.bool_)):
        if cond:
            fn()
    else:
        pl.when(cond)(fn)


def inside(value, low, high):
    if isinstance(value, int):
        return low <= value < high
    return (value >= low) & (value < high)


RING = 3
AHEAD = 2


def row_of(ref):
    return ref[...].astype(F32).reshape(1, -1)


def layer_kernel(
    halo, x_hbm, doc_hbm, slope_hbm, bq_hbm, bv_hbm, bo_hbm, g1_hbm, s1_hbm, g2_hbm, s2_hbm, bup_hbm, bdown_hbm,
    cot_hbm, wqkv_hbm, wout_hbm, wup_hbm, wdown_hbm,
    out_hbm, gin_hbm, gup_hbm, gdown_hbm, gout_hbm, gqkv_hbm, vec_hbm,
    gup, gdown, gout, gqkv, vec,
    x_ref, doc_ref, slope_ref, bq_ref, bv_ref, bo_ref, g1_ref, s1_ref, g2_ref, s2_ref, bup_ref, bdown_ref,
    qkv, act1t, ot, dist, doch, x2, cot, act2, act2t, hid_t, dpre, dn2, dn1, dnh, dqkv, wu, wd, bias, bup,
    grad, held, r1, r2, r3, r4, vin,
    rsem, isem, qsem, osem, wsem, csem, cs, cr, ss, rs, hs, hr, vs, vr, esem,
):
    tokens, width = x_ref.shape
    heads = width // HEAD_DIM
    ff = wup_hbm.shape[1]
    half_ff = ff // 2
    steps = half_ff // 256
    seq = lax.axis_index("seq")
    me = coords()
    first_down, first_out, first_qkv, chunks = steps, 2 * steps, 2 * steps + 2, 2 * steps + 8
    scale = HEAD_DIM**-0.5

    act1 = dqkv.at[:, pl.ds(0, width)]
    o_s = dqkv.at[pl.ds(halo, tokens), pl.ds(width, width)]
    xh = dqkv.at[pl.ds(0, halo), pl.ds(2 * width, width)]
    wout_low = dqkv.at[pl.ds(halo, 512), pl.ds(2 * width, width)]

    dn_come = qkv.at[pl.ds(0, halo), pl.ds(0, width)]
    dn_send = qkv.at[pl.ds(0, halo), pl.ds(width, width)]

    def wqkv_part(j):
        return wu.at[j] if j < 2 else hid_t.at[pl.ds((j - 2) * width, width)]

    qloads = [
        pltpu.make_async_copy(wqkv_hbm.at[:, pl.ds(j * 512, 512)], wqkv_part(j), qsem.at[j]) for j in range(6)
    ]
    oloads = [
        pltpu.make_async_copy(wout_hbm.at[pl.ds(0, 512)], wout_low, osem.at[0]),
        pltpu.make_async_copy(wout_hbm.at[pl.ds(512, 512)], wd.at[1], osem.at[1]),
    ]
    cload = pltpu.make_async_copy(cot_hbm, cot, csem)
    iloads = [
        pltpu.make_async_copy(src, dst, isem.at[i])
        for i, (src, dst) in enumerate(
            (
                (x_hbm, x_ref), (g1_hbm, g1_ref), (s1_hbm, s1_ref), (bq_hbm, bq_ref), (bv_hbm, bv_ref),
                (doc_hbm, doc_ref), (slope_hbm, slope_ref), (bo_hbm, bo_ref), (g2_hbm, g2_ref), (s2_hbm, s2_ref),
                (bup_hbm, bup_ref), (bdown_hbm, bdown_ref),
            )
        )
    ]
    for cp in iloads + qloads + oloads + [cload]:
        cp.start()
    greet(("c", "x", "a", "b", "y"))
    part_rows = halo // 2
    send_x = [
        pltpu.make_async_remote_copy(
            src_ref=x_hbm.at[pl.ds(tokens - halo + (1 - i) * part_rows, part_rows)],
            dst_ref=xh.at[pl.ds((1 - i) * part_rows, part_rows)], send_sem=hs.at[i], recv_sem=hr.at[i],
            device_id=partner("y"), device_id_type=MESH,
        )
        for i in range(2)
    ]
    send_doc = pltpu.make_async_remote_copy(
        src_ref=doc_hbm, dst_ref=doch, send_sem=hs.at[3], recv_sem=hr.at[3],
        device_id=partner("y"), device_id_type=MESH,
    )

    @pl.when(seq == 0)
    def _():
        send_doc.start()
        for cp in send_x:
            cp.start()

    for cp in iloads:
        cp.wait()

    def weights(f, slot):
        col = pl.multiple_of(f * 256, 256)
        return [
            pltpu.make_async_copy(wup_hbm.at[:, pl.ds(col, 256)], wu.at[slot, :, pl.ds(0, 256)], wsem.at[slot, 0]),
            pltpu.make_async_copy(
                wup_hbm.at[:, pl.ds(half_ff + col, 256)], wu.at[slot, :, pl.ds(256, 256)], wsem.at[slot, 1]
            ),
            pltpu.make_async_copy(wdown_hbm.at[pl.ds(col, 256)], wd.at[slot, pl.ds(0, 256)], wsem.at[slot, 2]),
            pltpu.make_async_copy(
                wdown_hbm.at[pl.ds(half_ff + col, 256)], wd.at[slot, pl.ds(256, 256)], wsem.at[slot, 3]
            ),
        ]

    scatter = Scatter(held, (r1, r2, r3, r4), ss, rs)

    def core_copy(n):
        return pltpu.make_async_remote_copy(
            src_ref=grad.at[n % RING, 1 - me["c"]], dst_ref=held.at[n], send_sem=cs.at[n % RING], recv_sem=cr.at[n],
            device_id=partner("c"), device_id_type=MESH,
        )

    def join(n):
        core_copy(n).wait()
        held[n] = held[n] + grad[n % RING, me["c"]]

    def put(n, yy, m, tile):
        for q in range(4):
            place = dp_bits(m * 4 + q)
            place["y"] = yy
            for h in range(2):
                r0 = q * 64 + h * 32
                grad[n % RING, place["c"], block_index(n, h, place)] = tile[r0 : r0 + 32].astype(BF16)

    def store(n):
        for h in range(2):
            block = scatter.result(n, h)

            def up():
                gup[h * 32 : h * 32 + 32, pl.ds(pl.multiple_of(n * 256, 256), 256)] = block

            def down():
                i = n - first_down
                row = pl.multiple_of((i % 4) * 64 + h * 32, 32)
                gdown[pl.ds(row, 32), pl.ds(pl.multiple_of((i // 4) * 256, 256), 256)] = block

            def outp():
                gout[h * 32 : h * 32 + 32, pl.ds(pl.multiple_of((n - first_out) * 256, 256), 256)] = block

            def proj():
                gqkv[h * 32 : h * 32 + 32, pl.ds(pl.multiple_of((n - first_qkv) * 256, 256), 256)] = block

            when(inside(n, 0, first_down), up)
            when(inside(n, first_down, first_out), down)
            when(inside(n, first_out, first_qkv), outp)
            when(inside(n, first_qkv, chunks), proj)

    def service(t, ahead=True):
        if ahead:
            when(inside(t + AHEAD, 0, chunks), lambda: scatter.start(t + AHEAD, 0))

        def last():
            scatter.finish(t - 6, 3)
            store(t - 6)

        when(inside(t - 6, 0, chunks), last)
        for stage in (2, 1, 0):
            n = t - 2 * stage

            def step(stage=stage, n=n):
                scatter.finish(n, stage)
                scatter.start(n, stage + 1)

            when(inside(n, 0, chunks), step)

    gain1, shift1 = row_of(g1_ref), row_of(s1_ref)
    gain2, shift2 = row_of(g2_ref), row_of(s2_ref)

    def norm(v, gain, shift):
        center = v - jnp.mean(v, axis=-1, keepdims=True)
        inv = lax.rsqrt(jnp.mean(center * center, axis=-1, keepdims=True) + norm_eps)
        return center * inv * gain + shift

    bias[:, 0:width] = row_of(bq_ref)
    bias[:, width : 2 * width] = jnp.zeros((1, width), F32)
    bias[:, 2 * width :] = row_of(bv_ref)
    bup[...] = row_of(bup_ref)

    def norm_rows(m):
        for r in range(2 * m, 2 * m + 2):
            v = norm(x_ref[r * 128 : (r + 1) * 128].astype(F32), gain1, shift1).astype(BF16)
            act1[halo + r * 128 : halo + (r + 1) * 128] = v
            act1t[:, halo + r * 128 : halo + (r + 1) * 128] = v.T

    for m in range(tokens // 256):
        norm_rows(m)
    for j in range(6):
        qloads[j].wait()
        cols = slice(j * 512, (j + 1) * 512)
        for m in range(tokens // 256):
            rows = slice(halo + m * 256, halo + (m + 1) * 256)
            qkv[rows, cols] = (dot(act1[rows], wqkv_part(j)[...]) + bias[:, cols]).astype(BF16)
    for cp in weights(0, 0):
        cp.start()

    own_doc = doc_ref[...].astype(F32)
    own_cols = jnp.transpose(jnp.broadcast_to(own_doc, (128, tokens)))[:, 0:1]

    def distances(block, key_docs):
        keys = key_docs[block * 256 : block * 256 + 512]
        queries = own_doc[:, block * 256 : block * 256 + 256]
        key_pos = lax.broadcasted_iota(jnp.int32, (512, 256), 0)
        query_pos = lax.broadcasted_iota(jnp.int32, (512, 256), 1) + 256
        gap = query_pos - key_pos
        allowed = (gap >= 0) & (keys == queries)
        dist[block] = jnp.where(allowed, gap.astype(F32), FAR)

    def attend(block, which):
        def some_heads(i, carry):
            for u in range(FWD_HEADS):
                h = i * FWD_HEADS + u
                c0 = pl.multiple_of(h * HEAD_DIM, HEAD_DIM)
                slope = slope_ref[pl.ds(h, 1), 0:1]
                for t in which:
                    row = block * 256 + t * 128
                    q = qkv[halo + row : halo + row + 128, pl.ds(c0, HEAD_DIM)]
                    k = qkv[row : row + 384, pl.ds(width + c0, HEAD_DIM)]
                    v = qkv[row : row + 384, pl.ds(2 * width + c0, HEAD_DIM)]
                    far = dist[block, t * 128 : t * 128 + 384, t * 128 : t * 128 + 128]
                    s = dot_nt(k, q) * (LOG2E * scale) - slope * far
                    e = jnp.exp2(s - jnp.max(s, axis=0, keepdims=True))
                    p = (e * (1.0 / jnp.sum(e, axis=0, keepdims=True))).astype(BF16)
                    o_t = dot_tn(v, p)
                    ot[pl.ds(c0, HEAD_DIM), row : row + 128] = o_t.astype(BF16)
                    o_s[row : row + 128, pl.ds(c0, HEAD_DIM)] = o_t.T.astype(BF16)
            return carry

        lax.fori_loop(0, heads // FWD_HEADS, some_heads, 0)

    def project(block, which):
        for r in which:
            rows = slice(block * 256 + r * 128, block * 256 + (r + 1) * 128)
            second = (
                x_ref[rows].astype(F32) + dot(o_s[rows, 0:512], wout_low[...]) + dot(o_s[rows, 512:1024], wd[1])
            ) + row_of(bo_ref)
            x2[rows] = second
            v = norm(second, gain2, shift2).astype(BF16)
            act2[rows] = v
            act2t[:, rows] = v.T

    distances(1, jnp.concatenate([jnp.full((halo, 1), -1.0, F32), own_cols], axis=0))
    attend(1, (0, 1))
    for cp in oloads:
        cp.wait()
    project(1, (0, 1))

    @pl.when(seq == 0)
    def _():
        send_doc.wait_send()
        for cp in send_x:
            cp.wait_send()
        doch[...] = jnp.full(doch.shape, -1, jnp.int32)
        act1t[:, 0:halo] = jnp.zeros((width, halo), BF16)
        qkv[0:halo, width:] = jnp.zeros((halo, 2 * width), BF16)

    @pl.when(seq == 1)
    def _():
        send_doc.wait_recv()

    halo_doc = doch[...].astype(F32)[:, tokens - halo :]
    halo_cols = jnp.transpose(jnp.broadcast_to(halo_doc, (128, halo)))[:, 0:1]
    distances(0, jnp.concatenate([halo_cols, own_cols], axis=0))
    for i in range(2):
        rows = slice((1 - i) * part_rows, (2 - i) * part_rows)

        @pl.when(seq == 1)
        def _(i=i, rows=rows):
            send_x[i].wait_recv()
            v = norm(xh[rows].astype(F32), gain1, shift1).astype(BF16)
            act1[rows] = v
            act1t[:, rows] = v.T
            for j in range(2, 6):
                cols = slice(j * 512, (j + 1) * 512)
                qkv[rows, cols] = (dot(act1[rows], wqkv_part(j)[...]) + bias[:, cols]).astype(BF16)

        attend(0, (1 - i,))
        project(0, (1 - i,))

    cload.wait()
    vec[...] = jnp.zeros(vec.shape, F32)
    vec[7:8] = jnp.sum(cot[...].astype(F32), axis=0, keepdims=True)
    dn2[...] = jnp.zeros(dn2.shape, F32)

    def ff_step(f, carry):
        slot = f % 2
        for cp in weights(f, slot):
            cp.wait()

        @pl.when(f + 1 < steps)
        def _():
            for cp in weights(f + 1, 1 - slot):
                cp.start()

        for yy in range(2):
            if yy == 1:

                @pl.when(f >= 1)
                def _():
                    join(f - 1)
                    scatter.start(f - 1, 0)

            cols = slice(yy * 256, (yy + 1) * 256)
            first = pl.multiple_of(yy * half_ff + f * 256, 256)
            shift = bup[:, pl.ds(first, 256)]
            sums = jnp.zeros((1, 256), F32)
            for m in range(tokens // 256):
                rows = slice(m * 256, (m + 1) * 256)
                u = dot(act2[rows], wu[slot, :, cols]) + shift
                dh = dot_nt(cot[rows], wd[slot, cols])
                uu = u * u
                gate = 0.5 * jnp.tanh(u * (GELU_C + GELU_C * GELU_A * uu)) + 0.5
                act = u * gate
                hv = act.astype(BF16)
                slope = gate + act * (1.0 - gate) * (2.0 * GELU_C + 6.0 * GELU_C * GELU_A * uu)
                dv = (dh * slope).astype(BF16)
                dpre[rows, cols] = dv
                hid_t[pl.ds(first, 256), rows] = hv.T
                sums = sums + jnp.sum(dv.astype(F32), axis=0, keepdims=True)
            row = yy * (half_ff // width) + f // (width // 256)
            vec[pl.ds(8 + row, 1), pl.ds(pl.multiple_of((f % (width // 256)) * 256, 256), 256)] = sums

        for yy in range(2):
            cols = slice(yy * 256, (yy + 1) * 256)
            for m in range(width // 256):
                put(f, yy, m, dot(act2t[m * 256 : (m + 1) * 256], dpre[:, cols]))
        core_copy(f).start()
        for m in range(tokens // 256):
            rows = slice(m * 256, (m + 1) * 256)
            dn2[rows] += dot_nt(dpre[rows], wu[slot])
        service(f - 2, ahead=False)
        return carry

    lax.fori_loop(0, steps, ff_step, 0)
    join(steps - 1)
    scatter.start(steps - 1, 0)
    oloads = [pltpu.make_async_copy(wout_hbm.at[pl.ds(i * 512, 512)], wd.at[i], osem.at[i]) for i in range(2)]
    order = (2, 3, 4, 5, 0, 1)

    def qload(i):
        return pltpu.make_async_copy(wqkv_hbm.at[:, pl.ds(order[i] * 512, 512)], wu.at[i % 2], qsem.at[i % 2])

    for cp in oloads + [qload(0), qload(1)]:
        cp.start()

    def down_step(i, carry):
        n = first_down + i
        for yy in range(2):
            right = cot[:, pl.ds(pl.multiple_of(yy * 512 + (i // 4) * 256, 256), 256)]
            for m in range(4):
                left = jnp.concatenate(
                    [
                        hid_t[pl.ds(pl.multiple_of((m * 4 + q) * 256 + (i % 4) * 64, 64), 64)]
                        for q in range(4)
                    ],
                    axis=0,
                )
                put(n, yy, m, dot(left, right))
        core_copy(n).start()

        @pl.when(i >= 1)
        def _():
            join(n - 1)

        for at, t in ((2, steps - 2), (5, steps - 1), (7, steps)):

            @pl.when(i == at)
            def _(t=t):
                service(t)

        return carry

    lax.fori_loop(0, steps, down_step, 0)
    join(first_out - 1)

    def norm_two(r, carry):
        rows = pl.ds(pl.multiple_of(r * 64, 64), 64)
        v = x2[rows]
        center = v - jnp.mean(v, axis=-1, keepdims=True)
        inv = lax.rsqrt(jnp.mean(center * center, axis=-1, keepdims=True) + norm_eps)
        normed = center * inv
        dn = dn2[rows]
        e = dn * gain2
        vec[5:6] += jnp.sum(dn * normed, axis=0, keepdims=True)
        vec[6:7] += jnp.sum(dn, axis=0, keepdims=True)
        dx = cot[rows].astype(F32) + inv * (
            e - jnp.mean(e, axis=-1, keepdims=True) - normed * jnp.mean(e * normed, axis=-1, keepdims=True)
        )
        dn2[rows] = dx
        low = dx.astype(BF16)
        cot[rows] = low
        vec[2:3] += jnp.sum(low.astype(F32), axis=0, keepdims=True)
        return carry

    lax.fori_loop(0, tokens // 64, norm_two, 0)
    dx2, ab, do = dn2, cot, act2
    service(steps + 1)

    for j in range(2):
        for yy in range(2):
            c0 = yy * 512 + j * 256
            for m in range(width // 256):
                put(first_out + j, yy, m, dot(ot[m * 256 : (m + 1) * 256], ab[:, c0 : c0 + 256]))
        core_copy(first_out + j).start()
    service(steps + 2)
    for cp in oloads:
        cp.wait()
    for m in range(tokens // 256):
        rows = slice(m * 256, (m + 1) * 256)
        for i in range(2):
            do[rows, i * 512 : (i + 1) * 512] = dot_nt(ab[rows], wd[i]).astype(BF16)

    def dload(i):
        return pltpu.make_async_copy(wdown_hbm.at[pl.ds(i * 512, 512)], wd.at[i % 2], osem.at[i % 2])

    dload(0).start()
    dload(1).start()
    join(first_out)
    join(first_out + 1)
    service(steps + 3)

    dqkv[0:halo, 0:width] = jnp.zeros((halo, width), BF16)
    act2t[...] = jnp.zeros(act2t.shape, BF16)

    def head_back(h):
        c0 = pl.multiple_of(h * HEAD_DIM, HEAD_DIM)
        slope = slope_ref[pl.ds(h, 1), 0:1]
        parts = []
        for block in range(2):
            rows = slice(halo + block * 256, halo + (block + 1) * 256)
            krows = slice(block * 256, block * 256 + 512)
            q = qkv[rows, pl.ds(c0, HEAD_DIM)]
            k = qkv[krows, pl.ds(width + c0, HEAD_DIM)]
            g = do[block * 256 : (block + 1) * 256, pl.ds(c0, HEAD_DIM)]
            for t in range(2):
                row = block * 256 + t * 128
                keys, cols = slice(t * 128, t * 128 + 384), slice(t * 128, t * 128 + 128)
                qs = qkv[halo + row : halo + row + 128, pl.ds(c0, HEAD_DIM)]
                ks = qkv[row : row + 384, pl.ds(width + c0, HEAD_DIM)]
                vs = qkv[row : row + 384, pl.ds(2 * width + c0, HEAD_DIM)]
                s = dot_nt(ks, qs) * (LOG2E * scale) - slope * dist[block, keys, cols]
                e = jnp.exp2(s - jnp.max(s, axis=0, keepdims=True))
                p = e * (1.0 / jnp.sum(e, axis=0, keepdims=True))
                dp = dot_nt(vs, do[row : row + 128, pl.ds(c0, HEAD_DIM)])
                delta = jnp.sum(p * dp, axis=0, keepdims=True)
                keys = slice(block * 512 + t * 128, block * 512 + t * 128 + 384)
                act2t[keys, cols] = p.astype(BF16)
                act2t[keys, 256 + t * 128 : 384 + t * 128] = (p * (dp - delta)).astype(BF16)
            both = slice(block * 512, (block + 1) * 512)
            pb, ds = act2t[both, 0:256], act2t[both, 256:512]
            dqkv[rows, pl.ds(c0, HEAD_DIM)] = (dot_tn(k, ds) * scale).T.astype(BF16)
            parts.append((dot(ds, q) * scale, dot(pb, g)))
        for which in range(2):
            cols = pl.ds((1 + which) * width + c0, HEAD_DIM)
            first, second = parts[0][which], parts[1][which]
            dqkv[0:256, cols] = first[0:256].astype(BF16)
            dqkv[256:512, cols] = (first[256:512] + second[0:256]).astype(BF16)
            dqkv[512:768, cols] = second[256:512].astype(BF16)

    def heads_back(i, carry):
        for u in range(2):
            head_back(i * 2 + u)
        service(steps + 4 + i)
        return carry

    lax.fori_loop(0, heads // 2, heads_back, 0)
    vec[0:1] = jnp.sum(dqkv[halo:, 0:width].astype(F32), axis=0, keepdims=True)
    vec[1:2] = jnp.sum(dqkv[:, 2 * width :].astype(F32), axis=0, keepdims=True)

    state = {"t": steps + 4 + heads // 2}

    def serve():
        if state["t"] < chunks + 6:
            service(state["t"])
            state["t"] += 1

    back = pltpu.make_async_remote_copy(
        src_ref=dn_send, dst_ref=dn_come, send_sem=hs.at[2], recv_sem=hr.at[2],
        device_id=partner("y"), device_id_type=MESH,
    )

    def dn_part(i):
        cols = slice(order[i] * 512, (order[i] + 1) * 512)
        qload(i).wait()
        if i < 4:
            part = dot_nt(dqkv[0:halo, cols], wu[i % 2])
            if i == 0:
                dnh[...] = part
            elif i < 3:
                dnh[...] += part
            else:
                dn_send[...] = (dnh[...] + part).astype(BF16)
        for m in range(tokens // 256):
            rows = slice(m * 256, (m + 1) * 256)
            part = dot_nt(dqkv[halo + m * 256 : halo + (m + 1) * 256, cols], wu[i % 2])
            if i == 0:
                dn1[rows] = part
            else:
                dn1[rows] += part
        if i + 2 < 6:
            qload(i + 2).start()

    for j in range(6):
        n = first_qkv + j
        for yy in range(2):
            c0 = yy * (3 * width // 2) + j * 256
            for m in range(width // 256):
                put(n, yy, m, dot(act1t[m * 256 : (m + 1) * 256], dqkv[:, c0 : c0 + 256]))
        core_copy(n).start()
        if j >= 1:
            join(n - 1)
        if j in SERVE_AT:
            serve()
        if j == BACK_AT:
            for i in range(4):
                dn_part(i)

            @pl.when(seq == 1)
            def _():
                back.start()

            serve()
    join(chunks - 1)
    for i in (4, 5):
        dn_part(i)
    serve()

    def out_part(i):
        dload(i).wait()
        for m in range(tokens // 256):
            rows = slice(m * 256, (m + 1) * 256)
            part = dot_tn(hid_t[i * 512 : (i + 1) * 512, rows], wd[i % 2])
            if i == 0:
                part = part + row_of(bdown_ref)
            if i < 7:
                x2[rows] += part
            else:
                act2[rows] = (x2[rows] + part).astype(BF16)
        if i + 2 < 8:
            dload(i + 2).start()

    for i in range(3):
        out_part(i)
    for _ in range(N1_AFTER):
        serve()

    @pl.when(seq == 1)
    def _():
        back.wait_send()

    @pl.when(seq == 0)
    def _():
        back.wait_recv()
        dn1[tokens - halo :] += dn_come[...].astype(F32)

    def norm_one(r, carry):
        rows = pl.ds(pl.multiple_of(r * 64, 64), 64)
        v = x_ref[rows].astype(F32)
        center = v - jnp.mean(v, axis=-1, keepdims=True)
        inv = lax.rsqrt(jnp.mean(center * center, axis=-1, keepdims=True) + norm_eps)
        normed = center * inv
        dn = dn1[rows]
        e = dn * gain1
        vec[3:4] += jnp.sum(dn * normed, axis=0, keepdims=True)
        vec[4:5] += jnp.sum(dn, axis=0, keepdims=True)
        dn1[rows] = dx2[rows] + inv * (
            e - jnp.mean(e, axis=-1, keepdims=True) - normed * jnp.mean(e * normed, axis=-1, keepdims=True)
        )
        return carry

    lax.fori_loop(0, tokens // 64, norm_one, 0)
    save_gin = pltpu.make_async_copy(dn1, gin_hbm, esem.at[0])
    save_gin.start()

    kinds = ("c", "x", "y", "a", "b")

    def vec_copy(i):
        return pltpu.make_async_remote_copy(
            src_ref=vin.at[i, 0], dst_ref=vin.at[i, 1], send_sem=vs.at[i], recv_sem=vr.at[i],
            device_id=partner(kinds[i]), device_id_type=MESH,
        )

    vin[0, 0] = vec[...]
    vec_copy(0).start()
    save_out = pltpu.make_async_copy(act2, out_hbm, esem.at[1])
    for i in range(5):
        for _ in range(VEC_SERVES[i]):
            serve()
        if i == 0:
            out_part(3)
            out_part(4)
            out_part(5)
        if i == 1:
            out_part(6)
            out_part(7)
            save_out.start()
        vec_copy(i).wait()
        total = vin[i, 0] + vin[i, 1]
        if i < 4:
            vin[i + 1, 0] = total
            vec_copy(i + 1).start()
        else:
            vec[...] = total
    while state["t"] < chunks + 6:
        serve()
    saves = [
        pltpu.make_async_copy(src, dst, rsem.at[i])
        for i, (src, dst) in enumerate(
            ((gup, gup_hbm), (gdown, gdown_hbm), (gout, gout_hbm), (gqkv, gqkv_hbm), (vec, vec_hbm))
        )
    ]
    for cp in saves:
        cp.start()
    scatter.sent()
    for cp in saves:
        cp.wait()
    save_gin.wait()
    save_out.wait()


def finish_kernel(out_in, gin_in, gup, gdown, gout, gqkv, vec, *refs):
    out, gin, o_qkv, bq, bv, o_out, bo, g1, s1, g2, s2, o_up, b_up, o_down, b_down = refs
    out[...] = out_in[...]
    gin[...] = gin_in[...]
    o_qkv[...] = gqkv[...].astype(F32)
    o_out[...] = gout[...].astype(F32)
    o_up[...] = gup[...].astype(F32)
    o_down[...] = gdown[...].astype(F32)
    width = vec.shape[1]
    for i, ref in enumerate((bq, bv, bo, g1, s1, g2, s2, b_down)):
        ref[...] = vec[i]
    for i in range(b_up.shape[0] // width):
        b_up[i * width : (i + 1) * width] = vec[8 + i]


FWD_HEADS = 4
BACK_AT = 3
SERVE_AT = (1, 3, 5)
N1_AFTER = 1
VEC_SERVES = (1, 1, 1, 1, 1)


def vmem():
    return pl.BlockSpec(memory_space=pltpu.VMEM)


def hbm():
    return pl.BlockSpec(memory_space=pl.ANY)


def shape(dims, dtype):
    return jax.ShapeDtypeStruct(dims, dtype)


DMA = pltpu.SemaphoreType.DMA


def params(cid):
    return pltpu.CompilerParams(collective_id=cid, has_side_effects=True, vmem_limit_bytes=64 * 2**20 - 2**16)


def fast_local(
    inputs, doc_ids, w_qkv, bias_q, bias_v, w_out, bias_out, norm1_gain, norm1_bias, norm2_gain, norm2_bias,
    w_up, bias_up, w_down, bias_down, cotangent,
):
    x = inputs[0]
    tokens, width = x.shape
    ff = w_up.shape[1]
    halo = 256
    ext = tokens + halo
    heads = width // HEAD_DIM
    steps = ff // 512
    chunks = 2 * steps + 8
    slopes = jnp.asarray(
        np.broadcast_to((2.0 ** -(np.arange(heads) + 1.0) * LOG2E)[:, None], (heads, 128)).astype(np.float32)
    )
    shards = (
        (width // 16, ff // 2), (ff // 16, width // 2), (width // 16, width // 2), (width // 16, 3 * width // 2),
    )
    out, gin, g_up, g_down, g_out, g_qkv, vec = pl.pallas_call(
        functools.partial(layer_kernel, halo),
        out_shape=(shape((tokens, width), BF16), shape((tokens, width), F32))
        + tuple(shape(dims, BF16) for dims in shards)
        + (shape((16, width), F32),),
        in_specs=[hbm()] * 17,
        out_specs=(hbm(),) * 7,
        scratch_shapes=[pltpu.VMEM(dims, BF16) for dims in shards]
        + [pltpu.VMEM((16, width), F32)]
        + [pltpu.VMEM((tokens, width), BF16), pltpu.VMEM((1, tokens), jnp.int32), pltpu.VMEM((heads, 128), F32)]
        + [pltpu.VMEM((width,), BF16)] * 7
        + [pltpu.VMEM((ff,), BF16), pltpu.VMEM((width,), BF16)]
        + [
            pltpu.VMEM((ext, 3 * width), BF16),
            pltpu.VMEM((width, ext), BF16),
            pltpu.VMEM((width, tokens), BF16),
            pltpu.VMEM((2, 512, 256), F32),
            pltpu.VMEM((1, tokens), jnp.int32),
            pltpu.VMEM((tokens, width), F32),
            pltpu.VMEM((tokens, width), BF16),
            pltpu.VMEM((tokens, width), BF16),
            pltpu.VMEM((width, tokens), BF16),
            pltpu.VMEM((ff, tokens), BF16),
            pltpu.VMEM((tokens, 512), BF16),
            pltpu.VMEM((tokens, width), F32),
            pltpu.VMEM((tokens, width), F32),
            pltpu.VMEM((halo, width), F32),
            pltpu.VMEM((ext, 3 * width), BF16),
            pltpu.VMEM((2, width, 512), BF16),
            pltpu.VMEM((2, 512, width), BF16),
            pltpu.VMEM((1, 3 * width), F32),
            pltpu.VMEM((1, ff), F32),
            pltpu.VMEM((RING, 2, 32, 32, 256), BF16),
            pltpu.VMEM((chunks, 32, 32, 256), BF16),
        ]
        + arrival_shapes(chunks)
        + [
            pltpu.VMEM((5, 2, 16, width), F32),
            DMA((5,)), DMA((12,)), DMA((6,)), DMA((2,)), DMA((2, 4)), DMA, DMA((RING,)), DMA((chunks,)), DMA((4,)),
            DMA((4, chunks)), DMA((4,)), DMA((4,)), DMA((5,)), DMA((5,)), DMA((2,)),
        ],
        compiler_params=params(0),
        name="layer",
    )(
        x, doc_ids, slopes, bias_q, bias_v, bias_out, norm1_gain, norm1_bias, norm2_gain, norm2_bias, bias_up, bias_down,
        cotangent[0], w_qkv, w_out, w_up, w_down,
    )
    row = shape((width,), F32)
    return_shapes = (
        shape((tokens, width), BF16), shape((tokens, width), F32), shape(shards[3], F32), row, row, shape(shards[2], F32),
        row, row, row, row, row, shape(shards[0], F32), shape((ff,), F32), shape(shards[1], F32), row,
    )
    results = pl.pallas_call(
        finish_kernel,
        out_shape=return_shapes,
        in_specs=[vmem()] * 7,
        out_specs=(vmem(),) * 15,
        name="hand_over",
    )(out, gin, g_up, g_down, g_out, g_qkv, vec)
    return (results[0][None], results[1][None]) + tuple(results[2:])


def smooth_act(values):
    return jax.nn.gelu(values, approximate=True)


def layer_norm(values, norm_gain, norm_shift):
    center = values - jnp.mean(values, axis=-1, keepdims=True)
    inv_std = lax.rsqrt(jnp.mean(center * center, axis=-1, keepdims=True) + norm_eps)
    normed = center * inv_std
    return (normed * norm_gain + norm_shift, normed, inv_std)


def norm_back(grad_out, normed, inv_std, norm_gain):
    grad_gain = jnp.sum(grad_out * normed, axis=0)
    grad_shift = jnp.sum(grad_out, axis=0)
    inner_grad = grad_out * norm_gain
    grad_in = inv_std * (
        inner_grad
        - jnp.mean(inner_grad, axis=-1, keepdims=True)
        - normed * jnp.mean(inner_grad * normed, axis=-1, keepdims=True)
    )
    return (grad_in, grad_gain, grad_shift)


def block_scores(query_block, key_rows, first_row, head_slope, row_docs):
    block_rows = query_block.shape[0]
    length = key_rows.shape[0]
    raw_scores = lax.dot_general(
        query_block, key_rows, (((1,), (1,)), ((), ())), preferred_element_type=jnp.float32
    )
    query_pos = first_row + jnp.arange(block_rows, dtype=jnp.int32)
    key_pos = jnp.arange(length, dtype=jnp.int32)
    offset = query_pos[:, None] - key_pos[None, :]
    query_doc = lax.dynamic_slice_in_dim(row_docs, first_row, block_rows)
    allowed = (offset >= 0) & (query_doc[:, None] == row_docs[None, :])
    scores = raw_scores * key_rows.shape[1] ** (-0.5) - head_slope * offset.astype(jnp.float32)
    return jnp.where(allowed, scores, masked_score)


def head_forward(query_rows, key_rows, value_rows, head_slope, row_docs, block_rows):
    starts = jnp.arange(query_rows.shape[0] // block_rows, dtype=jnp.int32) * block_rows

    def one_block(first_row):
        query_block = lax.dynamic_slice_in_dim(query_rows, first_row, block_rows)
        scores = block_scores(query_block, key_rows, first_row, head_slope, row_docs)
        row_max = jnp.max(scores, axis=-1, keepdims=True)
        exponent = jnp.exp(scores - row_max)
        row_total = jnp.sum(exponent, axis=-1, keepdims=True)
        weights = (exponent / row_total).astype(jnp.bfloat16)
        block_out = jnp.dot(weights, value_rows, preferred_element_type=jnp.float32).astype(
            jnp.bfloat16
        )
        return (block_out, (row_max + jnp.log(row_total))[:, 0])

    block_outs, log_total = lax.map(one_block, starts)
    return (block_outs.reshape(-1, value_rows.shape[1]), log_total.reshape(-1))


def head_backward(
    query_rows, key_rows, value_rows, grad_rows, log_total, head_slope, row_docs, block_rows
):
    length, head_width = key_rows.shape
    inv_root = head_width ** (-0.5)
    starts = jnp.arange(length // block_rows, dtype=jnp.int32) * block_rows

    def one_block(running, first_row):
        grad_keys, grad_values = running
        query_block = lax.dynamic_slice_in_dim(query_rows, first_row, block_rows)
        grad_block = lax.dynamic_slice_in_dim(grad_rows, first_row, block_rows)
        total_block = lax.dynamic_slice_in_dim(log_total, first_row, block_rows)
        scores = block_scores(query_block, key_rows, first_row, head_slope, row_docs)
        weights = jnp.exp(scores - total_block[:, None])
        grad_weights = lax.dot_general(
            grad_block, value_rows, (((1,), (1,)), ((), ())), preferred_element_type=jnp.float32
        )
        inner_sum = jnp.sum(weights * grad_weights, axis=-1, keepdims=True)
        grad_scores = (weights * (grad_weights - inner_sum)).astype(jnp.bfloat16)
        grad_query = jnp.dot(grad_scores, key_rows, preferred_element_type=jnp.float32) * inv_root
        grad_keys = (
            grad_keys
            + lax.dot_general(
                grad_scores,
                query_block,
                (((0,), (0,)), ((), ())),
                preferred_element_type=jnp.float32,
            )
            * inv_root
        )
        grad_values = grad_values + lax.dot_general(
            weights.astype(jnp.bfloat16),
            grad_block,
            (((0,), (0,)), ((), ())),
            preferred_element_type=jnp.float32,
        )
        return ((grad_keys, grad_values), grad_query)

    zeros_block = jnp.zeros((length, head_width), jnp.float32)
    (grad_keys, grad_values), grad_query = lax.scan(one_block, (zeros_block, zeros_block), starts)
    return (
        grad_query.reshape(length, head_width).astype(jnp.bfloat16),
        grad_keys.astype(jnp.bfloat16),
        grad_values.astype(jnp.bfloat16),
    )


def local(
    inputs,
    doc_ids,
    w_qkv,
    bias_q,
    bias_v,
    w_out,
    bias_out,
    norm1_gain,
    norm1_bias,
    norm2_gain,
    norm2_bias,
    w_up,
    bias_up,
    w_down,
    bias_down,
    cotangent,
):
    model_width = w_out.shape[0]
    tokens = inputs.shape[1]
    head_count = model_width // HEAD_DIM
    float_inputs = inputs[0].astype(jnp.float32)
    gain_one = norm1_gain.astype(jnp.float32)
    gain_two = norm2_gain.astype(jnp.float32)
    normed_in, normed_one, inv_one = layer_norm(
        float_inputs, gain_one, norm1_bias.astype(jnp.float32)
    )
    act_one = normed_in.astype(jnp.bfloat16)
    projected = jnp.dot(act_one, w_qkv, preferred_element_type=jnp.float32)
    query_rows = (projected[:, :model_width] + bias_q.astype(jnp.float32)).astype(jnp.bfloat16)
    key_rows = projected[:, model_width : 2 * model_width].astype(jnp.bfloat16)
    value_rows = (projected[:, 2 * model_width :] + bias_v.astype(jnp.float32)).astype(jnp.bfloat16)
    query_rows = query_rows.reshape(tokens, head_count, HEAD_DIM)
    key_rows = key_rows.reshape(tokens, head_count, HEAD_DIM)
    value_rows = value_rows.reshape(tokens, head_count, HEAD_DIM)
    whole_q, whole_k, whole_v = (
        lax.all_to_all(query_rows, "seq", split_axis=1, concat_axis=0, tiled=True),
        lax.all_to_all(key_rows, "seq", split_axis=1, concat_axis=0, tiled=True),
        lax.all_to_all(value_rows, "seq", split_axis=1, concat_axis=0, tiled=True),
    )
    row_docs = lax.all_gather(doc_ids, "seq", axis=1, tiled=True)[0]
    local_heads = whole_q.shape[1]
    length = whole_q.shape[0]
    block_rows = min(512, length)
    first_head = lax.axis_index("seq") * local_heads
    slopes = jnp.exp2(
        -(first_head + 1 + jnp.arange(local_heads, dtype=jnp.int32)).astype(jnp.float32)
    )
    head_q = jnp.moveaxis(whole_q, 1, 0)
    head_k = jnp.moveaxis(whole_k, 1, 0)
    head_v = jnp.moveaxis(whole_v, 1, 0)

    def forward_head(operands):
        return head_forward(
            operands[0], operands[1], operands[2], operands[3], row_docs, block_rows
        )

    head_outs, head_totals = lax.map(forward_head, (head_q, head_k, head_v, slopes))
    mixed_heads = lax.all_to_all(
        jnp.moveaxis(head_outs, 0, 1), "seq", split_axis=0, concat_axis=1, tiled=True
    )
    mixed_flat = mixed_heads.reshape(tokens, model_width)
    second = (
        float_inputs
        + jnp.dot(mixed_flat, w_out, preferred_element_type=jnp.float32)
        + bias_out.astype(jnp.float32)
    )
    normed_mid, normed_two, inv_two = layer_norm(second, gain_two, norm2_bias.astype(jnp.float32))
    act_two = normed_mid.astype(jnp.bfloat16)
    pre_act = jnp.dot(act_two, w_up, preferred_element_type=jnp.float32) + bias_up.astype(
        jnp.float32
    )
    activated, act_pullback = jax.vjp(smooth_act, pre_act)
    hidden = activated.astype(jnp.bfloat16)
    result = (
        second
        + jnp.dot(hidden, w_down, preferred_element_type=jnp.float32)
        + bias_down.astype(jnp.float32)
    )
    grad_out = cotangent[0].astype(jnp.float32)
    grad_low = grad_out.astype(jnp.bfloat16)
    g_bias_down = jnp.sum(grad_low.astype(jnp.float32), axis=0)
    g_w_down = lax.dot_general(
        hidden, grad_low, (((0,), (0,)), ((), ())), preferred_element_type=jnp.float32
    )
    grad_hidden = lax.dot_general(
        grad_low, w_down, (((1,), (1,)), ((), ())), preferred_element_type=jnp.float32
    )
    grad_pre = act_pullback(grad_hidden)[0].astype(jnp.bfloat16)
    g_bias_up = jnp.sum(grad_pre.astype(jnp.float32), axis=0)
    g_w_up = lax.dot_general(
        act_two, grad_pre, (((0,), (0,)), ((), ())), preferred_element_type=jnp.float32
    )
    grad_norm_two = lax.dot_general(
        grad_pre, w_up, (((1,), (1,)), ((), ())), preferred_element_type=jnp.float32
    )
    grad_mid, g_gain_two, g_shift_two = norm_back(grad_norm_two, normed_two, inv_two, gain_two)
    grad_second = grad_out + grad_mid
    grad_branch = grad_second.astype(jnp.bfloat16)
    g_bias_out = jnp.sum(grad_branch.astype(jnp.float32), axis=0)
    g_w_out = lax.dot_general(
        mixed_flat, grad_branch, (((0,), (0,)), ((), ())), preferred_element_type=jnp.float32
    )
    grad_mixed = lax.dot_general(
        grad_branch, w_out, (((1,), (1,)), ((), ())), preferred_element_type=jnp.float32
    ).astype(jnp.bfloat16)
    grad_whole = lax.all_to_all(
        grad_mixed.reshape(tokens, head_count, HEAD_DIM),
        "seq",
        split_axis=1,
        concat_axis=0,
        tiled=True,
    )
    grad_heads = jnp.moveaxis(grad_whole, 1, 0)

    def backward_head(operands):
        return head_backward(
            operands[0],
            operands[1],
            operands[2],
            operands[3],
            operands[4],
            operands[5],
            row_docs,
            block_rows,
        )

    grad_q, grad_k, grad_v = lax.map(
        backward_head, (head_q, head_k, head_v, grad_heads, head_totals, slopes)
    )
    back_q, back_k, back_v = (
        lax.all_to_all(jnp.moveaxis(grad_q, 0, 1), "seq", split_axis=0, concat_axis=1, tiled=True),
        lax.all_to_all(jnp.moveaxis(grad_k, 0, 1), "seq", split_axis=0, concat_axis=1, tiled=True),
        lax.all_to_all(jnp.moveaxis(grad_v, 0, 1), "seq", split_axis=0, concat_axis=1, tiled=True),
    )
    back_q = back_q.reshape(tokens, model_width)
    back_k = back_k.reshape(tokens, model_width)
    back_v = back_v.reshape(tokens, model_width)
    g_bias_q = jnp.sum(back_q.astype(jnp.float32), axis=0)
    g_bias_v = jnp.sum(back_v.astype(jnp.float32), axis=0)
    grad_proj = jnp.concatenate([back_q, back_k, back_v], axis=1)
    g_w_qkv = lax.dot_general(
        act_one, grad_proj, (((0,), (0,)), ((), ())), preferred_element_type=jnp.float32
    )
    grad_norm_one = lax.dot_general(
        grad_proj, w_qkv, (((1,), (1,)), ((), ())), preferred_element_type=jnp.float32
    )
    grad_first, g_gain_one, g_shift_one = norm_back(grad_norm_one, normed_one, inv_one, gain_one)
    grad_inputs = grad_second + grad_first
    matrices = (g_w_qkv, g_w_out, g_w_up, g_w_down)
    partial_sums = (
        lax.psum_scatter(
            matrices[0].astype(jnp.bfloat16), "dp", scatter_dimension=0, tiled=True
        ).astype(jnp.float32),
        lax.psum_scatter(
            matrices[1].astype(jnp.bfloat16), "dp", scatter_dimension=0, tiled=True
        ).astype(jnp.float32),
        lax.psum_scatter(
            matrices[2].astype(jnp.bfloat16), "dp", scatter_dimension=0, tiled=True
        ).astype(jnp.float32),
        lax.psum_scatter(
            matrices[3].astype(jnp.bfloat16), "dp", scatter_dimension=0, tiled=True
        ).astype(jnp.float32),
    )
    summed = (
        lax.psum_scatter(
            partial_sums[0].astype(jnp.bfloat16), "seq", scatter_dimension=1, tiled=True
        ).astype(jnp.float32),
        lax.psum_scatter(
            partial_sums[1].astype(jnp.bfloat16), "seq", scatter_dimension=1, tiled=True
        ).astype(jnp.float32),
        lax.psum_scatter(
            partial_sums[2].astype(jnp.bfloat16), "seq", scatter_dimension=1, tiled=True
        ).astype(jnp.float32),
        lax.psum_scatter(
            partial_sums[3].astype(jnp.bfloat16), "seq", scatter_dimension=1, tiled=True
        ).astype(jnp.float32),
    )
    vectors = lax.psum(
        (
            g_bias_q,
            g_bias_v,
            g_bias_out,
            g_gain_one,
            g_shift_one,
            g_gain_two,
            g_shift_two,
            g_bias_up,
            g_bias_down,
        ),
        ("dp", "seq"),
    )
    return (
        result.astype(jnp.bfloat16)[None],
        grad_inputs[None],
        summed[0],
        vectors[0],
        vectors[1],
        summed[1],
        vectors[2],
        vectors[3],
        vectors[4],
        vectors[5],
        vectors[6],
        summed[2],
        vectors[7],
        summed[3],
        vectors[8],
    )


def solution(mesh):
    in_specs = (
        P("dp", "seq", None),
        P("dp", "seq"),
        P(),
        P(),
        P(),
        P(),
        P(),
        P(),
        P(),
        P(),
        P(),
        P(),
        P(),
        P(),
        P(),
        P("dp", "seq", None),
    )
    out_specs = (
        P("dp", "seq", None),
        P("dp", "seq", None),
        P("dp", "seq"),
        P(),
        P(),
        P("dp", "seq"),
        P(),
        P(),
        P(),
        P(),
        P(),
        P("dp", "seq"),
        P(),
        P("dp", "seq"),
        P(),
    )
    sizes = (mesh.shape["dp"], mesh.shape["seq"])
    chosen = fast_local if sizes == (16, 2) else local
    return jax.shard_map(chosen, mesh=mesh, in_specs=in_specs, out_specs=out_specs, check_vma=False)
```

```python
import functools

import jax
import jax.numpy as jnp
import numpy as np
from jax import lax
from jax.experimental import pallas as pl
from jax.experimental.pallas import tpu as pltpu
from jax.sharding import PartitionSpec as P

HEAD_DIM = 128
MESH = pl.DeviceIdType.MESH
F32 = jnp.float32
BF16 = jnp.bfloat16
LOG2E = 1.4426950408889634
FAR = 1e30
GELU_C = 0.7978845608028654
GELU_A = 0.044715

norm_eps = 1e-05
masked_score = -1e30

NT = (((1,), (1,)), ((), ()))
TN = (((0,), (0,)), ((), ()))


def dot(a, b):
    return jnp.dot(a, b, preferred_element_type=F32)


def dot_nt(a, b):
    return lax.dot_general(a, b, NT, preferred_element_type=F32)


def dot_tn(a, b):
    return lax.dot_general(a, b, TN, preferred_element_type=F32)


def coords():
    dp = lax.axis_index("dp")
    return {
        "c": dp % 2,
        "x": (dp // 2) % 2,
        "a": (dp // 4) % 2,
        "b": dp // 8,
        "y": lax.axis_index("seq"),
    }


def partner(kind):
    dp = lax.axis_index("dp")
    if kind == "y":
        return {"seq": 1 - lax.axis_index("seq")}
    step = {"c": 1, "x": 2, "a": 4, "b": 8}[kind]
    bit = (dp // step) % 2
    return {"dp": dp + step - 2 * step * bit}


def greet(kinds):
    barrier = pltpu.get_barrier_semaphore()
    for kind in kinds:
        pl.semaphore_signal(barrier, inc=1, device_id=partner(kind), device_id_type=MESH)
    pl.semaphore_wait(barrier, len(kinds))


ORDERS = (("x", "a", "y", "b"), ("y", "a", "x", "b"))


ALONG_X = (18, 20, 22)


def order_of(chunk, half):
    return ORDERS[0 if isinstance(chunk, int) and chunk in ALONG_X else half]


def block_index(chunk, half, place):
    index = half * 16
    for kind, weight in zip(order_of(chunk, half), (8, 4, 2, 1)):
        index = index + place[kind] * weight
    return index


def dp_bits(dp):
    return {"c": dp % 2, "x": (dp // 2) % 2, "a": (dp // 4) % 2, "b": dp // 8}


class Scatter:
    def __init__(self, held, arrivals, send_sem, recv_sem):
        self.held, self.arrivals = held, arrivals
        self.send_sem, self.recv_sem = send_sem, recv_sem
        self.me = coords()

    def offset(self, chunk, half, stage, other):
        index = half * 16
        for k, weight in zip(range(stage + 1), (8, 4, 2, 1)):
            bit = self.me[order_of(chunk, half)[k]]
            if other and k == stage:
                bit = 1 - bit
            index = index + bit * weight
        return index

    def copy(self, chunk, stage, half):
        size = 8 >> stage
        return pltpu.make_async_remote_copy(
            src_ref=self.held.at[chunk, pl.ds(self.offset(chunk, half, stage, True), size)],
            dst_ref=self.arrivals[stage].at[chunk, half],
            send_sem=self.send_sem.at[stage],
            recv_sem=self.recv_sem.at[stage, chunk],
            device_id=partner(order_of(chunk, half)[stage]),
            device_id_type=MESH,
        )

    def start(self, chunk, stage):
        for half in range(2):
            self.copy(chunk, stage, half).start()

    def whole(self, stage, ref, at):
        return pltpu.make_async_remote_copy(
            src_ref=ref, dst_ref=ref, send_sem=self.send_sem.at[stage], recv_sem=self.recv_sem.at[stage, at],
            device_id=partner("x"), device_id_type=MESH,
        )

    def sent(self):
        for stage in range(4):
            self.whole(stage, self.arrivals[stage], 0).wait_send()

    def finish(self, chunk, stage):
        size = 8 >> stage
        self.whole(stage, self.arrivals[stage].at[chunk], chunk).wait_recv()
        for half in range(2):
            mine = pl.ds(self.offset(chunk, half, stage, False), size)
            self.held[chunk, mine] = self.held[chunk, mine] + self.arrivals[stage][chunk, half]

    def result(self, chunk, half):
        return self.held[chunk, self.offset(chunk, half, 3, False)]


def arrival_shapes(chunks):
    return [pltpu.VMEM((chunks, 2, 8 >> k, 32, 256), BF16) for k in range(4)]


def when(cond, fn):
    if isinstance(cond, (bool, np.bool_)):
        if cond:
            fn()
    else:
        pl.when(cond)(fn)


def inside(value, low, high):
    if isinstance(value, int):
        return low <= value < high
    return (value >= low) & (value < high)


RING = 3
AHEAD = 2


def row_of(ref):
    return ref[...].astype(F32).reshape(1, -1)


def layer_kernel(
    halo, x_hbm, doc_hbm, slope_hbm, bq_hbm, bv_hbm, bo_hbm, g1_hbm, s1_hbm, g2_hbm, s2_hbm, bup_hbm, bdown_hbm,
    cot_hbm, wqkv_hbm, wout_hbm, wup_hbm, wdown_hbm,
    out_hbm, gin_hbm, gup_hbm, gdown_hbm, gout_hbm, gqkv_hbm, vec_hbm,
    gup, gdown, gout, gqkv, vec,
    x_ref, doc_ref, slope_ref, bq_ref, bv_ref, bo_ref, g1_ref, s1_ref, g2_ref, s2_ref, bup_ref, bdown_ref,
    qkv, act1t, ot, dist, doch, x2, cot, act2, act2t, hid_t, dpre, dn2, dn1, dnh, dqkv, wu, wd, bias, bup,
    grad, held, r1, r2, r3, r4, vin,
    rsem, isem, qsem, osem, wsem, csem, cs, cr, ss, rs, hs, hr, vs, vr, esem,
):
    tokens, width = x_ref.shape
    heads = width // HEAD_DIM
    ff = wup_hbm.shape[1]
    half_ff = ff // 2
    steps = half_ff // 256
    seq = lax.axis_index("seq")
    me = coords()
    first_down, first_out, first_qkv, chunks = steps, 2 * steps, 2 * steps + 2, 2 * steps + 8
    scale = HEAD_DIM**-0.5

    act1 = dqkv.at[:, pl.ds(0, width)]
    o_s = dqkv.at[pl.ds(halo, tokens), pl.ds(width, width)]
    xh = dqkv.at[pl.ds(0, halo), pl.ds(2 * width, width)]
    wout_low = dqkv.at[pl.ds(halo, 512), pl.ds(2 * width, width)]

    dn_come = qkv.at[pl.ds(0, halo), pl.ds(0, width)]
    dn_send = qkv.at[pl.ds(0, halo), pl.ds(width, width)]

    def wqkv_part(j):
        return wu.at[j] if j < 2 else hid_t.at[pl.ds((j - 2) * width, width)]

    qloads = [
        pltpu.make_async_copy(wqkv_hbm.at[:, pl.ds(j * 512, 512)], wqkv_part(j), qsem.at[j]) for j in range(6)
    ]
    oloads = [
        pltpu.make_async_copy(wout_hbm.at[pl.ds(0, 512)], wout_low, osem.at[0]),
        pltpu.make_async_copy(wout_hbm.at[pl.ds(512, 512)], wd.at[1], osem.at[1]),
    ]
    cload = pltpu.make_async_copy(cot_hbm, cot, csem)
    iloads = [
        pltpu.make_async_copy(src, dst, isem.at[i])
        for i, (src, dst) in enumerate(
            (
                (x_hbm, x_ref), (g1_hbm, g1_ref), (s1_hbm, s1_ref), (bq_hbm, bq_ref), (bv_hbm, bv_ref),
                (doc_hbm, doc_ref), (slope_hbm, slope_ref), (bo_hbm, bo_ref), (g2_hbm, g2_ref), (s2_hbm, s2_ref),
                (bup_hbm, bup_ref), (bdown_hbm, bdown_ref),
            )
        )
    ]
    for cp in iloads + qloads + oloads + [cload]:
        cp.start()
    greet(("c", "x", "a", "b", "y"))
    part_rows = halo // 2
    send_x = [
        pltpu.make_async_remote_copy(
            src_ref=x_hbm.at[pl.ds(tokens - halo + (1 - i) * part_rows, part_rows)],
            dst_ref=xh.at[pl.ds((1 - i) * part_rows, part_rows)], send_sem=hs.at[i], recv_sem=hr.at[i],
            device_id=partner("y"), device_id_type=MESH,
        )
        for i in range(2)
    ]
    send_doc = pltpu.make_async_remote_copy(
        src_ref=doc_hbm, dst_ref=doch, send_sem=hs.at[3], recv_sem=hr.at[3],
        device_id=partner("y"), device_id_type=MESH,
    )

    @pl.when(seq == 0)
    def _():
        send_doc.start()
        for cp in send_x:
            cp.start()

    for cp in iloads:
        cp.wait()

    def weights(f, slot):
        col = pl.multiple_of(f * 256, 256)
        return [
            pltpu.make_async_copy(wup_hbm.at[:, pl.ds(col, 256)], wu.at[slot, :, pl.ds(0, 256)], wsem.at[slot, 0]),
            pltpu.make_async_copy(
                wup_hbm.at[:, pl.ds(half_ff + col, 256)], wu.at[slot, :, pl.ds(256, 256)], wsem.at[slot, 1]
            ),
            pltpu.make_async_copy(wdown_hbm.at[pl.ds(col, 256)], wd.at[slot, pl.ds(0, 256)], wsem.at[slot, 2]),
            pltpu.make_async_copy(
                wdown_hbm.at[pl.ds(half_ff + col, 256)], wd.at[slot, pl.ds(256, 256)], wsem.at[slot, 3]
            ),
        ]

    scatter = Scatter(held, (r1, r2, r3, r4), ss, rs)

    def core_copy(n):
        return pltpu.make_async_remote_copy(
            src_ref=grad.at[n % RING, 1 - me["c"]], dst_ref=held.at[n], send_sem=cs.at[n % RING], recv_sem=cr.at[n],
            device_id=partner("c"), device_id_type=MESH,
        )

    def join(n):
        core_copy(n).wait()
        held[n] = held[n] + grad[n % RING, me["c"]]

    def put(n, yy, m, tile):
        for q in range(4):
            place = dp_bits(m * 4 + q)
            place["y"] = yy
            for h in range(2):
                r0 = q * 64 + h * 32
                grad[n % RING, place["c"], block_index(n, h, place)] = tile[r0 : r0 + 32].astype(BF16)

    def store(n):
        for h in range(2):
            block = scatter.result(n, h)

            def up():
                gup[h * 32 : h * 32 + 32, pl.ds(pl.multiple_of(n * 256, 256), 256)] = block

            def down():
                i = n - first_down
                row = pl.multiple_of((i % 4) * 64 + h * 32, 32)
                gdown[pl.ds(row, 32), pl.ds(pl.multiple_of((i // 4) * 256, 256), 256)] = block

            def outp():
                gout[h * 32 : h * 32 + 32, pl.ds(pl.multiple_of((n - first_out) * 256, 256), 256)] = block

            def proj():
                gqkv[h * 32 : h * 32 + 32, pl.ds(pl.multiple_of((n - first_qkv) * 256, 256), 256)] = block

            when(inside(n, 0, first_down), up)
            when(inside(n, first_down, first_out), down)
            when(inside(n, first_out, first_qkv), outp)
            when(inside(n, first_qkv, chunks), proj)

    def service(t, ahead=True):
        if ahead:
            when(inside(t + AHEAD, 0, chunks), lambda: scatter.start(t + AHEAD, 0))

        def last():
            scatter.finish(t - 6, 3)
            store(t - 6)

        when(inside(t - 6, 0, chunks), last)
        for stage in (2, 1, 0):
            n = t - 2 * stage

            def step(stage=stage, n=n):
                scatter.finish(n, stage)
                scatter.start(n, stage + 1)

            when(inside(n, 0, chunks), step)

    gain1, shift1 = row_of(g1_ref), row_of(s1_ref)
    gain2, shift2 = row_of(g2_ref), row_of(s2_ref)

    def norm(v, gain, shift):
        center = v - jnp.mean(v, axis=-1, keepdims=True)
        inv = lax.rsqrt(jnp.mean(center * center, axis=-1, keepdims=True) + norm_eps)
        return center * inv * gain + shift

    bias[:, 0:width] = row_of(bq_ref)
    bias[:, width : 2 * width] = jnp.zeros((1, width), F32)
    bias[:, 2 * width :] = row_of(bv_ref)
    bup[...] = row_of(bup_ref)

    def norm_rows(m):
        for r in range(2 * m, 2 * m + 2):
            v = norm(x_ref[r * 128 : (r + 1) * 128].astype(F32), gain1, shift1).astype(BF16)
            act1[halo + r * 128 : halo + (r + 1) * 128] = v
            act1t[:, halo + r * 128 : halo + (r + 1) * 128] = v.T

    for m in range(tokens // 256):
        norm_rows(m)
    for j in range(6):
        qloads[j].wait()
        cols = slice(j * 512, (j + 1) * 512)
        for m in range(tokens // 256):
            rows = slice(halo + m * 256, halo + (m + 1) * 256)
            qkv[rows, cols] = (dot(act1[rows], wqkv_part(j)[...]) + bias[:, cols]).astype(BF16)
    for cp in weights(0, 0):
        cp.start()

    own_doc = doc_ref[...].astype(F32)
    own_cols = jnp.transpose(jnp.broadcast_to(own_doc, (128, tokens)))[:, 0:1]

    def distances(block, key_docs):
        keys = key_docs[block * 256 : block * 256 + 512]
        queries = own_doc[:, block * 256 : block * 256 + 256]
        key_pos = lax.broadcasted_iota(jnp.int32, (512, 256), 0)
        query_pos = lax.broadcasted_iota(jnp.int32, (512, 256), 1) + 256
        gap = query_pos - key_pos
        allowed = (gap >= 0) & (keys == queries)
        dist[block] = jnp.where(allowed, gap.astype(F32), FAR)

    def attend(block, which):
        def some_heads(i, carry):
            for u in range(FWD_HEADS):
                h = i * FWD_HEADS + u
                c0 = pl.multiple_of(h * HEAD_DIM, HEAD_DIM)
                slope = slope_ref[pl.ds(h, 1), 0:1]
                for t in which:
                    row = block * 256 + t * 128
                    q = qkv[halo + row : halo + row + 128, pl.ds(c0, HEAD_DIM)]
                    k = qkv[row : row + 384, pl.ds(width + c0, HEAD_DIM)]
                    v = qkv[row : row + 384, pl.ds(2 * width + c0, HEAD_DIM)]
                    far = dist[block, t * 128 : t * 128 + 384, t * 128 : t * 128 + 128]
                    s = dot_nt(k, q) * (LOG2E * scale) - slope * far
                    e = jnp.exp2(s - jnp.max(s, axis=0, keepdims=True))
                    p = (e * (1.0 / jnp.sum(e, axis=0, keepdims=True))).astype(BF16)
                    o_t = dot_tn(v, p)
                    ot[pl.ds(c0, HEAD_DIM), row : row + 128] = o_t.astype(BF16)
                    o_s[row : row + 128, pl.ds(c0, HEAD_DIM)] = o_t.T.astype(BF16)
            return carry

        lax.fori_loop(0, heads // FWD_HEADS, some_heads, 0)

    def project(block, which):
        for r in which:
            rows = slice(block * 256 + r * 128, block * 256 + (r + 1) * 128)
            second = (
                x_ref[rows].astype(F32) + dot(o_s[rows, 0:512], wout_low[...]) + dot(o_s[rows, 512:1024], wd[1])
            ) + row_of(bo_ref)
            x2[rows] = second
            v = norm(second, gain2, shift2).astype(BF16)
            act2[rows] = v
            act2t[:, rows] = v.T

    distances(1, jnp.concatenate([jnp.full((halo, 1), -1.0, F32), own_cols], axis=0))
    attend(1, (0, 1))
    for cp in oloads:
        cp.wait()
    project(1, (0, 1))

    @pl.when(seq == 0)
    def _():
        send_doc.wait_send()
        for cp in send_x:
            cp.wait_send()
        doch[...] = jnp.full(doch.shape, -1, jnp.int32)
        act1t[:, 0:halo] = jnp.zeros((width, halo), BF16)
        qkv[0:halo, width:] = jnp.zeros((halo, 2 * width), BF16)

    @pl.when(seq == 1)
    def _():
        send_doc.wait_recv()

    halo_doc = doch[...].astype(F32)[:, tokens - halo :]
    halo_cols = jnp.transpose(jnp.broadcast_to(halo_doc, (128, halo)))[:, 0:1]
    distances(0, jnp.concatenate([halo_cols, own_cols], axis=0))
    for i in range(2):
        rows = slice((1 - i) * part_rows, (2 - i) * part_rows)

        @pl.when(seq == 1)
        def _(i=i, rows=rows):
            send_x[i].wait_recv()
            v = norm(xh[rows].astype(F32), gain1, shift1).astype(BF16)
            act1[rows] = v
            act1t[:, rows] = v.T
            for j in range(2, 6):
                cols = slice(j * 512, (j + 1) * 512)
                qkv[rows, cols] = (dot(act1[rows], wqkv_part(j)[...]) + bias[:, cols]).astype(BF16)

        attend(0, (1 - i,))
        project(0, (1 - i,))

    cload.wait()
    vec[...] = jnp.zeros(vec.shape, F32)
    vec[7:8] = jnp.sum(cot[...].astype(F32), axis=0, keepdims=True)
    dn2[...] = jnp.zeros(dn2.shape, F32)

    def ff_step(f, carry):
        slot = f % 2
        for cp in weights(f, slot):
            cp.wait()

        @pl.when(f + 1 < steps)
        def _():
            for cp in weights(f + 1, 1 - slot):
                cp.start()

        for yy in range(2):
            if yy == 1:

                @pl.when(f >= 1)
                def _():
                    join(f - 1)
                    scatter.start(f - 1, 0)

            cols = slice(yy * 256, (yy + 1) * 256)
            first = pl.multiple_of(yy * half_ff + f * 256, 256)
            shift = bup[:, pl.ds(first, 256)]
            sums = jnp.zeros((1, 256), F32)
            for m in range(tokens // 256):
                rows = slice(m * 256, (m + 1) * 256)
                u = dot(act2[rows], wu[slot, :, cols]) + shift
                dh = dot_nt(cot[rows], wd[slot, cols])
                uu = u * u
                gate = 0.5 * jnp.tanh(u * (GELU_C + GELU_C * GELU_A * uu)) + 0.5
                act = u * gate
                hv = act.astype(BF16)
                slope = gate + act * (1.0 - gate) * (2.0 * GELU_C + 6.0 * GELU_C * GELU_A * uu)
                dv = (dh * slope).astype(BF16)
                dpre[rows, cols] = dv
                hid_t[pl.ds(first, 256), rows] = hv.T
                sums = sums + jnp.sum(dv.astype(F32), axis=0, keepdims=True)
            row = yy * (half_ff // width) + f // (width // 256)
            vec[pl.ds(8 + row, 1), pl.ds(pl.multiple_of((f % (width // 256)) * 256, 256), 256)] = sums

        for yy in range(2):
            cols = slice(yy * 256, (yy + 1) * 256)
            for m in range(width // 256):
                put(f, yy, m, dot(act2t[m * 256 : (m + 1) * 256], dpre[:, cols]))
        core_copy(f).start()
        for m in range(tokens // 256):
            rows = slice(m * 256, (m + 1) * 256)
            dn2[rows] += dot_nt(dpre[rows], wu[slot])
        service(f - 2, ahead=False)
        return carry

    lax.fori_loop(0, steps, ff_step, 0)
    join(steps - 1)
    scatter.start(steps - 1, 0)
    oloads = [pltpu.make_async_copy(wout_hbm.at[pl.ds(i * 512, 512)], wd.at[i], osem.at[i]) for i in range(2)]
    order = (2, 3, 4, 5, 0, 1)

    def qload(i):
        return pltpu.make_async_copy(wqkv_hbm.at[:, pl.ds(order[i] * 512, 512)], wu.at[i % 2], qsem.at[i % 2])

    for cp in oloads + [qload(0), qload(1)]:
        cp.start()

    def down_step(i, carry):
        n = first_down + i
        for yy in range(2):
            right = cot[:, pl.ds(pl.multiple_of(yy * 512 + (i // 4) * 256, 256), 256)]
            for m in range(4):
                left = jnp.concatenate(
                    [
                        hid_t[pl.ds(pl.multiple_of((m * 4 + q) * 256 + (i % 4) * 64, 64), 64)]
                        for q in range(4)
                    ],
                    axis=0,
                )
                put(n, yy, m, dot(left, right))
        core_copy(n).start()

        @pl.when(i >= 1)
        def _():
            join(n - 1)

        for at, t in ((2, steps - 2), (5, steps - 1), (7, steps)):

            @pl.when(i == at)
            def _(t=t):
                service(t)

        return carry

    lax.fori_loop(0, steps, down_step, 0)
    join(first_out - 1)

    def norm_two(r, carry):
        rows = pl.ds(pl.multiple_of(r * 64, 64), 64)
        v = x2[rows]
        center = v - jnp.mean(v, axis=-1, keepdims=True)
        inv = lax.rsqrt(jnp.mean(center * center, axis=-1, keepdims=True) + norm_eps)
        normed = center * inv
        dn = dn2[rows]
        e = dn * gain2
        vec[5:6] += jnp.sum(dn * normed, axis=0, keepdims=True)
        vec[6:7] += jnp.sum(dn, axis=0, keepdims=True)
        dx = cot[rows].astype(F32) + inv * (
            e - jnp.mean(e, axis=-1, keepdims=True) - normed * jnp.mean(e * normed, axis=-1, keepdims=True)
        )
        dn2[rows] = dx
        low = dx.astype(BF16)
        cot[rows] = low
        vec[2:3] += jnp.sum(low.astype(F32), axis=0, keepdims=True)
        return carry

    lax.fori_loop(0, tokens // 64, norm_two, 0)
    dx2, ab, do = dn2, cot, act2
    service(steps + 1)

    for j in range(2):
        for yy in range(2):
            c0 = yy * 512 + j * 256
            for m in range(width // 256):
                put(first_out + j, yy, m, dot(ot[m * 256 : (m + 1) * 256], ab[:, c0 : c0 + 256]))
        core_copy(first_out + j).start()
    service(steps + 2)
    for cp in oloads:
        cp.wait()
    for m in range(tokens // 256):
        rows = slice(m * 256, (m + 1) * 256)
        for i in range(2):
            do[rows, i * 512 : (i + 1) * 512] = dot_nt(ab[rows], wd[i]).astype(BF16)

    def dload(i):
        return pltpu.make_async_copy(wdown_hbm.at[pl.ds(i * 512, 512)], wd.at[i % 2], osem.at[i % 2])

    dload(0).start()
    dload(1).start()
    join(first_out)
    join(first_out + 1)
    service(steps + 3)

    dqkv[0:halo, 0:width] = jnp.zeros((halo, width), BF16)
    act2t[...] = jnp.zeros(act2t.shape, BF16)

    def head_back(h):
        c0 = pl.multiple_of(h * HEAD_DIM, HEAD_DIM)
        slope = slope_ref[pl.ds(h, 1), 0:1]
        parts = []
        for block in range(2):
            rows = slice(halo + block * 256, halo + (block + 1) * 256)
            krows = slice(block * 256, block * 256 + 512)
            q = qkv[rows, pl.ds(c0, HEAD_DIM)]
            k = qkv[krows, pl.ds(width + c0, HEAD_DIM)]
            g = do[block * 256 : (block + 1) * 256, pl.ds(c0, HEAD_DIM)]
            for t in range(2):
                row = block * 256 + t * 128
                keys, cols = slice(t * 128, t * 128 + 384), slice(t * 128, t * 128 + 128)
                qs = qkv[halo + row : halo + row + 128, pl.ds(c0, HEAD_DIM)]
                ks = qkv[row : row + 384, pl.ds(width + c0, HEAD_DIM)]
                vs = qkv[row : row + 384, pl.ds(2 * width + c0, HEAD_DIM)]
                s = dot_nt(ks, qs) * (LOG2E * scale) - slope * dist[block, keys, cols]
                e = jnp.exp2(s - jnp.max(s, axis=0, keepdims=True))
                p = e * (1.0 / jnp.sum(e, axis=0, keepdims=True))
                dp = dot_nt(vs, do[row : row + 128, pl.ds(c0, HEAD_DIM)])
                delta = jnp.sum(p * dp, axis=0, keepdims=True)
                keys = slice(block * 512 + t * 128, block * 512 + t * 128 + 384)
                act2t[keys, cols] = p.astype(BF16)
                act2t[keys, 256 + t * 128 : 384 + t * 128] = (p * (dp - delta)).astype(BF16)
            both = slice(block * 512, (block + 1) * 512)
            pb, ds = act2t[both, 0:256], act2t[both, 256:512]
            dqkv[rows, pl.ds(c0, HEAD_DIM)] = (dot_tn(k, ds) * scale).T.astype(BF16)
            parts.append((dot(ds, q) * scale, dot(pb, g)))
        for which in range(2):
            cols = pl.ds((1 + which) * width + c0, HEAD_DIM)
            first, second = parts[0][which], parts[1][which]
            dqkv[0:256, cols] = first[0:256].astype(BF16)
            dqkv[256:512, cols] = (first[256:512] + second[0:256]).astype(BF16)
            dqkv[512:768, cols] = second[256:512].astype(BF16)

    def heads_back(i, carry):
        for u in range(2):
            head_back(i * 2 + u)
        service(steps + 4 + i)
        return carry

    lax.fori_loop(0, heads // 2, heads_back, 0)
    vec[0:1] = jnp.sum(dqkv[halo:, 0:width].astype(F32), axis=0, keepdims=True)
    vec[1:2] = jnp.sum(dqkv[:, 2 * width :].astype(F32), axis=0, keepdims=True)

    state = {"t": steps + 4 + heads // 2}

    def serve():
        if state["t"] < chunks + 6:
            service(state["t"])
            state["t"] += 1

    back = pltpu.make_async_remote_copy(
        src_ref=dn_send, dst_ref=dn_come, send_sem=hs.at[2], recv_sem=hr.at[2],
        device_id=partner("y"), device_id_type=MESH,
    )

    def dn_part(i):
        cols = slice(order[i] * 512, (order[i] + 1) * 512)
        qload(i).wait()
        if i < 4:
            part = dot_nt(dqkv[0:halo, cols], wu[i % 2])
            if i == 0:
                dnh[...] = part
            elif i < 3:
                dnh[...] += part
            else:
                dn_send[...] = (dnh[...] + part).astype(BF16)
        for m in range(tokens // 256):
            rows = slice(m * 256, (m + 1) * 256)
            part = dot_nt(dqkv[halo + m * 256 : halo + (m + 1) * 256, cols], wu[i % 2])
            if i == 0:
                dn1[rows] = part
            else:
                dn1[rows] += part
        if i + 2 < 6:
            qload(i + 2).start()

    for j in range(6):
        n = first_qkv + j
        for yy in range(2):
            c0 = yy * (3 * width // 2) + j * 256
            for m in range(width // 256):
                put(n, yy, m, dot(act1t[m * 256 : (m + 1) * 256], dqkv[:, c0 : c0 + 256]))
        core_copy(n).start()
        if j >= 1:
            join(n - 1)
        if j in SERVE_AT:
            serve()
        if j == BACK_AT:
            for i in range(4):
                dn_part(i)

            @pl.when(seq == 1)
            def _():
                back.start()

            serve()
    join(chunks - 1)
    for i in (4, 5):
        dn_part(i)
    serve()

    def out_part(i):
        dload(i).wait()
        for m in range(tokens // 256):
            rows = slice(m * 256, (m + 1) * 256)
            part = dot_tn(hid_t[i * 512 : (i + 1) * 512, rows], wd[i % 2])
            if i == 0:
                part = part + row_of(bdown_ref)
            if i < 7:
                x2[rows] += part
            else:
                act2[rows] = (x2[rows] + part).astype(BF16)
        if i + 2 < 8:
            dload(i + 2).start()

    for i in range(OUT_SPLIT[0]):
        out_part(i)
    for _ in range(N1_AFTER):
        serve()

    @pl.when(seq == 1)
    def _():
        back.wait_send()

    @pl.when(seq == 0)
    def _():
        back.wait_recv()
        dn1[tokens - halo :] += dn_come[...].astype(F32)

    def norm_one(r, carry):
        rows = pl.ds(pl.multiple_of(r * 64, 64), 64)
        v = x_ref[rows].astype(F32)
        center = v - jnp.mean(v, axis=-1, keepdims=True)
        inv = lax.rsqrt(jnp.mean(center * center, axis=-1, keepdims=True) + norm_eps)
        normed = center * inv
        dn = dn1[rows]
        e = dn * gain1
        vec[3:4] += jnp.sum(dn * normed, axis=0, keepdims=True)
        vec[4:5] += jnp.sum(dn, axis=0, keepdims=True)
        dn1[rows] = dx2[rows] + inv * (
            e - jnp.mean(e, axis=-1, keepdims=True) - normed * jnp.mean(e * normed, axis=-1, keepdims=True)
        )
        return carry

    lax.fori_loop(0, tokens // 64, norm_one, 0)
    save_gin = pltpu.make_async_copy(dn1, gin_hbm, esem.at[0])
    save_gin.start()

    kinds = ("c", "x", "y", "a", "b")

    def vec_copy(i):
        return pltpu.make_async_remote_copy(
            src_ref=vin.at[i, 0], dst_ref=vin.at[i, 1], send_sem=vs.at[i], recv_sem=vr.at[i],
            device_id=partner(kinds[i]), device_id_type=MESH,
        )

    vin[0, 0] = vec[...]
    vec_copy(0).start()
    save_out = pltpu.make_async_copy(act2, out_hbm, esem.at[1])
    for i in range(5):
        for _ in range(VEC_SERVES[i]):
            serve()
        if i == 0:
            for k in range(*OUT_SPLIT):
                out_part(k)
        if i == 1:
            for k in range(OUT_SPLIT[1], 8):
                out_part(k)
            save_out.start()
        vec_copy(i).wait()
        total = vin[i, 0] + vin[i, 1]
        if i < 4:
            vin[i + 1, 0] = total
            vec_copy(i + 1).start()
        else:
            vec[...] = total
    while state["t"] < chunks + 6:
        serve()
    saves = [
        pltpu.make_async_copy(src, dst, rsem.at[i])
        for i, (src, dst) in enumerate(
            ((gup, gup_hbm), (gdown, gdown_hbm), (gout, gout_hbm), (gqkv, gqkv_hbm), (vec, vec_hbm))
        )
    ]
    for cp in saves:
        cp.start()
    scatter.sent()
    for cp in saves:
        cp.wait()
    save_gin.wait()
    save_out.wait()


def finish_kernel(out_in, gin_in, gup, gdown, gout, gqkv, vec, *refs):
    out, gin, o_qkv, bq, bv, o_out, bo, g1, s1, g2, s2, o_up, b_up, o_down, b_down = refs
    out[...] = out_in[...]
    gin[...] = gin_in[...]
    o_qkv[...] = gqkv[...].astype(F32)
    o_out[...] = gout[...].astype(F32)
    o_up[...] = gup[...].astype(F32)
    o_down[...] = gdown[...].astype(F32)
    width = vec.shape[1]
    for i, ref in enumerate((bq, bv, bo, g1, s1, g2, s2, b_down)):
        ref[...] = vec[i]
    for i in range(b_up.shape[0] // width):
        b_up[i * width : (i + 1) * width] = vec[8 + i]


FWD_HEADS = 4
BACK_AT = 3
SERVE_AT = (1, 3, 5)
N1_AFTER = 1
VEC_SERVES = (1, 2, 2, 2, 2)
OUT_SPLIT = (3, 6)


def vmem():
    return pl.BlockSpec(memory_space=pltpu.VMEM)


def hbm():
    return pl.BlockSpec(memory_space=pl.ANY)


def shape(dims, dtype):
    return jax.ShapeDtypeStruct(dims, dtype)


DMA = pltpu.SemaphoreType.DMA


def params(cid):
    return pltpu.CompilerParams(collective_id=cid, has_side_effects=True, vmem_limit_bytes=64 * 2**20 - 2**16)


def fast_local(
    inputs, doc_ids, w_qkv, bias_q, bias_v, w_out, bias_out, norm1_gain, norm1_bias, norm2_gain, norm2_bias,
    w_up, bias_up, w_down, bias_down, cotangent,
):
    x = inputs[0]
    tokens, width = x.shape
    ff = w_up.shape[1]
    halo = 256
    ext = tokens + halo
    heads = width // HEAD_DIM
    steps = ff // 512
    chunks = 2 * steps + 8
    slopes = jnp.asarray(
        np.broadcast_to((2.0 ** -(np.arange(heads) + 1.0) * LOG2E)[:, None], (heads, 128)).astype(np.float32)
    )
    shards = (
        (width // 16, ff // 2), (ff // 16, width // 2), (width // 16, width // 2), (width // 16, 3 * width // 2),
    )
    out, gin, g_up, g_down, g_out, g_qkv, vec = pl.pallas_call(
        functools.partial(layer_kernel, halo),
        out_shape=(shape((tokens, width), BF16), shape((tokens, width), F32))
        + tuple(shape(dims, BF16) for dims in shards)
        + (shape((16, width), F32),),
        in_specs=[hbm()] * 17,
        out_specs=(hbm(),) * 7,
        scratch_shapes=[pltpu.VMEM(dims, BF16) for dims in shards]
        + [pltpu.VMEM((16, width), F32)]
        + [pltpu.VMEM((tokens, width), BF16), pltpu.VMEM((1, tokens), jnp.int32), pltpu.VMEM((heads, 128), F32)]
        + [pltpu.VMEM((width,), BF16)] * 7
        + [pltpu.VMEM((ff,), BF16), pltpu.VMEM((width,), BF16)]
        + [
            pltpu.VMEM((ext, 3 * width), BF16),
            pltpu.VMEM((width, ext), BF16),
            pltpu.VMEM((width, tokens), BF16),
            pltpu.VMEM((2, 512, 256), F32),
            pltpu.VMEM((1, tokens), jnp.int32),
            pltpu.VMEM((tokens, width), F32),
            pltpu.VMEM((tokens, width), BF16),
            pltpu.VMEM((tokens, width), BF16),
            pltpu.VMEM((width, tokens), BF16),
            pltpu.VMEM((ff, tokens), BF16),
            pltpu.VMEM((tokens, 512), BF16),
            pltpu.VMEM((tokens, width), F32),
            pltpu.VMEM((tokens, width), F32),
            pltpu.VMEM((halo, width), F32),
            pltpu.VMEM((ext, 3 * width), BF16),
            pltpu.VMEM((2, width, 512), BF16),
            pltpu.VMEM((2, 512, width), BF16),
            pltpu.VMEM((1, 3 * width), F32),
            pltpu.VMEM((1, ff), F32),
            pltpu.VMEM((RING, 2, 32, 32, 256), BF16),
            pltpu.VMEM((chunks, 32, 32, 256), BF16),
        ]
        + arrival_shapes(chunks)
        + [
            pltpu.VMEM((5, 2, 16, width), F32),
            DMA((5,)), DMA((12,)), DMA((6,)), DMA((2,)), DMA((2, 4)), DMA, DMA((RING,)), DMA((chunks,)), DMA((4,)),
            DMA((4, chunks)), DMA((4,)), DMA((4,)), DMA((5,)), DMA((5,)), DMA((2,)),
        ],
        compiler_params=params(0),
        name="layer",
    )(
        x, doc_ids, slopes, bias_q, bias_v, bias_out, norm1_gain, norm1_bias, norm2_gain, norm2_bias, bias_up, bias_down,
        cotangent[0], w_qkv, w_out, w_up, w_down,
    )
    row = shape((width,), F32)
    return_shapes = (
        shape((tokens, width), BF16), shape((tokens, width), F32), shape(shards[3], F32), row, row, shape(shards[2], F32),
        row, row, row, row, row, shape(shards[0], F32), shape((ff,), F32), shape(shards[1], F32), row,
    )
    results = pl.pallas_call(
        finish_kernel,
        out_shape=return_shapes,
        in_specs=[vmem()] * 7,
        out_specs=(vmem(),) * 15,
        name="hand_over",
    )(out, gin, g_up, g_down, g_out, g_qkv, vec)
    return (results[0][None], results[1][None]) + tuple(results[2:])


def smooth_act(values):
    return jax.nn.gelu(values, approximate=True)


def layer_norm(values, norm_gain, norm_shift):
    center = values - jnp.mean(values, axis=-1, keepdims=True)
    inv_std = lax.rsqrt(jnp.mean(center * center, axis=-1, keepdims=True) + norm_eps)
    normed = center * inv_std
    return (normed * norm_gain + norm_shift, normed, inv_std)


def norm_back(grad_out, normed, inv_std, norm_gain):
    grad_gain = jnp.sum(grad_out * normed, axis=0)
    grad_shift = jnp.sum(grad_out, axis=0)
    inner_grad = grad_out * norm_gain
    grad_in = inv_std * (
        inner_grad
        - jnp.mean(inner_grad, axis=-1, keepdims=True)
        - normed * jnp.mean(inner_grad * normed, axis=-1, keepdims=True)
    )
    return (grad_in, grad_gain, grad_shift)


def block_scores(query_block, key_rows, first_row, head_slope, row_docs):
    block_rows = query_block.shape[0]
    length = key_rows.shape[0]
    raw_scores = lax.dot_general(
        query_block, key_rows, (((1,), (1,)), ((), ())), preferred_element_type=jnp.float32
    )
    query_pos = first_row + jnp.arange(block_rows, dtype=jnp.int32)
    key_pos = jnp.arange(length, dtype=jnp.int32)
    offset = query_pos[:, None] - key_pos[None, :]
    query_doc = lax.dynamic_slice_in_dim(row_docs, first_row, block_rows)
    allowed = (offset >= 0) & (query_doc[:, None] == row_docs[None, :])
    scores = raw_scores * key_rows.shape[1] ** (-0.5) - head_slope * offset.astype(jnp.float32)
    return jnp.where(allowed, scores, masked_score)


def head_forward(query_rows, key_rows, value_rows, head_slope, row_docs, block_rows):
    starts = jnp.arange(query_rows.shape[0] // block_rows, dtype=jnp.int32) * block_rows

    def one_block(first_row):
        query_block = lax.dynamic_slice_in_dim(query_rows, first_row, block_rows)
        scores = block_scores(query_block, key_rows, first_row, head_slope, row_docs)
        row_max = jnp.max(scores, axis=-1, keepdims=True)
        exponent = jnp.exp(scores - row_max)
        row_total = jnp.sum(exponent, axis=-1, keepdims=True)
        weights = (exponent / row_total).astype(jnp.bfloat16)
        block_out = jnp.dot(weights, value_rows, preferred_element_type=jnp.float32).astype(
            jnp.bfloat16
        )
        return (block_out, (row_max + jnp.log(row_total))[:, 0])

    block_outs, log_total = lax.map(one_block, starts)
    return (block_outs.reshape(-1, value_rows.shape[1]), log_total.reshape(-1))


def head_backward(
    query_rows, key_rows, value_rows, grad_rows, log_total, head_slope, row_docs, block_rows
):
    length, head_width = key_rows.shape
    inv_root = head_width ** (-0.5)
    starts = jnp.arange(length // block_rows, dtype=jnp.int32) * block_rows

    def one_block(running, first_row):
        grad_keys, grad_values = running
        query_block = lax.dynamic_slice_in_dim(query_rows, first_row, block_rows)
        grad_block = lax.dynamic_slice_in_dim(grad_rows, first_row, block_rows)
        total_block = lax.dynamic_slice_in_dim(log_total, first_row, block_rows)
        scores = block_scores(query_block, key_rows, first_row, head_slope, row_docs)
        weights = jnp.exp(scores - total_block[:, None])
        grad_weights = lax.dot_general(
            grad_block, value_rows, (((1,), (1,)), ((), ())), preferred_element_type=jnp.float32
        )
        inner_sum = jnp.sum(weights * grad_weights, axis=-1, keepdims=True)
        grad_scores = (weights * (grad_weights - inner_sum)).astype(jnp.bfloat16)
        grad_query = jnp.dot(grad_scores, key_rows, preferred_element_type=jnp.float32) * inv_root
        grad_keys = (
            grad_keys
            + lax.dot_general(
                grad_scores,
                query_block,
                (((0,), (0,)), ((), ())),
                preferred_element_type=jnp.float32,
            )
            * inv_root
        )
        grad_values = grad_values + lax.dot_general(
            weights.astype(jnp.bfloat16),
            grad_block,
            (((0,), (0,)), ((), ())),
            preferred_element_type=jnp.float32,
        )
        return ((grad_keys, grad_values), grad_query)

    zeros_block = jnp.zeros((length, head_width), jnp.float32)
    (grad_keys, grad_values), grad_query = lax.scan(one_block, (zeros_block, zeros_block), starts)
    return (
        grad_query.reshape(length, head_width).astype(jnp.bfloat16),
        grad_keys.astype(jnp.bfloat16),
        grad_values.astype(jnp.bfloat16),
    )


def local(
    inputs,
    doc_ids,
    w_qkv,
    bias_q,
    bias_v,
    w_out,
    bias_out,
    norm1_gain,
    norm1_bias,
    norm2_gain,
    norm2_bias,
    w_up,
    bias_up,
    w_down,
    bias_down,
    cotangent,
):
    model_width = w_out.shape[0]
    tokens = inputs.shape[1]
    head_count = model_width // HEAD_DIM
    float_inputs = inputs[0].astype(jnp.float32)
    gain_one = norm1_gain.astype(jnp.float32)
    gain_two = norm2_gain.astype(jnp.float32)
    normed_in, normed_one, inv_one = layer_norm(
        float_inputs, gain_one, norm1_bias.astype(jnp.float32)
    )
    act_one = normed_in.astype(jnp.bfloat16)
    projected = jnp.dot(act_one, w_qkv, preferred_element_type=jnp.float32)
    query_rows = (projected[:, :model_width] + bias_q.astype(jnp.float32)).astype(jnp.bfloat16)
    key_rows = projected[:, model_width : 2 * model_width].astype(jnp.bfloat16)
    value_rows = (projected[:, 2 * model_width :] + bias_v.astype(jnp.float32)).astype(jnp.bfloat16)
    query_rows = query_rows.reshape(tokens, head_count, HEAD_DIM)
    key_rows = key_rows.reshape(tokens, head_count, HEAD_DIM)
    value_rows = value_rows.reshape(tokens, head_count, HEAD_DIM)
    whole_q, whole_k, whole_v = (
        lax.all_to_all(query_rows, "seq", split_axis=1, concat_axis=0, tiled=True),
        lax.all_to_all(key_rows, "seq", split_axis=1, concat_axis=0, tiled=True),
        lax.all_to_all(value_rows, "seq", split_axis=1, concat_axis=0, tiled=True),
    )
    row_docs = lax.all_gather(doc_ids, "seq", axis=1, tiled=True)[0]
    local_heads = whole_q.shape[1]
    length = whole_q.shape[0]
    block_rows = min(512, length)
    first_head = lax.axis_index("seq") * local_heads
    slopes = jnp.exp2(
        -(first_head + 1 + jnp.arange(local_heads, dtype=jnp.int32)).astype(jnp.float32)
    )
    head_q = jnp.moveaxis(whole_q, 1, 0)
    head_k = jnp.moveaxis(whole_k, 1, 0)
    head_v = jnp.moveaxis(whole_v, 1, 0)

    def forward_head(operands):
        return head_forward(
            operands[0], operands[1], operands[2], operands[3], row_docs, block_rows
        )

    head_outs, head_totals = lax.map(forward_head, (head_q, head_k, head_v, slopes))
    mixed_heads = lax.all_to_all(
        jnp.moveaxis(head_outs, 0, 1), "seq", split_axis=0, concat_axis=1, tiled=True
    )
    mixed_flat = mixed_heads.reshape(tokens, model_width)
    second = (
        float_inputs
        + jnp.dot(mixed_flat, w_out, preferred_element_type=jnp.float32)
        + bias_out.astype(jnp.float32)
    )
    normed_mid, normed_two, inv_two = layer_norm(second, gain_two, norm2_bias.astype(jnp.float32))
    act_two = normed_mid.astype(jnp.bfloat16)
    pre_act = jnp.dot(act_two, w_up, preferred_element_type=jnp.float32) + bias_up.astype(
        jnp.float32
    )
    activated, act_pullback = jax.vjp(smooth_act, pre_act)
    hidden = activated.astype(jnp.bfloat16)
    result = (
        second
        + jnp.dot(hidden, w_down, preferred_element_type=jnp.float32)
        + bias_down.astype(jnp.float32)
    )
    grad_out = cotangent[0].astype(jnp.float32)
    grad_low = grad_out.astype(jnp.bfloat16)
    g_bias_down = jnp.sum(grad_low.astype(jnp.float32), axis=0)
    g_w_down = lax.dot_general(
        hidden, grad_low, (((0,), (0,)), ((), ())), preferred_element_type=jnp.float32
    )
    grad_hidden = lax.dot_general(
        grad_low, w_down, (((1,), (1,)), ((), ())), preferred_element_type=jnp.float32
    )
    grad_pre = act_pullback(grad_hidden)[0].astype(jnp.bfloat16)
    g_bias_up = jnp.sum(grad_pre.astype(jnp.float32), axis=0)
    g_w_up = lax.dot_general(
        act_two, grad_pre, (((0,), (0,)), ((), ())), preferred_element_type=jnp.float32
    )
    grad_norm_two = lax.dot_general(
        grad_pre, w_up, (((1,), (1,)), ((), ())), preferred_element_type=jnp.float32
    )
    grad_mid, g_gain_two, g_shift_two = norm_back(grad_norm_two, normed_two, inv_two, gain_two)
    grad_second = grad_out + grad_mid
    grad_branch = grad_second.astype(jnp.bfloat16)
    g_bias_out = jnp.sum(grad_branch.astype(jnp.float32), axis=0)
    g_w_out = lax.dot_general(
        mixed_flat, grad_branch, (((0,), (0,)), ((), ())), preferred_element_type=jnp.float32
    )
    grad_mixed = lax.dot_general(
        grad_branch, w_out, (((1,), (1,)), ((), ())), preferred_element_type=jnp.float32
    ).astype(jnp.bfloat16)
    grad_whole = lax.all_to_all(
        grad_mixed.reshape(tokens, head_count, HEAD_DIM),
        "seq",
        split_axis=1,
        concat_axis=0,
        tiled=True,
    )
    grad_heads = jnp.moveaxis(grad_whole, 1, 0)

    def backward_head(operands):
        return head_backward(
            operands[0],
            operands[1],
            operands[2],
            operands[3],
            operands[4],
            operands[5],
            row_docs,
            block_rows,
        )

    grad_q, grad_k, grad_v = lax.map(
        backward_head, (head_q, head_k, head_v, grad_heads, head_totals, slopes)
    )
    back_q, back_k, back_v = (
        lax.all_to_all(jnp.moveaxis(grad_q, 0, 1), "seq", split_axis=0, concat_axis=1, tiled=True),
        lax.all_to_all(jnp.moveaxis(grad_k, 0, 1), "seq", split_axis=0, concat_axis=1, tiled=True),
        lax.all_to_all(jnp.moveaxis(grad_v, 0, 1), "seq", split_axis=0, concat_axis=1, tiled=True),
    )
    back_q = back_q.reshape(tokens, model_width)
    back_k = back_k.reshape(tokens, model_width)
    back_v = back_v.reshape(tokens, model_width)
    g_bias_q = jnp.sum(back_q.astype(jnp.float32), axis=0)
    g_bias_v = jnp.sum(back_v.astype(jnp.float32), axis=0)
    grad_proj = jnp.concatenate([back_q, back_k, back_v], axis=1)
    g_w_qkv = lax.dot_general(
        act_one, grad_proj, (((0,), (0,)), ((), ())), preferred_element_type=jnp.float32
    )
    grad_norm_one = lax.dot_general(
        grad_proj, w_qkv, (((1,), (1,)), ((), ())), preferred_element_type=jnp.float32
    )
    grad_first, g_gain_one, g_shift_one = norm_back(grad_norm_one, normed_one, inv_one, gain_one)
    grad_inputs = grad_second + grad_first
    matrices = (g_w_qkv, g_w_out, g_w_up, g_w_down)
    partial_sums = (
        lax.psum_scatter(
            matrices[0].astype(jnp.bfloat16), "dp", scatter_dimension=0, tiled=True
        ).astype(jnp.float32),
        lax.psum_scatter(
            matrices[1].astype(jnp.bfloat16), "dp", scatter_dimension=0, tiled=True
        ).astype(jnp.float32),
        lax.psum_scatter(
            matrices[2].astype(jnp.bfloat16), "dp", scatter_dimension=0, tiled=True
        ).astype(jnp.float32),
        lax.psum_scatter(
            matrices[3].astype(jnp.bfloat16), "dp", scatter_dimension=0, tiled=True
        ).astype(jnp.float32),
    )
    summed = (
        lax.psum_scatter(
            partial_sums[0].astype(jnp.bfloat16), "seq", scatter_dimension=1, tiled=True
        ).astype(jnp.float32),
        lax.psum_scatter(
            partial_sums[1].astype(jnp.bfloat16), "seq", scatter_dimension=1, tiled=True
        ).astype(jnp.float32),
        lax.psum_scatter(
            partial_sums[2].astype(jnp.bfloat16), "seq", scatter_dimension=1, tiled=True
        ).astype(jnp.float32),
        lax.psum_scatter(
            partial_sums[3].astype(jnp.bfloat16), "seq", scatter_dimension=1, tiled=True
        ).astype(jnp.float32),
    )
    vectors = lax.psum(
        (
            g_bias_q,
            g_bias_v,
            g_bias_out,
            g_gain_one,
            g_shift_one,
            g_gain_two,
            g_shift_two,
            g_bias_up,
            g_bias_down,
        ),
        ("dp", "seq"),
    )
    return (
        result.astype(jnp.bfloat16)[None],
        grad_inputs[None],
        summed[0],
        vectors[0],
        vectors[1],
        summed[1],
        vectors[2],
        vectors[3],
        vectors[4],
        vectors[5],
        vectors[6],
        summed[2],
        vectors[7],
        summed[3],
        vectors[8],
    )


def solution(mesh):
    in_specs = (
        P("dp", "seq", None),
        P("dp", "seq"),
        P(),
        P(),
        P(),
        P(),
        P(),
        P(),
        P(),
        P(),
        P(),
        P(),
        P(),
        P(),
        P(),
        P("dp", "seq", None),
    )
    out_specs = (
        P("dp", "seq", None),
        P("dp", "seq", None),
        P("dp", "seq"),
        P(),
        P(),
        P("dp", "seq"),
        P(),
        P(),
        P(),
        P(),
        P(),
        P("dp", "seq"),
        P(),
        P("dp", "seq"),
        P(),
    )
    sizes = (mesh.shape["dp"], mesh.shape["seq"])
    chosen = fast_local if sizes == (16, 2) else local
    return jax.shard_map(chosen, mesh=mesh, in_specs=in_specs, out_specs=out_specs, check_vma=False)
```

```python
import functools

import jax
import jax.numpy as jnp
import numpy as np
from jax import lax
from jax.experimental import pallas as pl
from jax.experimental.pallas import tpu as pltpu
from jax.sharding import PartitionSpec as P

HEAD_DIM = 128
MESH = pl.DeviceIdType.MESH
F32 = jnp.float32
BF16 = jnp.bfloat16
LOG2E = 1.4426950408889634
FAR = 1e30
GELU_C = 0.7978845608028654
GELU_A = 0.044715

norm_eps = 1e-05
masked_score = -1e30

NT = (((1,), (1,)), ((), ()))
TN = (((0,), (0,)), ((), ()))


def dot(a, b):
    return jnp.dot(a, b, preferred_element_type=F32)


def dot_nt(a, b):
    return lax.dot_general(a, b, NT, preferred_element_type=F32)


def dot_tn(a, b):
    return lax.dot_general(a, b, TN, preferred_element_type=F32)


def coords():
    dp = lax.axis_index("dp")
    return {
        "c": dp % 2,
        "x": (dp // 2) % 2,
        "a": (dp // 4) % 2,
        "b": dp // 8,
        "y": lax.axis_index("seq"),
    }


def partner(kind):
    dp = lax.axis_index("dp")
    if kind == "y":
        return {"seq": 1 - lax.axis_index("seq")}
    step = {"c": 1, "x": 2, "a": 4, "b": 8}[kind]
    bit = (dp // step) % 2
    return {"dp": dp + step - 2 * step * bit}


def greet(kinds):
    barrier = pltpu.get_barrier_semaphore()
    for kind in kinds:
        pl.semaphore_signal(barrier, inc=1, device_id=partner(kind), device_id_type=MESH)
    pl.semaphore_wait(barrier, len(kinds))


ORDERS = (("x", "a", "y", "b"), ("y", "a", "x", "b"))


ALONG_X = (18, 20, 22)


def order_of(chunk, half):
    return ORDERS[0 if isinstance(chunk, int) and chunk in ALONG_X else half]


def block_index(chunk, half, place):
    index = half * 16
    for kind, weight in zip(order_of(chunk, half), (8, 4, 2, 1)):
        index = index + place[kind] * weight
    return index


def dp_bits(dp):
    return {"c": dp % 2, "x": (dp // 2) % 2, "a": (dp // 4) % 2, "b": dp // 8}


class Scatter:
    def __init__(self, held, arrivals, send_sem, recv_sem):
        self.held, self.arrivals = held, arrivals
        self.send_sem, self.recv_sem = send_sem, recv_sem
        self.me = coords()

    def offset(self, chunk, half, stage, other):
        index = half * 16
        for k, weight in zip(range(stage + 1), (8, 4, 2, 1)):
            bit = self.me[order_of(chunk, half)[k]]
            if other and k == stage:
                bit = 1 - bit
            index = index + bit * weight
        return index

    def copy(self, chunk, stage, half):
        size = 8 >> stage
        return pltpu.make_async_remote_copy(
            src_ref=self.held.at[chunk, pl.ds(self.offset(chunk, half, stage, True), size)],
            dst_ref=self.arrivals[stage].at[chunk, half],
            send_sem=self.send_sem.at[stage],
            recv_sem=self.recv_sem.at[stage, chunk],
            device_id=partner(order_of(chunk, half)[stage]),
            device_id_type=MESH,
        )

    def start(self, chunk, stage):
        for half in range(2):
            self.copy(chunk, stage, half).start()

    def whole(self, stage, ref, at):
        return pltpu.make_async_remote_copy(
            src_ref=ref, dst_ref=ref, send_sem=self.send_sem.at[stage], recv_sem=self.recv_sem.at[stage, at],
            device_id=partner("x"), device_id_type=MESH,
        )

    def sent(self):
        for stage in range(4):
            self.whole(stage, self.arrivals[stage], 0).wait_send()

    def finish(self, chunk, stage):
        size = 8 >> stage
        self.whole(stage, self.arrivals[stage].at[chunk], chunk).wait_recv()
        for half in range(2):
            mine = pl.ds(self.offset(chunk, half, stage, False), size)
            self.held[chunk, mine] = self.held[chunk, mine] + self.arrivals[stage][chunk, half]

    def result(self, chunk, half):
        return self.held[chunk, self.offset(chunk, half, 3, False)]


def arrival_shapes(chunks):
    return [pltpu.VMEM((chunks, 2, 8 >> k, 32, 256), BF16) for k in range(4)]


def when(cond, fn):
    if isinstance(cond, (bool, np.bool_)):
        if cond:
            fn()
    else:
        pl.when(cond)(fn)


def inside(value, low, high):
    if isinstance(value, int):
        return low <= value < high
    return (value >= low) & (value < high)


RING = 3
AHEAD = 2


def row_of(ref):
    return ref[...].astype(F32).reshape(1, -1)


def layer_kernel(
    halo, x_hbm, doc_hbm, slope_hbm, bq_hbm, bv_hbm, bo_hbm, g1_hbm, s1_hbm, g2_hbm, s2_hbm, bup_hbm, bdown_hbm,
    cot_hbm, wqkv_hbm, wout_hbm, wup_hbm, wdown_hbm,
    out_hbm, gin_hbm, gup_hbm, gdown_hbm, gout_hbm, gqkv_hbm, vec_hbm,
    gup, gdown, gout, gqkv, vec,
    x_ref, doc_ref, slope_ref, bq_ref, bv_ref, bo_ref, g1_ref, s1_ref, g2_ref, s2_ref, bup_ref, bdown_ref,
    qkv, act1t, ot, dist, doch, x2, cot, act2, act2t, hid_t, dpre, dn2, dn1, dnh, dqkv, wu, wd, bias, bup,
    grad, held, r1, r2, r3, r4, vin,
    rsem, isem, qsem, osem, wsem, csem, cs, cr, ss, rs, hs, hr, vs, vr, esem,
):
    tokens, width = x_ref.shape
    heads = width // HEAD_DIM
    ff = wup_hbm.shape[1]
    half_ff = ff // 2
    steps = half_ff // 256
    seq = lax.axis_index("seq")
    me = coords()
    first_down, first_out, first_qkv, chunks = steps, 2 * steps, 2 * steps + 2, 2 * steps + 8
    scale = HEAD_DIM**-0.5

    act1 = dqkv.at[:, pl.ds(0, width)]
    o_s = dqkv.at[pl.ds(halo, tokens), pl.ds(width, width)]
    xh = dqkv.at[pl.ds(0, halo), pl.ds(2 * width, width)]
    wout_low = dqkv.at[pl.ds(halo, 512), pl.ds(2 * width, width)]

    dn_come = qkv.at[pl.ds(0, halo), pl.ds(0, width)]
    dn_send = qkv.at[pl.ds(0, halo), pl.ds(width, width)]

    def wqkv_part(j):
        return wu.at[j] if j < 2 else hid_t.at[pl.ds((j - 2) * width, width)]

    qloads = [
        pltpu.make_async_copy(wqkv_hbm.at[:, pl.ds(j * 512, 512)], wqkv_part(j), qsem.at[j]) for j in range(6)
    ]
    oloads = [
        pltpu.make_async_copy(wout_hbm.at[pl.ds(0, 512)], wout_low, osem.at[0]),
        pltpu.make_async_copy(wout_hbm.at[pl.ds(512, 512)], wd.at[1], osem.at[1]),
    ]
    cload = pltpu.make_async_copy(cot_hbm, cot, csem)
    iloads = [
        pltpu.make_async_copy(src, dst, isem.at[i])
        for i, (src, dst) in enumerate(
            (
                (x_hbm, x_ref), (g1_hbm, g1_ref), (s1_hbm, s1_ref), (bq_hbm, bq_ref), (bv_hbm, bv_ref),
                (doc_hbm, doc_ref), (slope_hbm, slope_ref), (bo_hbm, bo_ref), (g2_hbm, g2_ref), (s2_hbm, s2_ref),
                (bup_hbm, bup_ref), (bdown_hbm, bdown_ref),
            )
        )
    ]
    for cp in iloads + qloads + oloads + [cload]:
        cp.start()
    greet(("c", "x", "a", "b", "y"))
    part_rows = halo // 2
    send_x = [
        pltpu.make_async_remote_copy(
            src_ref=x_hbm.at[pl.ds(tokens - halo + (1 - i) * part_rows, part_rows)],
            dst_ref=xh.at[pl.ds((1 - i) * part_rows, part_rows)], send_sem=hs.at[i], recv_sem=hr.at[i],
            device_id=partner("y"), device_id_type=MESH,
        )
        for i in range(2)
    ]
    send_doc = pltpu.make_async_remote_copy(
        src_ref=doc_hbm, dst_ref=doch, send_sem=hs.at[3], recv_sem=hr.at[3],
        device_id=partner("y"), device_id_type=MESH,
    )

    @pl.when(seq == 0)
    def _():
        send_doc.start()
        for cp in send_x:
            cp.start()

    for cp in iloads:
        cp.wait()

    def weights(f, slot):
        col = pl.multiple_of(f * 256, 256)
        return [
            pltpu.make_async_copy(wup_hbm.at[:, pl.ds(col, 256)], wu.at[slot, :, pl.ds(0, 256)], wsem.at[slot, 0]),
            pltpu.make_async_copy(
                wup_hbm.at[:, pl.ds(half_ff + col, 256)], wu.at[slot, :, pl.ds(256, 256)], wsem.at[slot, 1]
            ),
            pltpu.make_async_copy(wdown_hbm.at[pl.ds(col, 256)], wd.at[slot, pl.ds(0, 256)], wsem.at[slot, 2]),
            pltpu.make_async_copy(
                wdown_hbm.at[pl.ds(half_ff + col, 256)], wd.at[slot, pl.ds(256, 256)], wsem.at[slot, 3]
            ),
        ]

    scatter = Scatter(held, (r1, r2, r3, r4), ss, rs)

    def core_copy(n):
        return pltpu.make_async_remote_copy(
            src_ref=grad.at[n % RING, 1 - me["c"]], dst_ref=held.at[n], send_sem=cs.at[n % RING], recv_sem=cr.at[n],
            device_id=partner("c"), device_id_type=MESH,
        )

    def join(n):
        core_copy(n).wait()
        held[n] = held[n] + grad[n % RING, me["c"]]

    def put(n, yy, m, tile):
        for q in range(4):
            place = dp_bits(m * 4 + q)
            place["y"] = yy
            for h in range(2):
                r0 = q * 64 + h * 32
                grad[n % RING, place["c"], block_index(n, h, place)] = tile[r0 : r0 + 32].astype(BF16)

    def store(n):
        for h in range(2):
            block = scatter.result(n, h)

            def up():
                gup[h * 32 : h * 32 + 32, pl.ds(pl.multiple_of(n * 256, 256), 256)] = block

            def down():
                i = n - first_down
                row = pl.multiple_of((i % 4) * 64 + h * 32, 32)
                gdown[pl.ds(row, 32), pl.ds(pl.multiple_of((i // 4) * 256, 256), 256)] = block

            def outp():
                gout[h * 32 : h * 32 + 32, pl.ds(pl.multiple_of((n - first_out) * 256, 256), 256)] = block

            def proj():
                gqkv[h * 32 : h * 32 + 32, pl.ds(pl.multiple_of((n - first_qkv) * 256, 256), 256)] = block

            when(inside(n, 0, first_down), up)
            when(inside(n, first_down, first_out), down)
            when(inside(n, first_out, first_qkv), outp)
            when(inside(n, first_qkv, chunks), proj)

    def service(t, ahead=True):
        if ahead:
            when(inside(t + AHEAD, 0, chunks), lambda: scatter.start(t + AHEAD, 0))

        def last():
            scatter.finish(t - 6, 3)
            store(t - 6)

        when(inside(t - 6, 0, chunks), last)
        for stage in (2, 1, 0):
            n = t - 2 * stage

            def step(stage=stage, n=n):
                scatter.finish(n, stage)
                scatter.start(n, stage + 1)

            when(inside(n, 0, chunks), step)

    gain1, shift1 = row_of(g1_ref), row_of(s1_ref)
    gain2, shift2 = row_of(g2_ref), row_of(s2_ref)

    def norm(v, gain, shift):
        center = v - jnp.mean(v, axis=-1, keepdims=True)
        inv = lax.rsqrt(jnp.mean(center * center, axis=-1, keepdims=True) + norm_eps)
        return center * inv * gain + shift

    bias[:, 0:width] = row_of(bq_ref)
    bias[:, width : 2 * width] = jnp.zeros((1, width), F32)
    bias[:, 2 * width :] = row_of(bv_ref)
    bup[...] = row_of(bup_ref)

    def norm_rows(m):
        for r in range(2 * m, 2 * m + 2):
            v = norm(x_ref[r * 128 : (r + 1) * 128].astype(F32), gain1, shift1).astype(BF16)
            act1[halo + r * 128 : halo + (r + 1) * 128] = v
            act1t[:, halo + r * 128 : halo + (r + 1) * 128] = v.T

    for m in range(tokens // 256):
        norm_rows(m)
    for j in range(6):
        qloads[j].wait()
        cols = slice(j * 512, (j + 1) * 512)
        for m in range(tokens // 256):
            rows = slice(halo + m * 256, halo + (m + 1) * 256)
            qkv[rows, cols] = (dot(act1[rows], wqkv_part(j)[...]) + bias[:, cols]).astype(BF16)
    for cp in weights(0, 0):
        cp.start()

    own_doc = doc_ref[...].astype(F32)
    own_cols = jnp.transpose(jnp.broadcast_to(own_doc, (128, tokens)))[:, 0:1]

    def distances(block, key_docs):
        keys = key_docs[block * 256 : block * 256 + 512]
        queries = own_doc[:, block * 256 : block * 256 + 256]
        key_pos = lax.broadcasted_iota(jnp.int32, (512, 256), 0)
        query_pos = lax.broadcasted_iota(jnp.int32, (512, 256), 1) + 256
        gap = query_pos - key_pos
        allowed = (gap >= 0) & (keys == queries)
        dist[block] = jnp.where(allowed, gap.astype(F32), FAR)

    def attend(block, which):
        def some_heads(i, carry):
            for u in range(FWD_HEADS):
                h = i * FWD_HEADS + u
                c0 = pl.multiple_of(h * HEAD_DIM, HEAD_DIM)
                slope = slope_ref[pl.ds(h, 1), 0:1]
                for t in which:
                    row = block * 256 + t * 128
                    q = qkv[halo + row : halo + row + 128, pl.ds(c0, HEAD_DIM)]
                    k = qkv[row : row + 384, pl.ds(width + c0, HEAD_DIM)]
                    v = qkv[row : row + 384, pl.ds(2 * width + c0, HEAD_DIM)]
                    far = dist[block, t * 128 : t * 128 + 384, t * 128 : t * 128 + 128]
                    s = dot_nt(k, q) * (LOG2E * scale) - slope * far
                    e = jnp.exp2(s - jnp.max(s, axis=0, keepdims=True))
                    p = (e * (1.0 / jnp.sum(e, axis=0, keepdims=True))).astype(BF16)
                    o_t = dot_tn(v, p)
                    ot[pl.ds(c0, HEAD_DIM), row : row + 128] = o_t.astype(BF16)
                    o_s[row : row + 128, pl.ds(c0, HEAD_DIM)] = o_t.T.astype(BF16)
            return carry

        lax.fori_loop(0, heads // FWD_HEADS, some_heads, 0)

    def project(block, which):
        for r in which:
            rows = slice(block * 256 + r * 128, block * 256 + (r + 1) * 128)
            second = (
                x_ref[rows].astype(F32) + dot(o_s[rows, 0:512], wout_low[...]) + dot(o_s[rows, 512:1024], wd[1])
            ) + row_of(bo_ref)
            x2[rows] = second
            v = norm(second, gain2, shift2).astype(BF16)
            act2[rows] = v
            act2t[:, rows] = v.T

    distances(1, jnp.concatenate([jnp.full((halo, 1), -1.0, F32), own_cols], axis=0))
    attend(1, (0, 1))
    for cp in oloads:
        cp.wait()
    project(1, (0, 1))

    @pl.when(seq == 0)
    def _():
        send_doc.wait_send()
        for cp in send_x:
            cp.wait_send()
        doch[...] = jnp.full(doch.shape, -1, jnp.int32)
        act1t[:, 0:halo] = jnp.zeros((width, halo), BF16)
        qkv[0:halo, width:] = jnp.zeros((halo, 2 * width), BF16)

    @pl.when(seq == 1)
    def _():
        send_doc.wait_recv()

    halo_doc = doch[...].astype(F32)[:, tokens - halo :]
    halo_cols = jnp.transpose(jnp.broadcast_to(halo_doc, (128, halo)))[:, 0:1]
    distances(0, jnp.concatenate([halo_cols, own_cols], axis=0))
    for i in range(2):
        rows = slice((1 - i) * part_rows, (2 - i) * part_rows)

        @pl.when(seq == 1)
        def _(i=i, rows=rows):
            send_x[i].wait_recv()
            v = norm(xh[rows].astype(F32), gain1, shift1).astype(BF16)
            act1[rows] = v
            act1t[:, rows] = v.T
            for j in range(2, 6):
                cols = slice(j * 512, (j + 1) * 512)
                qkv[rows, cols] = (dot(act1[rows], wqkv_part(j)[...]) + bias[:, cols]).astype(BF16)

        attend(0, (1 - i,))
        project(0, (1 - i,))

    cload.wait()
    vec[...] = jnp.zeros(vec.shape, F32)
    vec[7:8] = jnp.sum(cot[...].astype(F32), axis=0, keepdims=True)
    dn2[...] = jnp.zeros(dn2.shape, F32)

    def ff_step(f, carry):
        slot = f % 2
        for cp in weights(f, slot):
            cp.wait()

        @pl.when(f + 1 < steps)
        def _():
            for cp in weights(f + 1, 1 - slot):
                cp.start()

        for yy in range(2):
            if yy == 1:

                @pl.when(f >= 1)
                def _():
                    join(f - 1)
                    scatter.start(f - 1, 0)

            cols = slice(yy * 256, (yy + 1) * 256)
            first = pl.multiple_of(yy * half_ff + f * 256, 256)
            shift = bup[:, pl.ds(first, 256)]
            sums = jnp.zeros((1, 256), F32)
            for m in range(tokens // 256):
                rows = slice(m * 256, (m + 1) * 256)
                u = dot(act2[rows], wu[slot, :, cols]) + shift
                dh = dot_nt(cot[rows], wd[slot, cols])
                uu = u * u
                gate = 0.5 * jnp.tanh(u * (GELU_C + GELU_C * GELU_A * uu)) + 0.5
                act = u * gate
                hv = act.astype(BF16)
                slope = gate + act * (1.0 - gate) * (2.0 * GELU_C + 6.0 * GELU_C * GELU_A * uu)
                dv = (dh * slope).astype(BF16)
                dpre[rows, cols] = dv
                hid_t[pl.ds(first, 256), rows] = hv.T
                sums = sums + jnp.sum(dv.astype(F32), axis=0, keepdims=True)
            row = yy * (half_ff // width) + f // (width // 256)
            vec[pl.ds(8 + row, 1), pl.ds(pl.multiple_of((f % (width // 256)) * 256, 256), 256)] = sums

        for yy in range(2):
            cols = slice(yy * 256, (yy + 1) * 256)
            for m in range(width // 256):
                put(f, yy, m, dot(act2t[m * 256 : (m + 1) * 256], dpre[:, cols]))
        core_copy(f).start()
        for m in range(tokens // 256):
            rows = slice(m * 256, (m + 1) * 256)
            dn2[rows] += dot_nt(dpre[rows], wu[slot])
        service(f - 2, ahead=False)
        return carry

    lax.fori_loop(0, steps, ff_step, 0)
    join(steps - 1)
    scatter.start(steps - 1, 0)
    oloads = [pltpu.make_async_copy(wout_hbm.at[pl.ds(i * 512, 512)], wd.at[i], osem.at[i]) for i in range(2)]
    order = (2, 3, 4, 5, 0, 1)

    def qload(i):
        return pltpu.make_async_copy(wqkv_hbm.at[:, pl.ds(order[i] * 512, 512)], wu.at[i % 2], qsem.at[i % 2])

    for cp in oloads + [qload(0), qload(1)]:
        cp.start()

    def down_step(i, carry):
        n = first_down + i
        for yy in range(2):
            right = cot[:, pl.ds(pl.multiple_of(yy * 512 + (i // 4) * 256, 256), 256)]
            for m in range(4):
                left = jnp.concatenate(
                    [
                        hid_t[pl.ds(pl.multiple_of((m * 4 + q) * 256 + (i % 4) * 64, 64), 64)]
                        for q in range(4)
                    ],
                    axis=0,
                )
                put(n, yy, m, dot(left, right))
        core_copy(n).start()

        @pl.when(i >= 1)
        def _():
            join(n - 1)

        for at, t in ((2, steps - 2), (5, steps - 1), (7, steps)):

            @pl.when(i == at)
            def _(t=t):
                service(t)

        return carry

    lax.fori_loop(0, steps, down_step, 0)
    join(first_out - 1)

    def norm_two(r, carry):
        rows = pl.ds(pl.multiple_of(r * 64, 64), 64)
        v = x2[rows]
        center = v - jnp.mean(v, axis=-1, keepdims=True)
        inv = lax.rsqrt(jnp.mean(center * center, axis=-1, keepdims=True) + norm_eps)
        normed = center * inv
        dn = dn2[rows]
        e = dn * gain2
        vec[5:6] += jnp.sum(dn * normed, axis=0, keepdims=True)
        vec[6:7] += jnp.sum(dn, axis=0, keepdims=True)
        dx = cot[rows].astype(F32) + inv * (
            e - jnp.mean(e, axis=-1, keepdims=True) - normed * jnp.mean(e * normed, axis=-1, keepdims=True)
        )
        dn2[rows] = dx
        low = dx.astype(BF16)
        cot[rows] = low
        vec[2:3] += jnp.sum(low.astype(F32), axis=0, keepdims=True)
        return carry

    lax.fori_loop(0, tokens // 64, norm_two, 0)
    dx2, ab, do = dn2, cot, act2
    service(steps + 1)

    for j in range(2):
        for yy in range(2):
            c0 = yy * 512 + j * 256
            for m in range(width // 256):
                put(first_out + j, yy, m, dot(ot[m * 256 : (m + 1) * 256], ab[:, c0 : c0 + 256]))
        core_copy(first_out + j).start()
    service(steps + 2)
    for cp in oloads:
        cp.wait()
    for m in range(tokens // 256):
        rows = slice(m * 256, (m + 1) * 256)
        for i in range(2):
            do[rows, i * 512 : (i + 1) * 512] = dot_nt(ab[rows], wd[i]).astype(BF16)

    def dload(i):
        return pltpu.make_async_copy(wdown_hbm.at[pl.ds(i * 512, 512)], wd.at[i % 2], osem.at[i % 2])

    dload(0).start()
    dload(1).start()
    join(first_out)
    join(first_out + 1)
    service(steps + 3)

    dqkv[0:halo, 0:width] = jnp.zeros((halo, width), BF16)
    act2t[...] = jnp.zeros(act2t.shape, BF16)

    def head_back(h):
        c0 = pl.multiple_of(h * HEAD_DIM, HEAD_DIM)
        slope = slope_ref[pl.ds(h, 1), 0:1]
        parts = []
        for block in range(2):
            rows = slice(halo + block * 256, halo + (block + 1) * 256)
            krows = slice(block * 256, block * 256 + 512)
            q = qkv[rows, pl.ds(c0, HEAD_DIM)]
            k = qkv[krows, pl.ds(width + c0, HEAD_DIM)]
            g = do[block * 256 : (block + 1) * 256, pl.ds(c0, HEAD_DIM)]
            for t in range(2):
                row = block * 256 + t * 128
                keys, cols = slice(t * 128, t * 128 + 384), slice(t * 128, t * 128 + 128)
                qs = qkv[halo + row : halo + row + 128, pl.ds(c0, HEAD_DIM)]
                ks = qkv[row : row + 384, pl.ds(width + c0, HEAD_DIM)]
                vs = qkv[row : row + 384, pl.ds(2 * width + c0, HEAD_DIM)]
                s = dot_nt(ks, qs) * (LOG2E * scale) - slope * dist[block, keys, cols]
                e = jnp.exp2(s - jnp.max(s, axis=0, keepdims=True))
                p = e * (1.0 / jnp.sum(e, axis=0, keepdims=True))
                dp = dot_nt(vs, do[row : row + 128, pl.ds(c0, HEAD_DIM)])
                delta = jnp.sum(p * dp, axis=0, keepdims=True)
                keys = slice(block * 512 + t * 128, block * 512 + t * 128 + 384)
                act2t[keys, cols] = p.astype(BF16)
                act2t[keys, 256 + t * 128 : 384 + t * 128] = (p * (dp - delta)).astype(BF16)
            both = slice(block * 512, (block + 1) * 512)
            pb, ds = act2t[both, 0:256], act2t[both, 256:512]
            dqkv[rows, pl.ds(c0, HEAD_DIM)] = (dot_tn(k, ds) * scale).T.astype(BF16)
            parts.append((dot(ds, q) * scale, dot(pb, g)))
        for which in range(2):
            cols = pl.ds((1 + which) * width + c0, HEAD_DIM)
            first, second = parts[0][which], parts[1][which]
            dqkv[0:256, cols] = first[0:256].astype(BF16)
            dqkv[256:512, cols] = (first[256:512] + second[0:256]).astype(BF16)
            dqkv[512:768, cols] = second[256:512].astype(BF16)

    def heads_back(i, carry):
        for u in range(2):
            head_back(i * 2 + u)
        service(steps + 4 + i)
        return carry

    lax.fori_loop(0, heads // 2, heads_back, 0)
    vec[0:1] = jnp.sum(dqkv[halo:, 0:width].astype(F32), axis=0, keepdims=True)
    vec[1:2] = jnp.sum(dqkv[:, 2 * width :].astype(F32), axis=0, keepdims=True)

    state = {"t": steps + 4 + heads // 2}

    def serve():
        if state["t"] < chunks + 6:
            service(state["t"])
            state["t"] += 1

    back = pltpu.make_async_remote_copy(
        src_ref=dn_send, dst_ref=dn_come, send_sem=hs.at[2], recv_sem=hr.at[2],
        device_id=partner("y"), device_id_type=MESH,
    )

    def dn_part(i):
        cols = slice(order[i] * 512, (order[i] + 1) * 512)
        qload(i).wait()
        if i < 4:
            part = dot_nt(dqkv[0:halo, cols], wu[i % 2])
            if i == 0:
                dnh[...] = part
            elif i < 3:
                dnh[...] += part
            else:
                dn_send[...] = (dnh[...] + part).astype(BF16)
        for m in range(tokens // 256):
            rows = slice(m * 256, (m + 1) * 256)
            part = dot_nt(dqkv[halo + m * 256 : halo + (m + 1) * 256, cols], wu[i % 2])
            if i == 0:
                dn1[rows] = part
            else:
                dn1[rows] += part
        if i + 2 < 6:
            qload(i + 2).start()

    for j in range(6):
        n = first_qkv + j
        for yy in range(2):
            c0 = yy * (3 * width // 2) + j * 256
            for m in range(width // 256):
                put(n, yy, m, dot(act1t[m * 256 : (m + 1) * 256], dqkv[:, c0 : c0 + 256]))
        core_copy(n).start()
        if j >= 1:
            join(n - 1)
        if j in SERVE_AT:
            serve()
        if j == BACK_AT:
            for i in range(4):
                dn_part(i)

            @pl.when(seq == 1)
            def _():
                back.start()

            serve()
    join(chunks - 1)
    for i in (4, 5):
        dn_part(i)
    serve()

    def out_part(i):
        dload(i).wait()
        for m in range(tokens // 256):
            rows = slice(m * 256, (m + 1) * 256)
            part = dot_tn(hid_t[i * 512 : (i + 1) * 512, rows], wd[i % 2])
            if i == 0:
                part = part + row_of(bdown_ref)
            if i < 7:
                x2[rows] += part
            else:
                act2[rows] = (x2[rows] + part).astype(BF16)
        if i + 2 < 8:
            dload(i + 2).start()

    for i in range(OUT_SPLIT[0]):
        out_part(i)
    for _ in range(N1_AFTER):
        serve()

    @pl.when(seq == 1)
    def _():
        back.wait_send()

    @pl.when(seq == 0)
    def _():
        back.wait_recv()
        dn1[tokens - halo :] += dn_come[...].astype(F32)

    def norm_one(r, carry):
        rows = pl.ds(pl.multiple_of(r * 64, 64), 64)
        v = x_ref[rows].astype(F32)
        center = v - jnp.mean(v, axis=-1, keepdims=True)
        inv = lax.rsqrt(jnp.mean(center * center, axis=-1, keepdims=True) + norm_eps)
        normed = center * inv
        dn = dn1[rows]
        e = dn * gain1
        vec[3:4] += jnp.sum(dn * normed, axis=0, keepdims=True)
        vec[4:5] += jnp.sum(dn, axis=0, keepdims=True)
        dn1[rows] = dx2[rows] + inv * (
            e - jnp.mean(e, axis=-1, keepdims=True) - normed * jnp.mean(e * normed, axis=-1, keepdims=True)
        )
        return carry

    lax.fori_loop(0, tokens // 64, norm_one, 0)
    save_gin = pltpu.make_async_copy(dn1, gin_hbm, esem.at[0])
    save_gin.start()

    kinds = ("c", "x", "y", "a", "b")

    def vec_copy(i):
        return pltpu.make_async_remote_copy(
            src_ref=vin.at[i, 0], dst_ref=vin.at[i, 1], send_sem=vs.at[i], recv_sem=vr.at[i],
            device_id=partner(kinds[i]), device_id_type=MESH,
        )

    vin[0, 0] = vec[...]
    vec_copy(0).start()
    save_out = pltpu.make_async_copy(act2, out_hbm, esem.at[1])
    for i in range(5):
        for _ in range(VEC_SERVES[i]):
            serve()
        if i == 0:
            for k in range(*OUT_SPLIT):
                out_part(k)
        if i == 1:
            for k in range(OUT_SPLIT[1], 8):
                out_part(k)
            save_out.start()
        vec_copy(i).wait()
        total = vin[i, 0] + vin[i, 1]
        if i < 4:
            vin[i + 1, 0] = total
            vec_copy(i + 1).start()
        else:
            vec[...] = total
    while state["t"] < chunks + 6:
        serve()
    saves = [
        pltpu.make_async_copy(src, dst, rsem.at[i])
        for i, (src, dst) in enumerate(
            ((gup, gup_hbm), (gdown, gdown_hbm), (gout, gout_hbm), (gqkv, gqkv_hbm), (vec, vec_hbm))
        )
    ]
    for cp in saves:
        cp.start()
    scatter.sent()
    for cp in saves:
        cp.wait()
    save_gin.wait()
    save_out.wait()


def finish_kernel(out_in, gin_in, gup, gdown, gout, gqkv, vec, *refs):
    out, gin, o_qkv, bq, bv, o_out, bo, g1, s1, g2, s2, o_up, b_up, o_down, b_down = refs
    out[...] = out_in[...]
    gin[...] = gin_in[...]
    o_qkv[...] = gqkv[...].astype(F32)
    o_out[...] = gout[...].astype(F32)
    o_up[...] = gup[...].astype(F32)
    o_down[...] = gdown[...].astype(F32)
    width = vec.shape[1]
    for i, ref in enumerate((bq, bv, bo, g1, s1, g2, s2, b_down)):
        ref[...] = vec[i]
    for i in range(b_up.shape[0] // width):
        b_up[i * width : (i + 1) * width] = vec[8 + i]


FWD_HEADS = 4
BACK_AT = 3
SERVE_AT = (1, 3, 5)
N1_AFTER = 1
VEC_SERVES = (1, 2, 2, 2, 2)
OUT_SPLIT = (3, 6)


def vmem():
    return pl.BlockSpec(memory_space=pltpu.VMEM)


def hbm():
    return pl.BlockSpec(memory_space=pl.ANY)


def shape(dims, dtype):
    return jax.ShapeDtypeStruct(dims, dtype)


DMA = pltpu.SemaphoreType.DMA


def params(cid):
    return pltpu.CompilerParams(collective_id=cid, has_side_effects=True, vmem_limit_bytes=64 * 2**20 - 2**16)


def fast_local(
    inputs, doc_ids, w_qkv, bias_q, bias_v, w_out, bias_out, norm1_gain, norm1_bias, norm2_gain, norm2_bias,
    w_up, bias_up, w_down, bias_down, cotangent,
):
    x = inputs[0]
    tokens, width = x.shape
    ff = w_up.shape[1]
    halo = 256
    ext = tokens + halo
    heads = width // HEAD_DIM
    steps = ff // 512
    chunks = 2 * steps + 8
    slopes = jnp.asarray(
        np.broadcast_to((2.0 ** -(np.arange(heads) + 1.0) * LOG2E)[:, None], (heads, 128)).astype(np.float32)
    )
    shards = (
        (width // 16, ff // 2), (ff // 16, width // 2), (width // 16, width // 2), (width // 16, 3 * width // 2),
    )
    out, gin, g_up, g_down, g_out, g_qkv, vec = pl.pallas_call(
        functools.partial(layer_kernel, halo),
        out_shape=(shape((tokens, width), BF16), shape((tokens, width), F32))
        + tuple(shape(dims, BF16) for dims in shards)
        + (shape((12, width), F32),),
        in_specs=[hbm()] * 17,
        out_specs=(hbm(),) * 7,
        scratch_shapes=[pltpu.VMEM(dims, BF16) for dims in shards]
        + [pltpu.VMEM((12, width), F32)]
        + [pltpu.VMEM((tokens, width), BF16), pltpu.VMEM((1, tokens), jnp.int32), pltpu.VMEM((heads, 128), F32)]
        + [pltpu.VMEM((width,), BF16)] * 7
        + [pltpu.VMEM((ff,), BF16), pltpu.VMEM((width,), BF16)]
        + [
            pltpu.VMEM((ext, 3 * width), BF16),
            pltpu.VMEM((width, ext), BF16),
            pltpu.VMEM((width, tokens), BF16),
            pltpu.VMEM((2, 512, 256), F32),
            pltpu.VMEM((1, tokens), jnp.int32),
            pltpu.VMEM((tokens, width), F32),
            pltpu.VMEM((tokens, width), BF16),
            pltpu.VMEM((tokens, width), BF16),
            pltpu.VMEM((width, tokens), BF16),
            pltpu.VMEM((ff, tokens), BF16),
            pltpu.VMEM((tokens, 512), BF16),
            pltpu.VMEM((tokens, width), F32),
            pltpu.VMEM((tokens, width), F32),
            pltpu.VMEM((halo, width), F32),
            pltpu.VMEM((ext, 3 * width), BF16),
            pltpu.VMEM((2, width, 512), BF16),
            pltpu.VMEM((2, 512, width), BF16),
            pltpu.VMEM((1, 3 * width), F32),
            pltpu.VMEM((1, ff), F32),
            pltpu.VMEM((RING, 2, 32, 32, 256), BF16),
            pltpu.VMEM((chunks, 32, 32, 256), BF16),
        ]
        + arrival_shapes(chunks)
        + [
            pltpu.VMEM((5, 2, 12, width), F32),
            DMA((5,)), DMA((12,)), DMA((6,)), DMA((2,)), DMA((2, 4)), DMA, DMA((RING,)), DMA((chunks,)), DMA((4,)),
            DMA((4, chunks)), DMA((4,)), DMA((4,)), DMA((5,)), DMA((5,)), DMA((2,)),
        ],
        compiler_params=params(0),
        name="layer",
    )(
        x, doc_ids, slopes, bias_q, bias_v, bias_out, norm1_gain, norm1_bias, norm2_gain, norm2_bias, bias_up, bias_down,
        cotangent[0], w_qkv, w_out, w_up, w_down,
    )
    row = shape((width,), F32)
    return_shapes = (
        shape((tokens, width), BF16), shape((tokens, width), F32), shape(shards[3], F32), row, row, shape(shards[2], F32),
        row, row, row, row, row, shape(shards[0], F32), shape((ff,), F32), shape(shards[1], F32), row,
    )
    results = pl.pallas_call(
        finish_kernel,
        out_shape=return_shapes,
        in_specs=[vmem()] * 7,
        out_specs=(vmem(),) * 15,
        name="hand_over",
    )(out, gin, g_up, g_down, g_out, g_qkv, vec)
    return (results[0][None], results[1][None]) + tuple(results[2:])


def smooth_act(values):
    return jax.nn.gelu(values, approximate=True)


def layer_norm(values, norm_gain, norm_shift):
    center = values - jnp.mean(values, axis=-1, keepdims=True)
    inv_std = lax.rsqrt(jnp.mean(center * center, axis=-1, keepdims=True) + norm_eps)
    normed = center * inv_std
    return (normed * norm_gain + norm_shift, normed, inv_std)


def norm_back(grad_out, normed, inv_std, norm_gain):
    grad_gain = jnp.sum(grad_out * normed, axis=0)
    grad_shift = jnp.sum(grad_out, axis=0)
    inner_grad = grad_out * norm_gain
    grad_in = inv_std * (
        inner_grad
        - jnp.mean(inner_grad, axis=-1, keepdims=True)
        - normed * jnp.mean(inner_grad * normed, axis=-1, keepdims=True)
    )
    return (grad_in, grad_gain, grad_shift)


def block_scores(query_block, key_rows, first_row, head_slope, row_docs):
    block_rows = query_block.shape[0]
    length = key_rows.shape[0]
    raw_scores = lax.dot_general(
        query_block, key_rows, (((1,), (1,)), ((), ())), preferred_element_type=jnp.float32
    )
    query_pos = first_row + jnp.arange(block_rows, dtype=jnp.int32)
    key_pos = jnp.arange(length, dtype=jnp.int32)
    offset = query_pos[:, None] - key_pos[None, :]
    query_doc = lax.dynamic_slice_in_dim(row_docs, first_row, block_rows)
    allowed = (offset >= 0) & (query_doc[:, None] == row_docs[None, :])
    scores = raw_scores * key_rows.shape[1] ** (-0.5) - head_slope * offset.astype(jnp.float32)
    return jnp.where(allowed, scores, masked_score)


def head_forward(query_rows, key_rows, value_rows, head_slope, row_docs, block_rows):
    starts = jnp.arange(query_rows.shape[0] // block_rows, dtype=jnp.int32) * block_rows

    def one_block(first_row):
        query_block = lax.dynamic_slice_in_dim(query_rows, first_row, block_rows)
        scores = block_scores(query_block, key_rows, first_row, head_slope, row_docs)
        row_max = jnp.max(scores, axis=-1, keepdims=True)
        exponent = jnp.exp(scores - row_max)
        row_total = jnp.sum(exponent, axis=-1, keepdims=True)
        weights = (exponent / row_total).astype(jnp.bfloat16)
        block_out = jnp.dot(weights, value_rows, preferred_element_type=jnp.float32).astype(
            jnp.bfloat16
        )
        return (block_out, (row_max + jnp.log(row_total))[:, 0])

    block_outs, log_total = lax.map(one_block, starts)
    return (block_outs.reshape(-1, value_rows.shape[1]), log_total.reshape(-1))


def head_backward(
    query_rows, key_rows, value_rows, grad_rows, log_total, head_slope, row_docs, block_rows
):
    length, head_width = key_rows.shape
    inv_root = head_width ** (-0.5)
    starts = jnp.arange(length // block_rows, dtype=jnp.int32) * block_rows

    def one_block(running, first_row):
        grad_keys, grad_values = running
        query_block = lax.dynamic_slice_in_dim(query_rows, first_row, block_rows)
        grad_block = lax.dynamic_slice_in_dim(grad_rows, first_row, block_rows)
        total_block = lax.dynamic_slice_in_dim(log_total, first_row, block_rows)
        scores = block_scores(query_block, key_rows, first_row, head_slope, row_docs)
        weights = jnp.exp(scores - total_block[:, None])
        grad_weights = lax.dot_general(
            grad_block, value_rows, (((1,), (1,)), ((), ())), preferred_element_type=jnp.float32
        )
        inner_sum = jnp.sum(weights * grad_weights, axis=-1, keepdims=True)
        grad_scores = (weights * (grad_weights - inner_sum)).astype(jnp.bfloat16)
        grad_query = jnp.dot(grad_scores, key_rows, preferred_element_type=jnp.float32) * inv_root
        grad_keys = (
            grad_keys
            + lax.dot_general(
                grad_scores,
                query_block,
                (((0,), (0,)), ((), ())),
                preferred_element_type=jnp.float32,
            )
            * inv_root
        )
        grad_values = grad_values + lax.dot_general(
            weights.astype(jnp.bfloat16),
            grad_block,
            (((0,), (0,)), ((), ())),
            preferred_element_type=jnp.float32,
        )
        return ((grad_keys, grad_values), grad_query)

    zeros_block = jnp.zeros((length, head_width), jnp.float32)
    (grad_keys, grad_values), grad_query = lax.scan(one_block, (zeros_block, zeros_block), starts)
    return (
        grad_query.reshape(length, head_width).astype(jnp.bfloat16),
        grad_keys.astype(jnp.bfloat16),
        grad_values.astype(jnp.bfloat16),
    )


def local(
    inputs,
    doc_ids,
    w_qkv,
    bias_q,
    bias_v,
    w_out,
    bias_out,
    norm1_gain,
    norm1_bias,
    norm2_gain,
    norm2_bias,
    w_up,
    bias_up,
    w_down,
    bias_down,
    cotangent,
):
    model_width = w_out.shape[0]
    tokens = inputs.shape[1]
    head_count = model_width // HEAD_DIM
    float_inputs = inputs[0].astype(jnp.float32)
    gain_one = norm1_gain.astype(jnp.float32)
    gain_two = norm2_gain.astype(jnp.float32)
    normed_in, normed_one, inv_one = layer_norm(
        float_inputs, gain_one, norm1_bias.astype(jnp.float32)
    )
    act_one = normed_in.astype(jnp.bfloat16)
    projected = jnp.dot(act_one, w_qkv, preferred_element_type=jnp.float32)
    query_rows = (projected[:, :model_width] + bias_q.astype(jnp.float32)).astype(jnp.bfloat16)
    key_rows = projected[:, model_width : 2 * model_width].astype(jnp.bfloat16)
    value_rows = (projected[:, 2 * model_width :] + bias_v.astype(jnp.float32)).astype(jnp.bfloat16)
    query_rows = query_rows.reshape(tokens, head_count, HEAD_DIM)
    key_rows = key_rows.reshape(tokens, head_count, HEAD_DIM)
    value_rows = value_rows.reshape(tokens, head_count, HEAD_DIM)
    whole_q, whole_k, whole_v = (
        lax.all_to_all(query_rows, "seq", split_axis=1, concat_axis=0, tiled=True),
        lax.all_to_all(key_rows, "seq", split_axis=1, concat_axis=0, tiled=True),
        lax.all_to_all(value_rows, "seq", split_axis=1, concat_axis=0, tiled=True),
    )
    row_docs = lax.all_gather(doc_ids, "seq", axis=1, tiled=True)[0]
    local_heads = whole_q.shape[1]
    length = whole_q.shape[0]
    block_rows = min(512, length)
    first_head = lax.axis_index("seq") * local_heads
    slopes = jnp.exp2(
        -(first_head + 1 + jnp.arange(local_heads, dtype=jnp.int32)).astype(jnp.float32)
    )
    head_q = jnp.moveaxis(whole_q, 1, 0)
    head_k = jnp.moveaxis(whole_k, 1, 0)
    head_v = jnp.moveaxis(whole_v, 1, 0)

    def forward_head(operands):
        return head_forward(
            operands[0], operands[1], operands[2], operands[3], row_docs, block_rows
        )

    head_outs, head_totals = lax.map(forward_head, (head_q, head_k, head_v, slopes))
    mixed_heads = lax.all_to_all(
        jnp.moveaxis(head_outs, 0, 1), "seq", split_axis=0, concat_axis=1, tiled=True
    )
    mixed_flat = mixed_heads.reshape(tokens, model_width)
    second = (
        float_inputs
        + jnp.dot(mixed_flat, w_out, preferred_element_type=jnp.float32)
        + bias_out.astype(jnp.float32)
    )
    normed_mid, normed_two, inv_two = layer_norm(second, gain_two, norm2_bias.astype(jnp.float32))
    act_two = normed_mid.astype(jnp.bfloat16)
    pre_act = jnp.dot(act_two, w_up, preferred_element_type=jnp.float32) + bias_up.astype(
        jnp.float32
    )
    activated, act_pullback = jax.vjp(smooth_act, pre_act)
    hidden = activated.astype(jnp.bfloat16)
    result = (
        second
        + jnp.dot(hidden, w_down, preferred_element_type=jnp.float32)
        + bias_down.astype(jnp.float32)
    )
    grad_out = cotangent[0].astype(jnp.float32)
    grad_low = grad_out.astype(jnp.bfloat16)
    g_bias_down = jnp.sum(grad_low.astype(jnp.float32), axis=0)
    g_w_down = lax.dot_general(
        hidden, grad_low, (((0,), (0,)), ((), ())), preferred_element_type=jnp.float32
    )
    grad_hidden = lax.dot_general(
        grad_low, w_down, (((1,), (1,)), ((), ())), preferred_element_type=jnp.float32
    )
    grad_pre = act_pullback(grad_hidden)[0].astype(jnp.bfloat16)
    g_bias_up = jnp.sum(grad_pre.astype(jnp.float32), axis=0)
    g_w_up = lax.dot_general(
        act_two, grad_pre, (((0,), (0,)), ((), ())), preferred_element_type=jnp.float32
    )
    grad_norm_two = lax.dot_general(
        grad_pre, w_up, (((1,), (1,)), ((), ())), preferred_element_type=jnp.float32
    )
    grad_mid, g_gain_two, g_shift_two = norm_back(grad_norm_two, normed_two, inv_two, gain_two)
    grad_second = grad_out + grad_mid
    grad_branch = grad_second.astype(jnp.bfloat16)
    g_bias_out = jnp.sum(grad_branch.astype(jnp.float32), axis=0)
    g_w_out = lax.dot_general(
        mixed_flat, grad_branch, (((0,), (0,)), ((), ())), preferred_element_type=jnp.float32
    )
    grad_mixed = lax.dot_general(
        grad_branch, w_out, (((1,), (1,)), ((), ())), preferred_element_type=jnp.float32
    ).astype(jnp.bfloat16)
    grad_whole = lax.all_to_all(
        grad_mixed.reshape(tokens, head_count, HEAD_DIM),
        "seq",
        split_axis=1,
        concat_axis=0,
        tiled=True,
    )
    grad_heads = jnp.moveaxis(grad_whole, 1, 0)

    def backward_head(operands):
        return head_backward(
            operands[0],
            operands[1],
            operands[2],
            operands[3],
            operands[4],
            operands[5],
            row_docs,
            block_rows,
        )

    grad_q, grad_k, grad_v = lax.map(
        backward_head, (head_q, head_k, head_v, grad_heads, head_totals, slopes)
    )
    back_q, back_k, back_v = (
        lax.all_to_all(jnp.moveaxis(grad_q, 0, 1), "seq", split_axis=0, concat_axis=1, tiled=True),
        lax.all_to_all(jnp.moveaxis(grad_k, 0, 1), "seq", split_axis=0, concat_axis=1, tiled=True),
        lax.all_to_all(jnp.moveaxis(grad_v, 0, 1), "seq", split_axis=0, concat_axis=1, tiled=True),
    )
    back_q = back_q.reshape(tokens, model_width)
    back_k = back_k.reshape(tokens, model_width)
    back_v = back_v.reshape(tokens, model_width)
    g_bias_q = jnp.sum(back_q.astype(jnp.float32), axis=0)
    g_bias_v = jnp.sum(back_v.astype(jnp.float32), axis=0)
    grad_proj = jnp.concatenate([back_q, back_k, back_v], axis=1)
    g_w_qkv = lax.dot_general(
        act_one, grad_proj, (((0,), (0,)), ((), ())), preferred_element_type=jnp.float32
    )
    grad_norm_one = lax.dot_general(
        grad_proj, w_qkv, (((1,), (1,)), ((), ())), preferred_element_type=jnp.float32
    )
    grad_first, g_gain_one, g_shift_one = norm_back(grad_norm_one, normed_one, inv_one, gain_one)
    grad_inputs = grad_second + grad_first
    matrices = (g_w_qkv, g_w_out, g_w_up, g_w_down)
    partial_sums = (
        lax.psum_scatter(
            matrices[0].astype(jnp.bfloat16), "dp", scatter_dimension=0, tiled=True
        ).astype(jnp.float32),
        lax.psum_scatter(
            matrices[1].astype(jnp.bfloat16), "dp", scatter_dimension=0, tiled=True
        ).astype(jnp.float32),
        lax.psum_scatter(
            matrices[2].astype(jnp.bfloat16), "dp", scatter_dimension=0, tiled=True
        ).astype(jnp.float32),
        lax.psum_scatter(
            matrices[3].astype(jnp.bfloat16), "dp", scatter_dimension=0, tiled=True
        ).astype(jnp.float32),
    )
    summed = (
        lax.psum_scatter(
            partial_sums[0].astype(jnp.bfloat16), "seq", scatter_dimension=1, tiled=True
        ).astype(jnp.float32),
        lax.psum_scatter(
            partial_sums[1].astype(jnp.bfloat16), "seq", scatter_dimension=1, tiled=True
        ).astype(jnp.float32),
        lax.psum_scatter(
            partial_sums[2].astype(jnp.bfloat16), "seq", scatter_dimension=1, tiled=True
        ).astype(jnp.float32),
        lax.psum_scatter(
            partial_sums[3].astype(jnp.bfloat16), "seq", scatter_dimension=1, tiled=True
        ).astype(jnp.float32),
    )
    vectors = lax.psum(
        (
            g_bias_q,
            g_bias_v,
            g_bias_out,
            g_gain_one,
            g_shift_one,
            g_gain_two,
            g_shift_two,
            g_bias_up,
            g_bias_down,
        ),
        ("dp", "seq"),
    )
    return (
        result.astype(jnp.bfloat16)[None],
        grad_inputs[None],
        summed[0],
        vectors[0],
        vectors[1],
        summed[1],
        vectors[2],
        vectors[3],
        vectors[4],
        vectors[5],
        vectors[6],
        summed[2],
        vectors[7],
        summed[3],
        vectors[8],
    )


def solution(mesh):
    in_specs = (
        P("dp", "seq", None),
        P("dp", "seq"),
        P(),
        P(),
        P(),
        P(),
        P(),
        P(),
        P(),
        P(),
        P(),
        P(),
        P(),
        P(),
        P(),
        P("dp", "seq", None),
    )
    out_specs = (
        P("dp", "seq", None),
        P("dp", "seq", None),
        P("dp", "seq"),
        P(),
        P(),
        P("dp", "seq"),
        P(),
        P(),
        P(),
        P(),
        P(),
        P("dp", "seq"),
        P(),
        P("dp", "seq"),
        P(),
    )
    sizes = (mesh.shape["dp"], mesh.shape["seq"])
    chosen = fast_local if sizes == (16, 2) else local
    return jax.shard_map(chosen, mesh=mesh, in_specs=in_specs, out_specs=out_specs, check_vma=False)
```
